512 devices in a mesh: band: 8 (over y_lo, core), lon: 64 (over y_hi, x, z).
Axes of the slice: x: 4, y: 8 (y_hi: 2, y_lo: 4; y = y_hi * 4 + y_lo), z: 8, core: 2. Of those that a mesh axis runs over, the one named last changes fastest.
Arguments:
- e_field: float32 [3, 8, 64, 8192], P(None, None, 'band', 'lon'), may hold values from -10 to 10
- h_field: float32 [3, 8, 64, 8192], P(None, None, 'band', 'lon'), may hold values from -10 to 10
- conductivity: float32 [9, 8, 64, 8192], P(None, None, 'band', 'lon'), as said below
- zone_factor: int32 [8], replicated, may hold values from 1 to 8, as said below
- zone_bounds: int32 [7], replicated, may hold values from 1 to 63, as said below
Outputs:
- e_final: float32 [3, 8, 64, 8192], P(None, None, 'band', 'lon')
- h_final: float32 [3, 8, 64, 8192], P(None, None, 'band', 'lon')
The draws below stay inside these ranges and needn't reach their ends.
Inputs may be any that keep to these rules, and one draw needn't show every extreme that they name: `zone_factor`: every entry is a power of two. `zone_bounds`: strictly increasing; the first entry is 1 and the last is 63. `conductivity`: per cell the symmetric part of the 3 x 3 tensor is positive semidefinite.
All inputs are finite; a program needn't handle non-finite values.
Results may differ from the reference program's by a relative error of at most 0.0001.
Values sent between devices are 32-bit elements; how exact they have to be, the bound alone decides.
A program may use at most 64 MiB of HBM per device.

```python
import jax
import jax.numpy as jnp

LR = 8
ZONES = 8
STEPS = 4
LAT = 64
LON = 8192


def field_sample(key, offset, noise_lo, noise_hi):
    subkeys = jax.random.split(key, 4)
    grid_shape = (3, LR, LAT, LON)
    places = jnp.arange(LON, dtype=jnp.float32)[None, None, None, :] / LON
    phase = jax.random.uniform(subkeys[0], (3, 1, 1, 1), minval=0.0, maxval=1.0)
    strength = jax.random.uniform(subkeys[1], (3, 1, 1, 1), minval=0.6, maxval=1.2)
    smooth = strength * (offset + jnp.cos(2.0 * jnp.pi * (places + phase)))
    row_scale = jnp.exp(jax.random.uniform(subkeys[2], (1, 1, LAT, 1), minval=noise_lo, maxval=noise_hi))
    noise = jnp.clip(jax.random.normal(subkeys[3], grid_shape), -6.0, 6.0)
    return (smooth + row_scale * noise).astype(jnp.float32)


def draw_e_field(key, part):
    key = jax.random.fold_in(key, 21)
    return field_sample(key, 1.5, 0.0, 0.0)


def draw_h_field(key, part):
    key = jax.random.fold_in(key, 22)
    return field_sample(key, 1.5, 0.0, 0.0)


def draw_zone_factor(key, part):
    key = jax.random.fold_in(key, 11)
    levels = jax.random.randint(key, (ZONES,), 0, 4)
    places = jnp.arange(ZONES)
    levels = jnp.where((places == 0) | (places == ZONES - 1), 3, levels)
    levels = jnp.where(places == ZONES // 2, 0, levels)
    return (2 ** levels).astype(jnp.int32)


def draw_zone_bounds(key, part):
    key = jax.random.fold_in(key, 12)
    shuffled = jax.random.permutation(key, LAT - 3)[:ZONES - 3]
    middle = jnp.sort(shuffled).astype(jnp.int32) + 2
    first = jnp.ones((1,), jnp.int32)
    last = jnp.full((1,), LAT - 1, jnp.int32)
    return jnp.concatenate([first, middle, last]).astype(jnp.int32)


def draw_conductivity(key, part):
    key = jax.random.fold_in(key, 14)
    subkeys = jax.random.split(key, 4)
    grid_shape = (LR, LAT, LON)
    height = jnp.arange(LR, dtype=jnp.float32)[:, None, None] / max(LR - 1, 1)
    log_noise = jax.random.uniform(subkeys[0], grid_shape, minval=-0.5, maxval=0.5)
    hall_share = jax.random.uniform(subkeys[1], (3,) + grid_shape, minval=-1.5, maxval=1.5)
    layer_scale = 10.0 ** (-2.0 + 3.0 * height + log_noise)
    diagonal = layer_scale * (0.5 + jnp.exp(jax.random.uniform(subkeys[2], (3,) + grid_shape, minval=-2.3, maxval=0.7)))
    offdiag = layer_scale * 0.25 * jax.random.uniform(subkeys[3], (3,) + grid_shape, minval=-1.0, maxval=1.0)
    hall_part = layer_scale * hall_share
    entries = [diagonal[0], offdiag[0] + hall_part[0], offdiag[1] + hall_part[1], offdiag[0] - hall_part[0], diagonal[1], offdiag[2] + hall_part[2], offdiag[1] - hall_part[1], offdiag[2] - hall_part[2], diagonal[2]]
    return jnp.stack(entries).astype(jnp.float32)


def setup_inputs(seed: int = 0) -> dict:
    keys = jax.random.split(jax.random.key(seed), 6)
    e_field = draw_e_field(jax.random.fold_in(keys[5], 71), 0)
    h_field = draw_h_field(jax.random.fold_in(keys[5], 71), 0)
    conductivity = draw_conductivity(jax.random.fold_in(keys[5], 71), 0)
    zone_factor = draw_zone_factor(jax.random.fold_in(keys[5], 71), 0)
    zone_bounds = draw_zone_bounds(jax.random.fold_in(keys[5], 71), 0)
    return dict(e_field=e_field, h_field=h_field, conductivity=conductivity, zone_factor=zone_factor, zone_bounds=zone_bounds)


north_coef = 0.45
radial_coef = 0.5
east_coef = 0.12
metric_floor = 0.25


def inverse_parts(conduct):
    matrix = [[conduct[0] + 1.0, conduct[1], conduct[2]],
              [conduct[3], conduct[4] + 1.0, conduct[5]],
              [conduct[6], conduct[7], conduct[8] + 1.0]]

    def cofactor(across, within):
        upper_row = (across + 1) % 3
        lower_row = (across + 2) % 3
        left_col = (within + 1) % 3
        right_col = (within + 2) % 3
        return matrix[upper_row][left_col] * matrix[lower_row][right_col] - matrix[upper_row][right_col] * matrix[lower_row][left_col]

    determ = matrix[0][0] * cofactor(0, 0) + matrix[0][1] * cofactor(0, 1) + matrix[0][2] * cofactor(0, 2)
    inverse_det = 1.0 / determ
    return jnp.stack([cofactor(within, across) * inverse_det for across in range(3) for within in range(3)])


def apply_update(update, drive_term):
    return jnp.stack([update[3 * across] * drive_term[0] + update[3 * across + 1] * drive_term[1] + update[3 * across + 2] * drive_term[2] for across in range(3)])


def row_factors(zone_factor, zone_bounds, first_row, row_count, total_rows):
    rows_here = first_row + jnp.arange(row_count, dtype=jnp.int32)
    zone_of = jnp.sum((rows_here[:, None] >= zone_bounds[None, :]).astype(jnp.int32), axis=1)
    picked = zone_of[:, None] == jnp.arange(zone_factor.shape[0], dtype=jnp.int32)[None, :]
    factor = jnp.sum(jnp.where(picked, zone_factor[None, :], 0), axis=1).astype(jnp.int32)
    latitude = ((rows_here.astype(jnp.float32) + 0.5) / total_rows - 0.5) * jnp.pi
    metric = east_coef / jnp.maximum(factor.astype(jnp.float32) * jnp.cos(latitude), metric_floor)
    return factor, metric


def curl_parts(north_diff, east_diff, radial_diff):
    return jnp.stack([north_diff[2] - radial_diff[1], radial_diff[0] - east_diff[2], east_diff[1] - north_diff[0]])


def forward_curl(grid_field, lat_rim, lon_rim, metric_grid):
    north_next = jnp.concatenate([grid_field[:, :, 1:, :], lat_rim[:, :, None, :]], axis=2)
    east_next = jnp.concatenate([grid_field[:, :, :, 1:], lon_rim[:, :, :, None]], axis=3)
    upper_layer = jnp.concatenate([grid_field[:, 1:], jnp.zeros_like(grid_field[:, :1])], axis=1)
    return curl_parts(north_coef * (north_next - grid_field), metric_grid * (east_next - grid_field), radial_coef * (upper_layer - grid_field))


def backward_curl(grid_field, lat_rim, lon_rim, metric_grid):
    south_prev = jnp.concatenate([lat_rim[:, :, None, :], grid_field[:, :, :-1, :]], axis=2)
    west_prev = jnp.concatenate([lon_rim[:, :, :, None], grid_field[:, :, :, :-1]], axis=3)
    lower_layer = jnp.concatenate([jnp.zeros_like(grid_field[:, :1]), grid_field[:, :-1]], axis=1)
    return curl_parts(north_coef * (grid_field - south_prev), metric_grid * (grid_field - west_prev), radial_coef * (grid_field - lower_layer))


def merge_rows(grid_field, factor):
    lon_cells = grid_field.shape[-1]
    result = grid_field
    for group_size in (2, 4, 8):
        grouped = grid_field.reshape(grid_field.shape[:-1] + (lon_cells // group_size, group_size))
        averages = jnp.sum(grouped, axis=-1) / group_size
        spread_out = jnp.repeat(averages, group_size, axis=-1)
        result = jnp.where((factor == group_size)[None, None, :, None], spread_out, result)
    return result


def cap_ghost(pole_row):
    means = jnp.sum(pole_row, axis=-1) / LON
    return jnp.broadcast_to(means[:, :, None], pole_row.shape)


def reference(e_field, h_field, conductivity, zone_factor, zone_bounds):
    factor, metric = row_factors(zone_factor, zone_bounds, 0, LAT, LAT)
    metric_grid = metric[None, None, :, None]
    update = inverse_parts(conductivity)
    electric = e_field
    magnetic = h_field
    for step_idx in range(STEPS):
        north_rim = cap_ghost(electric[:, :, -1, :])
        magnetic = merge_rows(magnetic - forward_curl(electric, north_rim, electric[:, :, :, 0], metric_grid), factor)
        south_rim = cap_ghost(magnetic[:, :, 0, :])
        drive_term = 2.0 * electric + backward_curl(magnetic, south_rim, magnetic[:, :, :, -1], metric_grid)
        electric = merge_rows(apply_update(update, drive_term) - electric, factor)
    return electric, magnetic
```

```python
import functools

import jax
import jax.numpy as jnp
from jax import lax
from jax.experimental import pallas as pl
from jax.experimental.pallas import tpu as pltpu
from jax.sharding import PartitionSpec as P

MESH = pl.DeviceIdType.MESH
STEPS = 4
NORTH, RADIAL, EAST, FLOOR = 0.45, 0.5, 0.12, 0.25
FIELDS = 15


def lane_ids():
    return lax.broadcasted_iota(jnp.int32, (8, 128), 1)


def row_ids():
    return lax.broadcasted_iota(jnp.int32, (8, 128), 0)


def roll(x, by, axis):
    by = by % x.shape[axis]
    return x if by == 0 else pltpu.roll(x, by, axis)


def pair_shift(main, edge, by, axis):
    ids = lane_ids() if axis == 1 else row_ids()
    last = ids == (0 if by == 1 else (127 if axis == 1 else 7))
    rolled_main, rolled_edge = roll(main, by, axis), roll(edge, by, axis)
    return jnp.where(last, rolled_edge, rolled_main), jnp.where(last, rolled_main, rolled_edge)


def merge(x, gates):
    lanes = lane_ids()
    for step, gate in zip((1, 2, 4), gates):
        other = jnp.take_along_axis(x, lanes ^ step, axis=1)
        x = x + jnp.where(gate, other, x)
    return x * 0.125


def inverse(c):
    m = [[c[0] + 1.0, c[1], c[2]], [c[3], c[4] + 1.0, c[5]], [c[6], c[7], c[8] + 1.0]]

    def cof(a, b):
        i, j, p, q = (a + 1) % 3, (a + 2) % 3, (b + 1) % 3, (b + 2) % 3
        return m[i][p] * m[j][q] - m[i][q] * m[j][p]

    cofs = [[cof(a, b) for b in range(3)] for a in range(3)]
    det = m[0][0] * cofs[0][0] + m[0][1] * cofs[0][1] + m[0][2] * cofs[0][2]
    inv = 1.0 / det
    return [cofs[b][a] * inv for a in range(3) for b in range(3)]


def row_tables(zf, zb, rows, total):
    factor = jnp.full((8, 128), zf[0], jnp.int32)
    for z in range(zb.shape[0]):
        factor = jnp.where(rows >= zb[z], zf[z + 1], factor)
    lat = ((rows.astype(jnp.float32) + 0.5) / total - 0.5) * jnp.pi
    metric = EAST / jnp.maximum(factor.astype(jnp.float32) * jnp.cos(lat), FLOOR)
    return metric, [factor > s for s in (1, 2, 4)]


def kernel(zf, zb, e_ref, h_ref, c_ref, eo_ref, ho_ref, rows_e, rows_h, rows_c, pack, got, got2, ee, hh, uu, mine, caps, sums,
           send, recv, cap_send, cap_recv, *, bands, lons):
    band, lon = lax.axis_index("band"), lax.axis_index("lon")
    at_south, at_north = band == 0, band == bands - 1
    north, south = band + 1, band - 1
    east, west = lax.rem(lon + 1, lons), lax.rem(lon + lons - 1, lons)
    pole = jnp.logical_or(at_south, at_north)

    barrier = pltpu.get_barrier_semaphore()

    def greet(b, l):
        pl.semaphore_signal(barrier, inc=1, device_id=(b, l), device_id_type=MESH)

    greet(band, east)
    greet(band, west)

    @pl.when(jnp.logical_not(at_north))
    def _():
        for l in (lon, east, west):
            greet(north, l)

    @pl.when(jnp.logical_not(at_south))
    def _():
        for l in (lon, east, west):
            greet(south, l)

    @pl.when(pole)
    def _():
        def one(d, _):
            greet(band, lax.rem(lon + d, lons))
            return 0
        lax.fori_loop(2, lons - 1, one, 0)

    lanes, rows = lane_ids(), row_ids()
    def pack_field(ref, first, count):
        def one(i, _):
            c, a = i // 2, lax.rem(i, 2)
            rolled = [roll(ref[c, a * 4 + q], 32 * q, 1) for q in range(4)]
            lo, hi = rolled[0], rolled[1]
            for q in range(1, 4):
                lo = jnp.where(lanes // 32 == q, rolled[q], lo)
                if q > 1:
                    hi = jnp.where(lanes // 32 == q - 1, rolled[q], hi)
            hi = jnp.where(lanes // 32 == 3, rolled[0], hi)
            pack[0, first * 2 + i] = lo
            pack[1, first * 2 + i] = hi
            return 0
        lax.fori_loop(0, count * 2, one, 0, unroll=3)

    pack_field(e_ref, 0, 3)
    pack_field(h_ref, 3, 3)
    pack_field(c_ref, 6, 9)

    @pl.when(pole)
    def _():
        pl.semaphore_wait(barrier, lons - 1 + 3)

    @pl.when(jnp.logical_not(pole))
    def _():
        pl.semaphore_wait(barrier, 8)

    def remote(src, dst, i, b, l):
        return pltpu.make_async_remote_copy(src_ref=src, dst_ref=dst, send_sem=send.at[i], recv_sem=recv.at[i],
                                            device_id=(b, l), device_id_type=MESH)

    def local(src, dst, i):
        return pltpu.make_async_copy(src, dst, recv.at[i])

    low, high = pl.ds(0, 4), pl.ds(4, 4)
    to_lon = [remote(pack.at[0], got.at[0], 0, band, west), remote(pack.at[1], got.at[1], 1, band, east)]
    to_north = [remote(pack.at[0, :, high], got2.at[0, :, high], 2, north, west),
                remote(pack.at[1, :, high], got2.at[1, :, high], 3, north, east)] + [
        remote(s.at[:, :, high], d.at[:, :, high], 4 + i, north, lon)
        for i, (s, d) in enumerate(((e_ref, rows_e), (h_ref, rows_h), (c_ref, rows_c)))]
    to_south = [remote(pack.at[0, :, low], got2.at[0, :, low], 7, south, west),
                remote(pack.at[1, :, low], got2.at[1, :, low], 8, south, east)] + [
        remote(s.at[:, :, low], d.at[:, :, low], 9 + i, south, lon)
        for i, (s, d) in enumerate(((e_ref, rows_e), (h_ref, rows_h), (c_ref, rows_c)))]
    own_high = [local(pack.at[0, :, high], got2.at[0, :, high], 2), local(pack.at[1, :, high], got2.at[1, :, high], 3)] + [
        local(s.at[:, :, high], d.at[:, :, high], 4 + i)
        for i, (s, d) in enumerate(((e_ref, rows_e), (h_ref, rows_h), (c_ref, rows_c)))]
    own_low = [local(pack.at[0, :, low], got2.at[0, :, low], 7), local(pack.at[1, :, low], got2.at[1, :, low], 8)] + [
        local(s.at[:, :, low], d.at[:, :, low], 9 + i)
        for i, (s, d) in enumerate(((e_ref, rows_e), (h_ref, rows_h), (c_ref, rows_c)))]
    for copy in to_lon:
        copy.start()

    @pl.when(jnp.logical_not(at_north))
    def _():
        for copy in to_north:
            copy.start()

    @pl.when(at_north)
    def _():
        for copy in own_low:
            copy.start()

    @pl.when(jnp.logical_not(at_south))
    def _():
        for copy in to_south:
            copy.start()

    @pl.when(at_south)
    def _():
        for copy in own_high:
            copy.start()

    metric, gates = [], []
    for block in range(2):
        shift = 0 if block == 0 else jnp.where(rows < 4, 8, -8)
        m, g = row_tables(zf, zb, band * 8 + rows + shift, 8 * bands)
        metric.append(m)
        gates.append(g)
    zero = jnp.zeros((8, 128), jnp.float32)
    for b in range(4):
        for c in range(3):
            ee[b, c, 8] = zero
            hh[b, c, 0] = zero

    def take_in(block, layer, load):
        for c in range(3):
            ee[block, c, layer] = load(c)
            hh[block, c, layer + 1] = load(3 + c)
        for i, value in enumerate(inverse([load(6 + c) for c in range(9)])):
            uu[block, i, layer] = value

    def own(k, _):
        take_in(0, k, lambda f: e_ref[f, k] if f < 3 else (h_ref[f - 3, k] if f < 6 else c_ref[f - 6, k]))
        return 0

    lax.fori_loop(0, 8, own, 0)

    def unpack(block, ref):
        def one(a, _):
            for q in range(4):
                take_in(block, a * 4 + q, lambda f: roll(
                    jnp.where(lanes // 32 == q, ref[0, 2 * f + a], ref[1, 2 * f + a]), -32 * q, 1))
            return 0
        lax.fori_loop(0, 2, one, 0)

    for copy in to_lon:
        copy.wait()
    unpack(1, got)

    @pl.when(jnp.logical_not(at_north))
    def _():
        for copy in to_north:
            copy.wait_send()
        for copy in to_south:
            copy.wait_recv()

    @pl.when(at_north)
    def _():
        for copy in own_low:
            copy.wait()

    @pl.when(jnp.logical_not(at_south))
    def _():
        for copy in to_south:
            copy.wait_send()
        for copy in to_north:
            copy.wait_recv()

    @pl.when(at_south)
    def _():
        for copy in own_high:
            copy.wait()

    def outer(k, _):
        take_in(2, k, lambda f: rows_e[f, k] if f < 3 else (rows_h[f - 3, k] if f < 6 else rows_c[f - 6, k]))
        return 0

    lax.fori_loop(0, 8, outer, 0)
    unpack(3, got2)

    def cap_means(step, read):
        for i in range(2):
            mine[step, i] = read(2 * i)

        def copy_to(d):
            return pltpu.make_async_remote_copy(src_ref=mine.at[step], dst_ref=caps.at[step, d - 1], send_sem=cap_send.at[step],
                                                recv_sem=cap_recv.at[step], device_id=(band, lax.rem(lon + d, lons)),
                                                device_id_type=MESH)

        def start(d, _):
            copy_to(d).start()
            return 0

        lax.fori_loop(1, lons, start, 0)
        pltpu.make_async_copy(caps.at[step], caps.at[step], cap_send.at[step]).wait()
        pltpu.make_async_copy(caps.at[step], caps.at[step], cap_recv.at[step]).wait()
        for i in range(2):
            total = mine[step, i] + jnp.sum(caps[step, :, i], axis=0)
            sums[i] = jnp.broadcast_to(jnp.sum(total, axis=1, keepdims=True) * (1.0 / (128 * lons)), (8, 128))

    def forward(k, _):
        f = [[ee[b, c, k] for b in range(4)] for c in range(3)]
        up = [[ee[b, c, k + 1] for b in range(4)] for c in range(2)]
        fe, fn = {}, {}
        for c in (1, 2):
            fe[c] = [*pair_shift(f[c][0], f[c][1], -1, 1), *pair_shift(f[c][2], f[c][3], -1, 1)]
        for c in (0, 2):
            a, b = pair_shift(f[c][0], f[c][2], -1, 0), pair_shift(f[c][1], f[c][3], -1, 0)
            ghost = jnp.broadcast_to(sums[c // 2, pl.ds(k, 1), :], (8, 128))
            cap = jnp.logical_and(rows == 7, at_north)
            fn[c] = [jnp.where(cap, ghost, a[0]), jnp.where(cap, ghost, b[0]), a[1], b[1]]
        for b in range(4):
            m, g = metric[b // 2], gates[b // 2]
            curl = (NORTH * (fn[2][b] - f[2][b]) - RADIAL * (up[1][b] - f[1][b]),
                    RADIAL * (up[0][b] - f[0][b]) - m * (fe[2][b] - f[2][b]),
                    m * (fe[1][b] - f[1][b]) - NORTH * (fn[0][b] - f[0][b]))
            for c in range(3):
                hh[b, c, k + 1] = merge(hh[b, c, k + 1] - curl[c], g)
        return 0

    def backward(k, _):
        f = [[hh[b, c, k + 1] for b in range(4)] for c in range(3)]
        down = [[hh[b, c, k] for b in range(4)] for c in range(2)]
        fw, fs = {}, {}
        for c in (1, 2):
            fw[c] = [*pair_shift(f[c][0], f[c][1], 1, 1), *pair_shift(f[c][2], f[c][3], 1, 1)]
        for c in (0, 2):
            a, b = pair_shift(f[c][0], f[c][2], 1, 0), pair_shift(f[c][1], f[c][3], 1, 0)
            ghost = jnp.broadcast_to(sums[c // 2, pl.ds(k, 1), :], (8, 128))
            cap = jnp.logical_and(rows == 0, at_south)
            fs[c] = [jnp.where(cap, ghost, a[0]), jnp.where(cap, ghost, b[0]), a[1], b[1]]
        for b in range(4):
            m, g = metric[b // 2], gates[b // 2]
            curl = (NORTH * (f[2][b] - fs[2][b]) - RADIAL * (f[1][b] - down[1][b]),
                    RADIAL * (f[0][b] - down[0][b]) - m * (f[2][b] - fw[2][b]),
                    m * (f[1][b] - fw[1][b]) - NORTH * (f[0][b] - fs[0][b]))
            old = [ee[b, c, k] for c in range(3)]
            drive = [2.0 * old[c] + curl[c] for c in range(3)]
            for a in range(3):
                new = uu[b, 3 * a, k] * drive[0] + uu[b, 3 * a + 1, k] * drive[1] + uu[b, 3 * a + 2, k] * drive[2] - old[a]
                ee[b, a, k] = merge(new, g)
        return 0

    def step(n, _):
        @pl.when(at_north)
        def _():
            cap_means(n, lambda c: ee[0, c, pl.ds(0, 8), 7, :])

        lax.fori_loop(0, 8, forward, 0)

        @pl.when(at_south)
        def _():
            cap_means(n, lambda c: hh[0, c, pl.ds(1, 8), 0, :])

        lax.fori_loop(0, 8, backward, 0)
        return 0

    lax.fori_loop(0, STEPS, step, 0)
    for c in range(3):
        eo_ref[c] = ee[0, c, pl.ds(0, 8)]
        ho_ref[c] = hh[0, c, pl.ds(1, 8)]


def solution(mesh):
    bands, lons = mesh.shape["band"], mesh.shape["lon"]

    def on_device(e, h, c, zone_factor, zone_bounds):
        vmem, smem = pl.BlockSpec(memory_space=pltpu.VMEM), pl.BlockSpec(memory_space=pltpu.SMEM)
        f32 = lambda *shape: pltpu.VMEM(shape, jnp.float32)
        like = jax.ShapeDtypeStruct(e.shape, e.dtype)
        return pl.pallas_call(
            functools.partial(kernel, bands=bands, lons=lons),
            out_shape=(like, like),
            in_specs=[smem, smem, vmem, vmem, vmem],
            out_specs=(vmem, vmem),
            scratch_shapes=[
                f32(3, 8, 8, 128), f32(3, 8, 8, 128), f32(9, 8, 8, 128),
                f32(2, 2 * FIELDS, 8, 128), f32(2, 2 * FIELDS, 8, 128), f32(2, 2 * FIELDS, 8, 128),
                f32(4, 3, 9, 8, 128), f32(4, 3, 9, 8, 128), f32(4, 9, 8, 8, 128),
                f32(STEPS, 2, 8, 128), f32(STEPS, lons - 1, 2, 8, 128), f32(2, 8, 128),
                pltpu.SemaphoreType.DMA((12,)), pltpu.SemaphoreType.DMA((12,)),
                pltpu.SemaphoreType.DMA((STEPS,)), pltpu.SemaphoreType.DMA((STEPS,)),
            ],
            compiler_params=pltpu.CompilerParams(collective_id=0, has_side_effects=True, vmem_limit_bytes=32 * 1024 * 1024),
        )(zone_factor, zone_bounds, e, h, c)

    spread = P(None, None, "band", "lon")
    return jax.shard_map(on_device, mesh=mesh, in_specs=(spread, spread, spread, P(), P()), out_specs=(spread, spread),
                         check_vma=False)
```

```python
import functools

import jax
import jax.numpy as jnp
from jax import lax
from jax.experimental import pallas as pl
from jax.experimental.pallas import tpu as pltpu
from jax.sharding import PartitionSpec as P

MESH = pl.DeviceIdType.MESH
STEPS = 4
NORTH, RADIAL, EAST, FLOOR = 0.45, 0.5, 0.12, 0.25
FIELDS = 15


def lane_ids():
    return lax.broadcasted_iota(jnp.int32, (8, 128), 1)


def row_ids():
    return lax.broadcasted_iota(jnp.int32, (8, 128), 0)


def roll(x, by, axis):
    by = by % x.shape[axis]
    return x if by == 0 else pltpu.roll(x, by, axis)


def pair_shift(main, edge, by, axis):
    ids = lane_ids() if axis == 1 else row_ids()
    last = ids == (0 if by == 1 else (127 if axis == 1 else 7))
    rolled_main, rolled_edge = roll(main, by, axis), roll(edge, by, axis)
    return jnp.where(last, rolled_edge, rolled_main), jnp.where(last, rolled_main, rolled_edge)


def merge(x, gates):
    lanes = lane_ids()
    for step, gate in zip((1, 2, 4), gates):
        other = jnp.take_along_axis(x, lanes ^ step, axis=1)
        x = x + jnp.where(gate, other, x)
    return x * 0.125


def inverse(c):
    m = [[c[0] + 1.0, c[1], c[2]], [c[3], c[4] + 1.0, c[5]], [c[6], c[7], c[8] + 1.0]]

    def cof(a, b):
        i, j, p, q = (a + 1) % 3, (a + 2) % 3, (b + 1) % 3, (b + 2) % 3
        return m[i][p] * m[j][q] - m[i][q] * m[j][p]

    cofs = [[cof(a, b) for b in range(3)] for a in range(3)]
    det = m[0][0] * cofs[0][0] + m[0][1] * cofs[0][1] + m[0][2] * cofs[0][2]
    inv = 1.0 / det
    return [cofs[b][a] * inv for a in range(3) for b in range(3)]


def row_tables(zf, zb, rows, total):
    factor = jnp.full((8, 128), zf[0], jnp.int32)
    for z in range(zb.shape[0]):
        factor = jnp.where(rows >= zb[z], zf[z + 1], factor)
    lat = ((rows.astype(jnp.float32) + 0.5) / total - 0.5) * jnp.pi
    metric = EAST / jnp.maximum(factor.astype(jnp.float32) * jnp.cos(lat), FLOOR)
    return metric, factor


def batched(fn, tiles):
    whole = fn(jnp.concatenate(tiles, axis=0))
    return [whole[8 * i : 8 * i + 8] for i in range(len(tiles))]


def total_of(terms):
    out = None
    for factor, tile in terms:
        if tile is None:
            continue
        if out is None:
            out = tile if isinstance(factor, float) and factor == 1.0 else factor * tile
        elif isinstance(factor, float) and factor == 1.0:
            out = out + tile
        elif isinstance(factor, float) and factor == -1.0:
            out = out - tile
        else:
            out = out + factor * tile
    return out


class PoleRows:
    def __init__(self, at_north, metric, gates):
        self.at_north, self.metric, self.gates = at_north, metric, gates

    def shift_layer(self, field, c, r, b, source, by):
        rows = row_ids()
        key = source if source == "free" else (source[0], source[1] + by)
        tile = field.get((c, r, b, key))
        if tile is None:
            return None
        return jnp.where(rows == (7 if by == 1 else 0), 0.0, pltpu.roll(tile, 7 if by == 1 else 1, 0))

    def turn(self, field, comps, by):
        ids = [i for i in field if i[0] in comps and i[2] == 0]
        if not ids:
            return {}
        edge = lane_ids() == (0 if by == 1 else 127)
        moved = batched(lambda x: pltpu.roll(x, by % 128, 1), [field[i[0], i[1], b, i[3]] for b in range(2) for i in ids])
        out = {}
        for n, i in enumerate(ids):
            main, other = moved[n], moved[n + len(ids)]
            out[i] = jnp.where(edge, other, main)
            out[i[0], i[1], 1, i[3]] = jnp.where(edge, main, other)
        return out

    def merge(self, field):
        ids = list(field)
        tiles = [field[i] for i in ids]
        for level, step in enumerate((1, 2, 4)):
            def swap(x):
                return jnp.take_along_axis(x, lax.broadcasted_iota(jnp.int32, x.shape, 1) ^ step, axis=1)
            others = batched(swap, tiles)
            tiles = [t + jnp.where(self.gates[i[1]][level], o, t) for i, t, o in zip(ids, tiles, others)]
        return {i: t * 0.125 for i, t in zip(ids, tiles)}

    def keys(self, field, spread, extra=()):
        found = []
        for source in [i[3] for i in field] + list(extra):
            for s in ([source] if source == "free" else [source, (source[0], source[1] + spread)]):
                if s not in found:
                    found.append(s)
        return found

    def forward(self, e, h, wanted, merged=True):
        ahead = -1 if self.at_north else 1
        fe = self.turn(e, (1, 2), -1)
        new = {}
        for source in self.keys(e, -1, [i[3] for i in h]):
            for c, r in wanted:
                for b in range(2):
                    m = self.metric[r]
                    up = lambda c: self.shift_layer(e, c, r, b, source, 1)
                    at = lambda c: e.get((c, r, b, source))
                    north = lambda c: e.get((c, r + ahead, b, source))
                    east = lambda c: fe.get((c, r, b, source))
                    if c == 0:
                        curl = [(-NORTH, north(2)), (NORTH, at(2)), (RADIAL, up(1)), (-RADIAL, at(1))]
                    elif c == 1:
                        curl = [(-RADIAL, up(0)), (RADIAL, at(0)), (m, east(2)), (-m, at(2))]
                    else:
                        curl = [(-m, east(1)), (m, at(1)), (NORTH, north(0)), (-NORTH, at(0))]
                    tile = total_of([(1.0, h.get((c, r, b, source)))] + curl)
                    if tile is not None:
                        new[c, r, b, source] = tile
        return self.merge(new) if merged else new

    def drive(self, e, h, rows):
        behind = 1 if self.at_north else -1
        fw = self.turn(h, (1, 2), 1)
        new = {}
        for source in self.keys(h, 1, [i[3] for i in e]):
            for r in rows:
                for b in range(2):
                    m = self.metric[r]
                    down = lambda c: self.shift_layer(h, c, r, b, source, -1)
                    at = lambda c: h.get((c, r, b, source))
                    south = lambda c: h.get((c, r + behind, b, source))
                    west = lambda c: fw.get((c, r, b, source))
                    curls = ([(NORTH, at(2)), (-NORTH, south(2)), (-RADIAL, at(1)), (RADIAL, down(1))],
                             [(RADIAL, at(0)), (-RADIAL, down(0)), (-m, at(2)), (m, west(2))],
                             [(m, at(1)), (-m, west(1)), (-NORTH, at(0)), (NORTH, south(0))])
                    for c in range(3):
                        tile = total_of([(2.0, e.get((c, r, b, source)))] + curls[c])
                        if tile is not None:
                            new[c, r, b, source] = tile
        return new

    def update(self, u, drive, e, wanted, merged=True):
        new = {}
        for source in self.keys(drive, 0, [i[3] for i in e]):
            for a, r in wanted:
                for b in range(2):
                    tile = total_of([(u[3 * a + c, r, b], drive.get((c, r, b, source))) for c in range(3)]
                                    + [(-1.0, e.get((a, r, b, source)))])
                    if tile is not None:
                        new[a, r, b, source] = tile
        return self.merge(new) if merged else new


def every(rows):
    return [(c, r) for r in rows for c in range(3)]


def only(field, source):
    return {i: t for i, t in field.items() if (i[3] == "free") == source}


def pole_chain(at_north, load_e, load_h, load_u, metric, gates):
    p = PoleRows(at_north, metric, gates)
    deep = range(4) if at_north else range(5)
    e = {(c, r, b, "free"): load_e(c, r, b) for c in range(3) for r in deep for b in range(2)}
    h = {(c, r, b, "free"): load_h(c, r, b) for c in range(3) for r in range(4) for b in range(2)}
    u = {(i, r, b): load_u(i, r, b) for i in range(9) for r in range(3 if at_north else 4) for b in range(2)}
    out = {}

    def note(n, field, initial=False):
        for (c, r, b, source), tile in field.items():
            if r == 0 and b == 0 and c != 1:
                out[("free", n) if source == "free" else ("response", n) + source, c] = tile

    unit = jnp.ones((8, 128), jnp.float32)
    ends = [(0, 0), (2, 0)]
    if at_north:
        note(0, e)
        h = p.forward(e, h, every(range(4)))
        for b in range(2):
            h[0, 0, b, (2, 0)] = -NORTH * unit
            h[2, 0, b, (0, 0)] = NORTH * unit
        def back(e, h, free_rows, rows, wanted=None, merged=True):
            new = {}
            for free, rr in ((True, free_rows), (False, rows)):
                ee, hh = only(e, free), only(h, free)
                d = p.drive(ee, hh, rr)
                new.update({(i, free): t for i, t in d.items()})
            drive = {i: t for (i, _), t in new.items()}
            want = wanted or every(sorted(set(free_rows) | set(rows)))
            return p.update(u, drive, {i: t for i, t in e.items() if (i[1] in (free_rows if i[3] == "free" else rows))}, want, merged)

        e = back(e, h, range(3), range(1))
        note(1, e)
        h = p.forward(e, h, every(range(3)))
        h = {i: t for i, t in h.items() if i[3] == "free" or i[1] < 2}
        e = back(e, h, range(2), range(2))
        note(2, e)
        h = p.forward(e, h, every(range(2)))
        e = back(e, h, range(1), range(1), ends, False)
        note(3, e)
    else:
        h = p.forward(e, h, every(range(4)))
        note(0, h)
        drive = p.drive(e, h, range(4))
        for b in range(2):
            drive[0, 0, b, (2, 0)] = -NORTH * unit
            drive[2, 0, b, (0, 0)] = NORTH * unit
        e = p.update(u, drive, {i: t for i, t in e.items() if i[1] < 4}, every(range(4)))
        h = p.forward(e, {i: t for i, t in h.items() if i[1] < 3}, every(range(3)))
        note(1, h)
        drive = p.drive(e, h, range(3))
        e = p.update(u, drive, {i: t for i, t in e.items() if i[1] < 3}, every(range(3)))
        h = p.forward(e, {i: t for i, t in h.items() if i[1] < 2}, every(range(2)))
        note(2, h)
        drive = p.drive(e, h, range(2))
        e = p.update(u, drive, {i: t for i, t in e.items() if i[1] < 2}, every(range(2)))
        h = p.forward(e, {i: t for i, t in h.items() if i[1] < 1}, ends, False)
        note(3, h)
    return out


def columns(tiles):
    lanes = lane_ids()
    count = 128
    tiles = tiles + [None] * (count - len(tiles))
    while count > 1:
        count //= 2
        first, second = tiles[:count], tiles[count:]
        low = (lanes & count) == 0
        zero = jnp.zeros((8, 128), jnp.float32)
        pairs = [(a, b) for a, b in zip(first, second) if a is not None]
        give = [jnp.where(low, zero if b is None else b, a) for a, b in pairs]
        take = [jnp.where(low, a, zero if b is None else b) for a, b in pairs]
        swapped = batched(lambda x: jnp.take_along_axis(x, lax.broadcasted_iota(jnp.int32, x.shape, 1) ^ count, axis=1), give)
        tiles = [t + s for t, s in zip(take, swapped)]
        tiles = tiles + [None] * (count - len(tiles))
    return tiles[0]


def solve_caps(names, total):
    rows = row_ids()
    spread = dict(zip(names, batched(lambda x: x, [jnp.take_along_axis(total, jnp.full((8, 128), q, jnp.int32), axis=1)
                                                   for q in range(len(names))])))
    caps = []

    def moved(tile, d):
        if d == 0:
            return tile
        kept = rows >= d if d > 0 else rows < 8 + d
        return jnp.where(kept, pltpu.roll(tile, d % 8, 0), 0.0)

    for n in range(STEPS):
        value = {c: spread[("free", n), c] for c in (0, 2)}
        for m in range(n):
            shifted = {}
            for name, c in names:
                if name[0] == "response" and name[1] == n - m:
                    if name[2:] not in shifted:
                        shifted[name[2:]] = moved(caps[m][name[2]], name[3])
                    value[c] = value[c] + spread[name, c] * shifted[name[2:]]
        caps.append(value)
    return caps


def kernel(zf, zb, e_in, h_in, c_in, eo_ref, ho_ref, e_ref, h_ref, c_ref, rows_e, rows_h, rows_c, pack, got, got2, ee, hh, uu, mine,
           caps, sums, load_sem, send, recv, cap_send, cap_recv, *, bands, lons):
    band, lon = lax.axis_index("band"), lax.axis_index("lon")
    at_south, at_north = band == 0, band == bands - 1
    inner_north, inner_south = jnp.logical_not(at_north), jnp.logical_not(at_south)
    north, south = band + 1, band - 1
    east, west = lax.rem(lon + 1, lons), lax.rem(lon + lons - 1, lons)
    pole = jnp.logical_or(at_south, at_north)

    loads = [pltpu.make_async_copy(s, d, load_sem.at[i]) for i, (s, d) in enumerate(((e_in, e_ref), (h_in, h_ref), (c_in, c_ref)))]
    for load in loads:
        load.start()

    barrier = pltpu.get_barrier_semaphore()

    def greet(b, l):
        pl.semaphore_signal(barrier, inc=1, device_id=(b, l), device_id_type=MESH)

    greet(band, east)
    greet(band, west)

    @pl.when(inner_north)
    def _():
        for l in (east, west, lon):
            greet(north, l)

    @pl.when(inner_south)
    def _():
        for l in (east, west, lon):
            greet(south, l)

    @pl.when(pole)
    def _():
        def one(d, _):
            greet(band, lax.rem(lon + d, lons))
            return 0
        lax.fori_loop(2, lons - 1, one, 0)

    lanes, rows = lane_ids(), row_ids()

    def pack_field(ref, first, count):
        def one(i, _):
            tiles = [(c, a) for c in range(3) for a in range(2)]
            rolled = [[roll(ref[i * 3 + c, a * 4 + q], 32 * q, 1) for q in range(4)] for c, a in tiles]
            for n, t in enumerate(rolled):
                lo, hi = t[0], t[1]
                for q in range(1, 4):
                    lo = jnp.where(lanes // 32 == q, t[q], lo)
                    if q > 1:
                        hi = jnp.where(lanes // 32 == q - 1, t[q], hi)
                hi = jnp.where(lanes // 32 == 3, t[0], hi)
                pack[0, first * 2 + i * 6 + n] = lo
                pack[1, first * 2 + i * 6 + n] = hi
            return 0
        if count == 3:
            one(0, 0)
        else:
            lax.fori_loop(0, count // 3, one, 0)

    def remote(src, dst, i, b, l):
        return pltpu.make_async_remote_copy(src_ref=src, dst_ref=dst, send_sem=send.at[i], recv_sem=recv.at[i],
                                            device_id=(b, l), device_id_type=MESH)

    fields, conduct = pl.ds(0, 12), pl.ds(12, 18)
    to_lon = [[remote(pack.at[k, part], got.at[k, part], 2 * n + k, band, (west, east)[k]) for k in range(2)]
              for n, part in enumerate((fields, conduct))]
    to_north = [[remote(pack.at[k, part, pl.ds(8 - d[k], d[k])], got2.at[k, part, pl.ds(8 - d[k], d[k])], 4 + 2 * n + k, north, (west, east)[k])
                 for k in range(2)] for n, (part, d) in enumerate(((fields, (4, 3)), (conduct, (3, 2))))]
    to_south = [[remote(pack.at[k, part, pl.ds(0, d[k])], got2.at[k, part, pl.ds(0, d[k])], 8 + 2 * n + k, south, (west, east)[k])
                 for k in range(2)] for n, (part, d) in enumerate(((fields, (3, 4)), (conduct, (2, 3))))]
    trio = ((e_ref, rows_e), (h_ref, rows_h), (c_ref, rows_c))
    rows_north = [remote(s.at[:, :, pl.ds(8 - d, d)], t.at[:, :, pl.ds(8 - d, d)], 12 + i, north, lon)
                  for i, ((s, t), d) in enumerate(zip(trio, (4, 4, 3)))]
    rows_south = [remote(s.at[:, :, pl.ds(0, d)], t.at[:, :, pl.ds(0, d)], 15 + i, south, lon)
                  for i, ((s, t), d) in enumerate(zip(trio, (4, 3, 3)))]

    def send_part(n):
        for copy in to_lon[n]:
            copy.start()

        @pl.when(inner_north)
        def _():
            for copy in to_north[n] + (rows_north[:2] if n == 0 else rows_north[2:]):
                copy.start()

        @pl.when(inner_south)
        def _():
            for copy in to_south[n] + (rows_south[:2] if n == 0 else rows_south[2:]):
                copy.start()

    loads[0].wait()
    loads[1].wait()
    pack_field(e_ref, 0, 3)
    pack_field(h_ref, 3, 3)

    @pl.when(pole)
    def _():
        pl.semaphore_wait(barrier, lons - 1 + 3)

    @pl.when(jnp.logical_not(pole))
    def _():
        pl.semaphore_wait(barrier, 8)

    send_part(0)
    loads[2].wait()
    pack_field(c_ref, 6, 9)
    send_part(1)

    metric, factors, gates = [], [], []
    for block in range(2):
        shift = 0 if block == 0 else jnp.where(rows < 4, 8, -8)
        m, f = row_tables(zf, zb, band * 8 + rows + shift, 8 * bands)
        metric.append(m)
        factors.append(f)
        gates.append([f > s for s in (1, 2, 4)])
    zero = jnp.zeros((8, 128), jnp.float32)
    for b in range(4):
        for c in range(3):
            ee[b, c, 8] = zero
            hh[b, c, 0] = zero
    for n in range(STEPS):
        for i in range(2):
            sums[n, i] = zero

    def take_in(block, layer, load):
        for c in range(3):
            ee[block, c, layer] = load(c)
            hh[block, c, layer + 1] = load(3 + c)
        for i, value in enumerate(inverse([load(6 + c) for c in range(9)])):
            uu[block, i, layer] = value

    def own(k, _):
        take_in(0, k, lambda f: e_ref[f, k] if f < 3 else (h_ref[f - 3, k] if f < 6 else c_ref[f - 6, k]))
        return 0

    lax.fori_loop(0, 8, own, 0)

    def unpack(block, ref):
        def one(a, _):
            for q in range(4):
                tiles = [roll(jnp.where(lanes // 32 == q, ref[0, 2 * f + a], ref[1, 2 * f + a]), -32 * q, 1) for f in range(FIELDS)]
                take_in(block, a * 4 + q, lambda f: tiles[f])
            return 0
        lax.fori_loop(0, 2, one, 0)

    for n in range(2):
        for copy in to_lon[n]:
            copy.wait_recv()
    unpack(1, got)

    offsets = sorted(((i // 32, i // 8 % 4, i % 8) for i in range(1, 64)),
                     key=lambda o: -(4 * o[0] + min(o[1], 4 - o[1]) + min(o[2], 8 - o[2])))

    def cap_copy(n, offset):
        hi, x, z = lon // 32, lax.rem(lon // 8, 4), lax.rem(lon, 8)
        target = lax.rem(hi + offset[0], 2) * 32 + lax.rem(x + offset[1], 4) * 8 + lax.rem(z + offset[2], 8)
        return pltpu.make_async_remote_copy(src_ref=mine, dst_ref=caps.at[n], send_sem=cap_send.at[0], recv_sem=cap_recv.at[0],
                                            device_id=(band, target), device_id_type=MESH)

    names = {}
    for name, is_north, condition in (("north", True, at_north), ("south", False, at_south)):
        @pl.when(condition)
        def _():
            def sub(r):
                return 7 - r if is_north else r
            m = [jnp.broadcast_to(metric[0][sub(r) : sub(r) + 1, :], (8, 128)) for r in range(5)]
            f = [jnp.broadcast_to(factors[0][sub(r) : sub(r) + 1, :], (8, 128)) for r in range(5)]
            found = pole_chain(is_north, lambda c, r, b: ee[b, c, pl.ds(0, 8), sub(r), :], lambda c, r, b: hh[b, c, pl.ds(1, 8), sub(r), :],
                               lambda i, r, b: uu[b, i, pl.ds(0, 8), sub(r), :], m, [[x > s for s in (1, 2, 4)] for x in f])
            names[name] = list(found)
            mine[...] = columns(list(found.values()))

    @pl.when(pole)
    def _():
        for n, offset in enumerate(offsets):
            cap_copy(n, offset).start()

    @pl.when(inner_north)
    def _():
        for n in range(2):
            for copy in to_south[n]:
                copy.wait_recv()
        for copy in rows_south:
            copy.wait_recv()

    @pl.when(inner_south)
    def _():
        for n in range(2):
            for copy in to_north[n]:
                copy.wait_recv()
        for copy in rows_north:
            copy.wait_recv()

    def outer(k, _):
        take_in(2, k, lambda f: rows_e[f, k] if f < 3 else (rows_h[f - 3, k] if f < 6 else rows_c[f - 6, k]))
        return 0

    lax.fori_loop(0, 8, outer, 0)
    unpack(3, got2)

    @pl.when(pole)
    def _():
        pltpu.make_async_copy(caps, caps, cap_recv.at[0]).wait()

    for name, condition in (("north", at_north), ("south", at_south)):
        @pl.when(condition)
        def _():
            total = (mine[...] + jnp.sum(caps[...], axis=0)) * (1.0 / (128 * lons))
            for n, value in enumerate(solve_caps(names[name], total)):
                sums[n, 0] = value[0]
                sums[n, 1] = value[2]

    lane3 = lax.broadcasted_iota(jnp.int32, (8, 8, 128), 2)
    row3 = lax.broadcasted_iota(jnp.int32, (8, 8, 128), 1)
    metric3 = [jnp.broadcast_to(m, (8, 8, 128)) for m in metric]
    gates3 = [[jnp.broadcast_to(g, (8, 8, 128)).reshape(64, 128) for g in gs] for gs in gates]
    lane2 = lax.broadcasted_iota(jnp.int32, (64, 128), 1)

    def turn(f, by, axis):
        size = 128 if axis == 2 else 8
        seam = (lane3 if axis == 2 else row3) == (0 if by == 1 else size - 1)
        moved = [pltpu.roll(x.reshape(64, 128), by % 128, 1).reshape(8, 8, 128) if axis == 2 else pltpu.roll(x, by % 8, 1) for x in f]
        other = (1, 0, 3, 2) if axis == 2 else (2, 3, 0, 1)
        return [jnp.where(seam, moved[other[b]], moved[b]) for b in range(4)]

    def merge_all(f, store):
        x = {(b, c): f[b][c].reshape(64, 128) for b in range(4) for c in range(3)}
        for level, step in enumerate((1, 2, 4)):
            other = {i: jnp.take_along_axis(v, lane2 ^ step, axis=1) for i, v in x.items()}
            x = {(b, c): v + jnp.where(gates3[b // 2][level], other[b, c], v) for (b, c), v in x.items()}
        for (b, c), v in x.items():
            store(b, c, (v * 0.125).reshape(8, 8, 128))

    def ghost(n, c):
        return jnp.concatenate([jnp.broadcast_to(sums[n, c // 2, k : k + 1, :].reshape(1, 1, 128), (1, 8, 128)) for k in range(8)])

    def forward(n):
        f = [[ee[b, c, 0:8] for b in range(4)] for c in range(3)]
        up = [[ee[b, c, 1:9] for b in range(4)] for c in range(2)]
        fe = {c: turn(f[c], -1, 2) for c in (1, 2)}
        fn = {c: turn(f[c], -1, 1) for c in (0, 2)}
        cap = jnp.logical_and(row3 == 7, at_north)
        for c in (0, 2):
            value = ghost(n, c)
            for b in range(2):
                fn[c][b] = jnp.where(cap, value, fn[c][b])
        new = []
        for b in range(4):
            m = metric3[b // 2]
            curl = (NORTH * (fn[2][b] - f[2][b]) - RADIAL * (up[1][b] - f[1][b]),
                    RADIAL * (up[0][b] - f[0][b]) - m * (fe[2][b] - f[2][b]),
                    m * (fe[1][b] - f[1][b]) - NORTH * (fn[0][b] - f[0][b]))
            new.append([hh[b, c, 1:9] - curl[c] for c in range(3)])

        def store(b, c, v):
            hh[b, c, 1:9] = v

        merge_all(new, store)

    def backward(n):
        f = [[hh[b, c, 1:9] for b in range(4)] for c in range(3)]
        down = [[hh[b, c, 0:8] for b in range(4)] for c in range(2)]
        fw = {c: turn(f[c], 1, 2) for c in (1, 2)}
        fs = {c: turn(f[c], 1, 1) for c in (0, 2)}
        cap = jnp.logical_and(row3 == 0, at_south)
        for c in (0, 2):
            value = ghost(n, c)
            for b in range(2):
                fs[c][b] = jnp.where(cap, value, fs[c][b])
        new = []
        for b in range(4):
            m = metric3[b // 2]
            curl = (NORTH * (f[2][b] - fs[2][b]) - RADIAL * (f[1][b] - down[1][b]),
                    RADIAL * (f[0][b] - down[0][b]) - m * (f[2][b] - fw[2][b]),
                    m * (f[1][b] - fw[1][b]) - NORTH * (f[0][b] - fs[0][b]))
            old = [ee[b, c, 0:8] for c in range(3)]
            drive = [2.0 * old[c] + curl[c] for c in range(3)]
            new.append([uu[b, 3 * a, 0:8] * drive[0] + uu[b, 3 * a + 1, 0:8] * drive[1] + uu[b, 3 * a + 2, 0:8] * drive[2] - old[a]
                        for a in range(3)])

        def store(b, c, v):
            ee[b, c, 0:8] = v

        merge_all(new, store)

    def step(n, _):
        forward(n)
        backward(n)
        return 0

    lax.fori_loop(0, STEPS, step, 0)
    for c in range(3):
        eo_ref[c] = ee[0, c, pl.ds(0, 8)]
        ho_ref[c] = hh[0, c, pl.ds(1, 8)]

    for n in range(2):
        for copy in to_lon[n]:
            copy.wait_send()

    @pl.when(inner_north)
    def _():
        for copy in to_north[0] + to_north[1] + rows_north:
            copy.wait_send()

    @pl.when(inner_south)
    def _():
        for copy in to_south[0] + to_south[1] + rows_south:
            copy.wait_send()

    @pl.when(pole)
    def _():
        pltpu.make_async_copy(caps, caps, cap_send.at[0]).wait()


def solution(mesh):
    bands, lons = mesh.shape["band"], mesh.shape["lon"]

    def on_device(e, h, c, zone_factor, zone_bounds):
        vmem, smem, hbm = (pl.BlockSpec(memory_space=m) for m in (pltpu.VMEM, pltpu.SMEM, pl.ANY))
        f32 = lambda *shape: pltpu.VMEM(shape, jnp.float32)
        like = jax.ShapeDtypeStruct(e.shape, e.dtype)
        return pl.pallas_call(
            functools.partial(kernel, bands=bands, lons=lons),
            out_shape=(like, like),
            in_specs=[smem, smem, hbm, hbm, hbm],
            out_specs=(vmem, vmem),
            scratch_shapes=[
                f32(3, 8, 8, 128), f32(3, 8, 8, 128), f32(9, 8, 8, 128),
                f32(3, 8, 8, 128), f32(3, 8, 8, 128), f32(9, 8, 8, 128),
                f32(2, 2 * FIELDS, 8, 128), f32(2, 2 * FIELDS, 8, 128), f32(2, 2 * FIELDS, 8, 128),
                f32(4, 3, 9, 8, 128), f32(4, 3, 9, 8, 128), f32(4, 9, 8, 8, 128),
                f32(8, 128), f32(lons - 1, 8, 128), f32(STEPS, 2, 8, 128),
                pltpu.SemaphoreType.DMA((3,)), pltpu.SemaphoreType.DMA((18,)), pltpu.SemaphoreType.DMA((18,)),
                pltpu.SemaphoreType.DMA((1,)), pltpu.SemaphoreType.DMA((1,)),
            ],
            compiler_params=pltpu.CompilerParams(collective_id=0, has_side_effects=True, vmem_limit_bytes=32 * 1024 * 1024),
        )(zone_factor, zone_bounds, e, h, c)

    spread = P(None, None, "band", "lon")
    return jax.shard_map(on_device, mesh=mesh, in_specs=(spread, spread, spread, P(), P()), out_specs=(spread, spread),
                         check_vma=False)
```

```python
import functools

import jax
import jax.numpy as jnp
from jax import lax
from jax.experimental import pallas as pl
from jax.experimental.pallas import tpu as pltpu
from jax.sharding import PartitionSpec as P

MESH = pl.DeviceIdType.MESH
STEPS = 4
NORTH, RADIAL, EAST, FLOOR = 0.45, 0.5, 0.12, 0.25
FIELDS = 15


def lane_ids():
    return lax.broadcasted_iota(jnp.int32, (8, 128), 1)


def row_ids():
    return lax.broadcasted_iota(jnp.int32, (8, 128), 0)


def roll(x, by, axis):
    by = by % x.shape[axis]
    return x if by == 0 else pltpu.roll(x, by, axis)


def pair_shift(main, edge, by, axis):
    ids = lane_ids() if axis == 1 else row_ids()
    last = ids == (0 if by == 1 else (127 if axis == 1 else 7))
    rolled_main, rolled_edge = roll(main, by, axis), roll(edge, by, axis)
    return jnp.where(last, rolled_edge, rolled_main), jnp.where(last, rolled_main, rolled_edge)


def merge(x, gates):
    lanes = lane_ids()
    for step, gate in zip((1, 2, 4), gates):
        other = jnp.take_along_axis(x, lanes ^ step, axis=1)
        x = x + jnp.where(gate, other, x)
    return x * 0.125


def inverse(c):
    m = [[c[0] + 1.0, c[1], c[2]], [c[3], c[4] + 1.0, c[5]], [c[6], c[7], c[8] + 1.0]]

    def cof(a, b):
        i, j, p, q = (a + 1) % 3, (a + 2) % 3, (b + 1) % 3, (b + 2) % 3
        return m[i][p] * m[j][q] - m[i][q] * m[j][p]

    cofs = [[cof(a, b) for b in range(3)] for a in range(3)]
    det = m[0][0] * cofs[0][0] + m[0][1] * cofs[0][1] + m[0][2] * cofs[0][2]
    inv = 1.0 / det
    return [cofs[b][a] * inv for a in range(3) for b in range(3)]


def row_tables(zf, zb, rows, total):
    factor = jnp.full((8, 128), zf[0], jnp.int32)
    for z in range(zb.shape[0]):
        factor = jnp.where(rows >= zb[z], zf[z + 1], factor)
    lat = ((rows.astype(jnp.float32) + 0.5) / total - 0.5) * jnp.pi
    metric = EAST / jnp.maximum(factor.astype(jnp.float32) * jnp.cos(lat), FLOOR)
    return metric, factor


def batched(fn, tiles):
    whole = fn(jnp.concatenate(tiles, axis=0))
    return [whole[8 * i : 8 * i + 8] for i in range(len(tiles))]


def total_of(terms):
    out = None
    for factor, tile in terms:
        if tile is None:
            continue
        if out is None:
            out = tile if isinstance(factor, float) and factor == 1.0 else factor * tile
        elif isinstance(factor, float) and factor == 1.0:
            out = out + tile
        elif isinstance(factor, float) and factor == -1.0:
            out = out - tile
        else:
            out = out + factor * tile
    return out


class PoleRows:
    def __init__(self, at_north, metric, gates):
        self.at_north, self.metric, self.gates = at_north, metric, gates

    def shift_layer(self, field, c, r, source, by):
        rows = row_ids()
        key = source if source == "free" else (source[0], source[1] + by)
        tile = field.get((c, r, key))
        if tile is None:
            return None
        return jnp.where(rows == (7 if by == 1 else 0), 0.0, pltpu.roll(tile, 7 if by == 1 else 1, 0))

    def turn(self, field, comps, by):
        ids = [i for i in field if i[0] in comps]
        return dict(zip(ids, batched(lambda x: pltpu.roll(x, by % 128, 1), [field[i] for i in ids]))) if ids else {}

    def merge(self, field):
        ids = list(field)
        tiles = [field[i] for i in ids]
        for level, step in enumerate((1, 2, 4)):
            def swap(x):
                return jnp.take_along_axis(x, lax.broadcasted_iota(jnp.int32, x.shape, 1) ^ step, axis=1)
            others = batched(swap, tiles)
            tiles = [t + jnp.where(self.gates[i[1]][level], o, t) for i, t, o in zip(ids, tiles, others)]
        return {i: t * 0.125 for i, t in zip(ids, tiles)}

    def keys(self, field, spread, extra=()):
        found = []
        for source in [i[2] for i in field] + list(extra):
            for s in ([source] if source == "free" else [source, (source[0], source[1] + spread)]):
                if s not in found:
                    found.append(s)
        return found

    def forward(self, e, h, wanted, merged=True):
        ahead = -1 if self.at_north else 1
        fe = self.turn(e, (1, 2), -1)
        new = {}
        for source in self.keys(e, -1, [i[2] for i in h]):
            for c, r in wanted:
                m = self.metric[r]
                up = lambda c: self.shift_layer(e, c, r, source, 1)
                at = lambda c: e.get((c, r, source))
                north = lambda c: e.get((c, r + ahead, source))
                east = lambda c: fe.get((c, r, source))
                if c == 0:
                    curl = [(-NORTH, north(2)), (NORTH, at(2)), (RADIAL, up(1)), (-RADIAL, at(1))]
                elif c == 1:
                    curl = [(-RADIAL, up(0)), (RADIAL, at(0)), (m, east(2)), (-m, at(2))]
                else:
                    curl = [(-m, east(1)), (m, at(1)), (NORTH, north(0)), (-NORTH, at(0))]
                tile = total_of([(1.0, h.get((c, r, source)))] + curl)
                if tile is not None:
                    new[c, r, source] = tile
        return self.merge(new) if merged else new

    def drive(self, e, h, rows):
        behind = 1 if self.at_north else -1
        fw = self.turn(h, (1, 2), 1)
        new = {}
        for source in self.keys(h, 1, [i[2] for i in e]):
            for r in rows:
                m = self.metric[r]
                down = lambda c: self.shift_layer(h, c, r, source, -1)
                at = lambda c: h.get((c, r, source))
                south = lambda c: h.get((c, r + behind, source))
                west = lambda c: fw.get((c, r, source))
                curls = ([(NORTH, at(2)), (-NORTH, south(2)), (-RADIAL, at(1)), (RADIAL, down(1))],
                         [(RADIAL, at(0)), (-RADIAL, down(0)), (-m, at(2)), (m, west(2))],
                         [(m, at(1)), (-m, west(1)), (-NORTH, at(0)), (NORTH, south(0))])
                for c in range(3):
                    tile = total_of([(2.0, e.get((c, r, source)))] + curls[c])
                    if tile is not None:
                        new[c, r, source] = tile
        return new

    def update(self, u, drive, e, wanted, merged=True):
        new = {}
        for source in self.keys(drive, 0, [i[2] for i in e]):
            for a, r in wanted:
                tile = total_of([(u[3 * a + c, r], drive.get((c, r, source))) for c in range(3)]
                                + [(-1.0, e.get((a, r, source)))])
                if tile is not None:
                    new[a, r, source] = tile
        return self.merge(new) if merged else new


def every(rows):
    return [(c, r) for r in rows for c in range(3)]


def only(field, source):
    return {i: t for i, t in field.items() if (i[2] == "free") == source}


def pole_chain(at_north, load, metric, gates):
    p = PoleRows(at_north, metric, gates)
    deep = range(4) if at_north else range(5)
    e = {(c, r, "free"): load("e", c, r) for c in range(3) for r in deep}
    h = {(c, r, "free"): load("h", c, r) for c in range(3) for r in range(4)}
    u = {(i, r): v for r in range(3 if at_north else 4) for i, v in enumerate(inverse([load("c", i, r) for i in range(9)]))}
    out = {}

    def note(n, field, initial=False):
        for (c, r, source), tile in field.items():
            if r == 0 and c != 1:
                out[("free", n) if source == "free" else ("response", n) + source, c] = tile

    unit = jnp.ones((8, 128), jnp.float32)
    ends = [(0, 0), (2, 0)]
    if at_north:
        note(0, e)
        h = p.forward(e, h, every(range(4)))
        h[0, 0, (2, 0)] = -NORTH * unit
        h[2, 0, (0, 0)] = NORTH * unit
        def back(e, h, free_rows, rows, wanted=None, merged=True):
            new = {}
            for free, rr in ((True, free_rows), (False, rows)):
                ee, hh = only(e, free), only(h, free)
                d = p.drive(ee, hh, rr)
                new.update({(i, free): t for i, t in d.items()})
            drive = {i: t for (i, _), t in new.items()}
            want = wanted or every(sorted(set(free_rows) | set(rows)))
            return p.update(u, drive, {i: t for i, t in e.items() if (i[1] in (free_rows if i[2] == "free" else rows))}, want, merged)

        e = back(e, h, range(3), range(1))
        note(1, e)
        h = p.forward(e, h, every(range(3)))
        h = {i: t for i, t in h.items() if i[2] == "free" or i[1] < 2}
        e = back(e, h, range(2), range(2))
        note(2, e)
        h = p.forward(e, h, every(range(2)))
        e = back(e, h, range(1), range(1), ends, False)
        note(3, e)
    else:
        h = p.forward(e, h, every(range(4)))
        note(0, h)
        drive = p.drive(e, h, range(4))
        drive[0, 0, (2, 0)] = -NORTH * unit
        drive[2, 0, (0, 0)] = NORTH * unit
        e = p.update(u, drive, {i: t for i, t in e.items() if i[1] < 4}, every(range(4)))
        h = p.forward(e, {i: t for i, t in h.items() if i[1] < 3}, every(range(3)))
        note(1, h)
        drive = p.drive(e, h, range(3))
        e = p.update(u, drive, {i: t for i, t in e.items() if i[1] < 3}, every(range(3)))
        h = p.forward(e, {i: t for i, t in h.items() if i[1] < 2}, every(range(2)))
        note(2, h)
        drive = p.drive(e, h, range(2))
        e = p.update(u, drive, {i: t for i, t in e.items() if i[1] < 2}, every(range(2)))
        h = p.forward(e, {i: t for i, t in h.items() if i[1] < 1}, ends, False)
        note(3, h)
    return out


def pole_items(at_north):
    return ([("e", c, r) for c in range(3) for r in range(4 if at_north else 5)] + [("h", c, r) for c in range(3) for r in range(4)]
            + [("c", i, r) for i in range(9) for r in range(3 if at_north else 4)])


def columns(tiles):
    lanes = lane_ids()
    count = 128
    tiles = tiles + [None] * (count - len(tiles))
    while count > 1:
        count //= 2
        first, second = tiles[:count], tiles[count:]
        low = (lanes & count) == 0
        zero = jnp.zeros((8, 128), jnp.float32)
        pairs = [(a, b) for a, b in zip(first, second) if a is not None]
        give = [jnp.where(low, zero if b is None else b, a) for a, b in pairs]
        take = [jnp.where(low, a, zero if b is None else b) for a, b in pairs]
        swapped = batched(lambda x: jnp.take_along_axis(x, lax.broadcasted_iota(jnp.int32, x.shape, 1) ^ count, axis=1), give)
        tiles = [t + s for t, s in zip(take, swapped)]
        tiles = tiles + [None] * (count - len(tiles))
    return tiles[0]


def solve_caps(names, total):
    rows = row_ids()
    spread = dict(zip(names, batched(lambda x: x, [jnp.take_along_axis(total, jnp.full((8, 128), q, jnp.int32), axis=1)
                                                   for q in range(len(names))])))
    caps = []

    def moved(tile, d):
        if d == 0:
            return tile
        kept = rows >= d if d > 0 else rows < 8 + d
        return jnp.where(kept, pltpu.roll(tile, d % 8, 0), 0.0)

    for n in range(STEPS):
        value = {c: spread[("free", n), c] for c in (0, 2)}
        for m in range(n):
            shifted = {}
            for name, c in names:
                if name[0] == "response" and name[1] == n - m:
                    if name[2:] not in shifted:
                        shifted[name[2:]] = moved(caps[m][name[2]], name[3])
                    value[c] = value[c] + spread[name, c] * shifted[name[2:]]
        caps.append(value)
    return caps


def kernel(zf_in, zb_in, e_in, h_in, c_in, eo_ref, ho_ref, zf, zb, e_ref, h_ref, c_ref, rows_e, rows_h, rows_c, pack, got, got2, pole_own, pole_pack, pole_got, pole_sum, ee, hh, uu, mine,
           caps, sums, load_sem, send, recv, cap_send, cap_recv, *, bands, lons):
    band, lon = lax.axis_index("band"), lax.axis_index("lon")
    at_south, at_north = band == 0, band == bands - 1
    inner_north, inner_south = jnp.logical_not(at_north), jnp.logical_not(at_south)
    north, south = band + 1, band - 1
    east, west = lax.rem(lon + 1, lons), lax.rem(lon + lons - 1, lons)
    pole = jnp.logical_or(at_south, at_north)

    loads = [pltpu.make_async_copy(s, d, load_sem.at[i]) for i, (s, d) in enumerate(((e_in, e_ref), (h_in, h_ref), (c_in, c_ref), (zf_in, zf), (zb_in, zb)))]
    for load in loads:
        load.start()

    barrier = pltpu.get_barrier_semaphore()

    def greet(b, l):
        pl.semaphore_signal(barrier, inc=1, device_id=(b, l), device_id_type=MESH)

    greet(band, east)
    greet(band, west)

    @pl.when(inner_north)
    def _():
        for l in (east, west, lon):
            greet(north, l)

    @pl.when(inner_south)
    def _():
        for l in (east, west, lon):
            greet(south, l)

    @pl.when(pole)
    def _():
        def one(d, _):
            greet(band, lax.rem(lon + d, lons))
            return 0
        lax.fori_loop(2, lons - 1, one, 0)

    lanes, rows = lane_ids(), row_ids()

    def pack_field(ref, first, count):
        def one(i, _):
            tiles = [(c, a) for c in range(3) for a in range(2)]
            rolled = [[roll(ref[i * 3 + c, a * 4 + q], 32 * q, 1) for q in range(4)] for c, a in tiles]
            for n, t in enumerate(rolled):
                lo, hi = t[0], t[1]
                for q in range(1, 4):
                    lo = jnp.where(lanes // 32 == q, t[q], lo)
                    if q > 1:
                        hi = jnp.where(lanes // 32 == q - 1, t[q], hi)
                hi = jnp.where(lanes // 32 == 3, t[0], hi)
                pack[0, first * 2 + i * 6 + n] = lo
                pack[1, first * 2 + i * 6 + n] = hi
            return 0
        if count == 3:
            one(0, 0)
        else:
            lax.fori_loop(0, count // 3, one, 0)

    def remote(src, dst, i, b, l):
        return pltpu.make_async_remote_copy(src_ref=src, dst_ref=dst, send_sem=send.at[i], recv_sem=recv.at[i],
                                            device_id=(b, l), device_id_type=MESH)

    fields, conduct = pl.ds(0, 12), pl.ds(12, 18)
    to_lon = [[remote(pack.at[k, part], got.at[k, part], 2 * n + k, band, (west, east)[k]) for k in range(2)]
              for n, part in enumerate((fields, conduct))]
    to_north = [[remote(pack.at[k, part, pl.ds(8 - d[k], d[k])], got2.at[k, part, pl.ds(8 - d[k], d[k])], 4 + 2 * n + k, north, (west, east)[k])
                 for k in range(2)] for n, (part, d) in enumerate(((fields, (4, 3)), (conduct, (3, 2))))]
    to_south = [[remote(pack.at[k, part, pl.ds(0, d[k])], got2.at[k, part, pl.ds(0, d[k])], 8 + 2 * n + k, south, (west, east)[k])
                 for k in range(2)] for n, (part, d) in enumerate(((fields, (3, 4)), (conduct, (2, 3))))]
    trio = ((e_ref, rows_e), (h_ref, rows_h), (c_ref, rows_c))
    rows_north = [remote(s.at[:, :, pl.ds(8 - d, d)], t.at[:, :, pl.ds(8 - d, d)], 12 + i, north, lon)
                  for i, ((s, t), d) in enumerate(zip(trio, (4, 4, 3)))]
    rows_south = [remote(s.at[:, :, pl.ds(0, d)], t.at[:, :, pl.ds(0, d)], 15 + i, south, lon)
                  for i, ((s, t), d) in enumerate(zip(trio, (4, 3, 3)))]

    def send_part(n):
        for copy in to_lon[n]:
            copy.start()

        @pl.when(inner_north)
        def _():
            for copy in to_north[n] + (rows_north[:2] if n == 0 else rows_north[2:]):
                copy.start()

        @pl.when(inner_south)
        def _():
            for copy in to_south[n] + (rows_south[:2] if n == 0 else rows_south[2:]):
                copy.start()

    loads[0].wait()
    loads[1].wait()
    poles = ((True, at_north), (False, at_south))
    refs = {"e": e_ref, "h": h_ref, "c": c_ref}

    def pole_copy(is_north):
        part = pl.ds(0, (len(pole_items(is_north)) + 1) // 2)
        return remote(pole_pack.at[part], pole_got.at[part], 18, band, east)

    @pl.when(pole)
    def _():
        loads[2].wait()

    for is_north, condition in poles:
        @pl.when(condition)
        def _():
            tiles = [refs[kind][i, pl.ds(0, 8), 7 - r if is_north else r, :] for kind, i, r in pole_items(is_north)]
            for n, tile in enumerate(tiles):
                pole_own[n] = tile
            for n in range(0, len(tiles), 2):
                pole_pack[n // 2] = jnp.where(lanes < 64, pltpu.roll(tiles[n], 64, 1), tiles[min(n + 1, len(tiles) - 1)])

    pack_field(e_ref, 0, 3)
    pack_field(h_ref, 3, 3)

    @pl.when(pole)
    def _():
        pl.semaphore_wait(barrier, lons - 1 + 3)

    @pl.when(jnp.logical_not(pole))
    def _():
        pl.semaphore_wait(barrier, 8)

    for is_north, condition in poles:
        @pl.when(condition)
        def _():
            pole_copy(is_north).start()

    send_part(0)

    @pl.when(jnp.logical_not(pole))
    def _():
        loads[2].wait()

    pack_field(c_ref, 6, 9)
    send_part(1)

    loads[3].wait()
    loads[4].wait()
    metric, factors, gates = [], [], []
    for block in range(2):
        shift = 0 if block == 0 else jnp.where(rows < 4, 8, -8)
        m, f = row_tables(zf, zb, band * 8 + rows + shift, 8 * bands)
        metric.append(m)
        factors.append(f)
        gates.append([f > s for s in (1, 2, 4)])
    zero = jnp.zeros((8, 128), jnp.float32)
    for b in range(4):
        for c in range(3):
            ee[b, c, 8] = zero
            hh[b, c, 0] = zero
    for n in range(STEPS):
        for i in range(2):
            sums[n, i] = zero

    def take_in(block, layer, load):
        for c in range(3):
            ee[block, c, layer] = load(c)
            hh[block, c, layer + 1] = load(3 + c)
        for i, value in enumerate(inverse([load(6 + c) for c in range(9)])):
            uu[block, i, layer] = value

    def own(k, _):
        take_in(0, k, lambda f: e_ref[f, k] if f < 3 else (h_ref[f - 3, k] if f < 6 else c_ref[f - 6, k]))
        return 0


    def unpack(block, ref):
        def one(a, _):
            for q in range(4):
                tiles = [roll(jnp.where(lanes // 32 == q, ref[0, 2 * f + a], ref[1, 2 * f + a]), -32 * q, 1) for f in range(FIELDS)]
                take_in(block, a * 4 + q, lambda f: tiles[f])
            return 0
        lax.fori_loop(0, 2, one, 0)

    offsets = sorted(((i // 32, i // 8 % 4, i % 8) for i in range(1, 64)),
                     key=lambda o: -(4 * o[0] + min(o[1], 4 - o[1]) + min(o[2], 8 - o[2])))

    def cap_copy(n, offset):
        hi, x, z = lon // 32, lax.rem(lon // 8, 4), lax.rem(lon, 8)
        target = lax.rem(hi + offset[0], 2) * 32 + lax.rem(x + offset[1], 4) * 8 + lax.rem(z + offset[2], 8)
        return pltpu.make_async_remote_copy(src_ref=mine, dst_ref=caps.at[n], send_sem=cap_send.at[0], recv_sem=cap_recv.at[0],
                                            device_id=(band, target), device_id_type=MESH)

    names = {}
    for is_north, condition in poles:
        @pl.when(condition)
        def _():
            items = pole_items(is_north)
            place = {item: n for n, item in enumerate(items)}
            edge = [7 - r if is_north else r for r in range(5)]
            m = [jnp.broadcast_to(metric[0][r : r + 1, :], (8, 128)) for r in edge]
            f = [jnp.broadcast_to(factors[0][r : r + 1, :], (8, 128)) for r in edge]
            g = [[x > k for k in (1, 2, 4)] for x in f]

            def seam(kind, i, r):
                n = place[kind, i, r]
                tile = pole_got[n // 2]
                return jnp.where(lanes < 64, tile if n % 2 == 0 else pltpu.roll(tile, 64, 1), pltpu.roll(pole_own[n], 64, 1))

            inner = pole_chain(is_north, lambda kind, i, r: pole_own[place[kind, i, r]], m, g)
            names[is_north] = list(inner)
            for n, tile in enumerate(inner.values()):
                pole_sum[n] = tile
            pole_copy(is_north).wait_recv()
            outer = pole_chain(is_north, seam, m, g)
            inside = jnp.logical_and(lanes >= 32, lanes < 96)
            mine[...] = columns([jnp.where(inside, pole_sum[n] + outer[name], 0.0) for n, name in enumerate(names[is_north])])

    @pl.when(pole)
    def _():
        for n, offset in enumerate(offsets):
            cap_copy(n, offset).start()

    lax.fori_loop(0, 8, own, 0)

    for n in range(2):
        for copy in to_lon[n]:
            copy.wait_recv()
    unpack(1, got)

    @pl.when(inner_north)
    def _():
        for n in range(2):
            for copy in to_south[n]:
                copy.wait_recv()
        for copy in rows_south:
            copy.wait_recv()

    @pl.when(inner_south)
    def _():
        for n in range(2):
            for copy in to_north[n]:
                copy.wait_recv()
        for copy in rows_north:
            copy.wait_recv()

    def outer(k, _):
        take_in(2, k, lambda f: rows_e[f, k] if f < 3 else (rows_h[f - 3, k] if f < 6 else rows_c[f - 6, k]))
        return 0

    lax.fori_loop(0, 8, outer, 0)
    unpack(3, got2)

    @pl.when(pole)
    def _():
        pltpu.make_async_copy(caps, caps, cap_recv.at[0]).wait()

    for is_north, condition in poles:
        @pl.when(condition)
        def _():
            total = (mine[...] + jnp.sum(caps[...], axis=0)) * (1.0 / (128 * lons))
            for n, value in enumerate(solve_caps(names[is_north], total)):
                sums[n, 0] = value[0]
                sums[n, 1] = value[2]

    lane3 = lax.broadcasted_iota(jnp.int32, (8, 8, 128), 2)
    row3 = lax.broadcasted_iota(jnp.int32, (8, 8, 128), 1)
    metric3 = [jnp.broadcast_to(m, (8, 8, 128)) for m in metric]
    gates3 = [[jnp.broadcast_to(g, (8, 8, 128)).reshape(64, 128) for g in gs] for gs in gates]
    lane2 = lax.broadcasted_iota(jnp.int32, (64, 128), 1)

    def turn(f, by, axis):
        size = 128 if axis == 2 else 8
        seam = (lane3 if axis == 2 else row3) == (0 if by == 1 else size - 1)
        moved = [pltpu.roll(x.reshape(64, 128), by % 128, 1).reshape(8, 8, 128) if axis == 2 else pltpu.roll(x, by % 8, 1) for x in f]
        other = (1, 0, 3, 2) if axis == 2 else (2, 3, 0, 1)
        return [jnp.where(seam, moved[other[b]], moved[b]) for b in range(4)]

    def merge_all(f, store):
        x = {(b, c): f[b][c].reshape(64, 128) for b in range(4) for c in range(3)}
        for level, step in enumerate((1, 2, 4)):
            other = {i: jnp.take_along_axis(v, lane2 ^ step, axis=1) for i, v in x.items()}
            x = {(b, c): v + jnp.where(gates3[b // 2][level], other[b, c], v) for (b, c), v in x.items()}
        for (b, c), v in x.items():
            store(b, c, (v * 0.125).reshape(8, 8, 128))

    def ghost(n, c):
        return jnp.concatenate([jnp.broadcast_to(sums[n, c // 2, k : k + 1, :].reshape(1, 1, 128), (1, 8, 128)) for k in range(8)])

    def forward(n):
        f = [[ee[b, c, 0:8] for b in range(4)] for c in range(3)]
        up = [[ee[b, c, 1:9] for b in range(4)] for c in range(2)]
        fe = {c: turn(f[c], -1, 2) for c in (1, 2)}
        fn = {c: turn(f[c], -1, 1) for c in (0, 2)}
        cap = jnp.logical_and(row3 == 7, at_north)
        for c in (0, 2):
            value = ghost(n, c)
            for b in range(2):
                fn[c][b] = jnp.where(cap, value, fn[c][b])
        new = []
        for b in range(4):
            m = metric3[b // 2]
            curl = (NORTH * (fn[2][b] - f[2][b]) - RADIAL * (up[1][b] - f[1][b]),
                    RADIAL * (up[0][b] - f[0][b]) - m * (fe[2][b] - f[2][b]),
                    m * (fe[1][b] - f[1][b]) - NORTH * (fn[0][b] - f[0][b]))
            new.append([hh[b, c, 1:9] - curl[c] for c in range(3)])

        def store(b, c, v):
            hh[b, c, 1:9] = v

        merge_all(new, store)

    def backward(n):
        f = [[hh[b, c, 1:9] for b in range(4)] for c in range(3)]
        down = [[hh[b, c, 0:8] for b in range(4)] for c in range(2)]
        fw = {c: turn(f[c], 1, 2) for c in (1, 2)}
        fs = {c: turn(f[c], 1, 1) for c in (0, 2)}
        cap = jnp.logical_and(row3 == 0, at_south)
        for c in (0, 2):
            value = ghost(n, c)
            for b in range(2):
                fs[c][b] = jnp.where(cap, value, fs[c][b])
        new = []
        for b in range(4):
            m = metric3[b // 2]
            curl = (NORTH * (f[2][b] - fs[2][b]) - RADIAL * (f[1][b] - down[1][b]),
                    RADIAL * (f[0][b] - down[0][b]) - m * (f[2][b] - fw[2][b]),
                    m * (f[1][b] - fw[1][b]) - NORTH * (f[0][b] - fs[0][b]))
            old = [ee[b, c, 0:8] for c in range(3)]
            drive = [2.0 * old[c] + curl[c] for c in range(3)]
            new.append([uu[b, 3 * a, 0:8] * drive[0] + uu[b, 3 * a + 1, 0:8] * drive[1] + uu[b, 3 * a + 2, 0:8] * drive[2] - old[a]
                        for a in range(3)])

        def store(b, c, v):
            ee[b, c, 0:8] = v

        merge_all(new, store)

    def step(n, _):
        forward(n)
        backward(n)
        return 0

    lax.fori_loop(0, STEPS, step, 0)
    for c in range(3):
        eo_ref[c] = ee[0, c, pl.ds(0, 8)]
        ho_ref[c] = hh[0, c, pl.ds(1, 8)]

    for n in range(2):
        for copy in to_lon[n]:
            copy.wait_send()

    @pl.when(inner_north)
    def _():
        for copy in to_north[0] + to_north[1] + rows_north:
            copy.wait_send()

    @pl.when(inner_south)
    def _():
        for copy in to_south[0] + to_south[1] + rows_south:
            copy.wait_send()

    @pl.when(pole)
    def _():
        pltpu.make_async_copy(caps, caps, cap_send.at[0]).wait()

    for is_north, condition in poles:
        @pl.when(condition)
        def _():
            pole_copy(is_north).wait_send()


def write_out(e_kept, h_kept, e_out, h_out, sem):
    copies = [pltpu.make_async_copy(e_kept, e_out, sem.at[0]), pltpu.make_async_copy(h_kept, h_out, sem.at[1])]
    for copy in copies:
        copy.start()
    for copy in copies:
        copy.wait()


def solution(mesh):
    bands, lons = mesh.shape["band"], mesh.shape["lon"]

    def on_device(e, h, c, zone_factor, zone_bounds):
        vmem, hbm = (pl.BlockSpec(memory_space=m) for m in (pltpu.VMEM, pltpu.HBM))
        f32 = lambda *shape: pltpu.VMEM(shape, jnp.float32)
        kept = pltpu.VMEM(e.shape, e.dtype)
        inputs = [pltpu.with_memory_space_constraint(x, pltpu.HBM) for x in (zone_factor, zone_bounds, e, h, c)]
        fields = pl.pallas_call(
            functools.partial(kernel, bands=bands, lons=lons),
            out_shape=(kept, kept),
            in_specs=[hbm] * 5,
            out_specs=(vmem, vmem),
            scratch_shapes=[
                pltpu.SMEM(zone_factor.shape, jnp.int32), pltpu.SMEM(zone_bounds.shape, jnp.int32),
                f32(3, 8, 8, 128), f32(3, 8, 8, 128), f32(9, 8, 8, 128),
                f32(3, 8, 8, 128), f32(3, 8, 8, 128), f32(9, 8, 8, 128),
                f32(2, 2 * FIELDS, 8, 128), f32(2, 2 * FIELDS, 8, 128), f32(2, 2 * FIELDS, 8, 128),
                f32(64, 8, 128), f32(32, 8, 128), f32(32, 8, 128), f32(64, 8, 128),
                f32(4, 3, 9, 8, 128), f32(4, 3, 9, 8, 128), f32(4, 9, 8, 8, 128),
                f32(8, 128), f32(lons - 1, 8, 128), f32(STEPS, 2, 8, 128),
                pltpu.SemaphoreType.DMA((5,)), pltpu.SemaphoreType.DMA((19,)), pltpu.SemaphoreType.DMA((19,)),
                pltpu.SemaphoreType.DMA((1,)), pltpu.SemaphoreType.DMA((1,)),
            ],
            compiler_params=pltpu.CompilerParams(collective_id=0, has_side_effects=True, vmem_limit_bytes=60 * 1024 * 1024),
        )(*inputs)
        like = jax.ShapeDtypeStruct(e.shape, e.dtype)
        return pl.pallas_call(
            write_out,
            out_shape=(like, like),
            in_specs=[vmem, vmem],
            out_specs=(hbm, hbm),
            scratch_shapes=[pltpu.SemaphoreType.DMA((2,))],
        )(*(pltpu.with_memory_space_constraint(x, pltpu.VMEM) for x in fields))

    spread = P(None, None, "band", "lon")
    return jax.shard_map(on_device, mesh=mesh, in_specs=(spread, spread, spread, P(), P()), out_specs=(spread, spread),
                         check_vma=False)
```

```python
import functools

import jax
import jax.numpy as jnp
from jax import lax
from jax.experimental import pallas as pl
from jax.experimental.pallas import tpu as pltpu
from jax.sharding import PartitionSpec as P

MESH = pl.DeviceIdType.MESH
STEPS = 4
NORTH, RADIAL, EAST, FLOOR = 0.45, 0.5, 0.12, 0.25
FIELDS = 15


def lane_ids():
    return lax.broadcasted_iota(jnp.int32, (8, 128), 1)


def row_ids():
    return lax.broadcasted_iota(jnp.int32, (8, 128), 0)


def roll(x, by, axis):
    by = by % x.shape[axis]
    return x if by == 0 else pltpu.roll(x, by, axis)


def pair_shift(main, edge, by, axis):
    ids = lane_ids() if axis == 1 else row_ids()
    last = ids == (0 if by == 1 else (127 if axis == 1 else 7))
    rolled_main, rolled_edge = roll(main, by, axis), roll(edge, by, axis)
    return jnp.where(last, rolled_edge, rolled_main), jnp.where(last, rolled_main, rolled_edge)


def merge(x, gates):
    lanes = lane_ids()
    for step, gate in zip((1, 2, 4), gates):
        other = jnp.take_along_axis(x, lanes ^ step, axis=1)
        x = x + jnp.where(gate, other, x)
    return x * 0.125


def inverse(c):
    m = [[c[0] + 1.0, c[1], c[2]], [c[3], c[4] + 1.0, c[5]], [c[6], c[7], c[8] + 1.0]]

    def cof(a, b):
        i, j, p, q = (a + 1) % 3, (a + 2) % 3, (b + 1) % 3, (b + 2) % 3
        return m[i][p] * m[j][q] - m[i][q] * m[j][p]

    cofs = [[cof(a, b) for b in range(3)] for a in range(3)]
    det = m[0][0] * cofs[0][0] + m[0][1] * cofs[0][1] + m[0][2] * cofs[0][2]
    inv = 1.0 / det
    return [cofs[b][a] * inv for a in range(3) for b in range(3)]


def row_tables(zf, zb, rows, total):
    factor = jnp.full((8, 128), zf[0], jnp.int32)
    for z in range(zb.shape[0]):
        factor = jnp.where(rows >= zb[z], zf[z + 1], factor)
    lat = ((rows.astype(jnp.float32) + 0.5) / total - 0.5) * jnp.pi
    metric = EAST / jnp.maximum(factor.astype(jnp.float32) * jnp.cos(lat), FLOOR)
    return metric, factor


def batched(fn, tiles):
    whole = fn(jnp.concatenate(tiles, axis=0))
    return [whole[8 * i : 8 * i + 8] for i in range(len(tiles))]


def total_of(terms):
    out = None
    for factor, tile in terms:
        if tile is None:
            continue
        if out is None:
            out = tile if isinstance(factor, float) and factor == 1.0 else factor * tile
        elif isinstance(factor, float) and factor == 1.0:
            out = out + tile
        elif isinstance(factor, float) and factor == -1.0:
            out = out - tile
        else:
            out = out + factor * tile
    return out


class PoleRows:
    def __init__(self, at_north, metric, gates):
        self.at_north, self.metric, self.gates = at_north, metric, gates

    def shift_layer(self, field, c, r, source, by):
        rows = row_ids()
        key = source if source == "free" else (source[0], source[1] + by)
        tile = field.get((c, r, key))
        if tile is None:
            return None
        return jnp.where(rows == (7 if by == 1 else 0), 0.0, pltpu.roll(tile, 7 if by == 1 else 1, 0))

    def turn(self, field, comps, by):
        ids = [i for i in field if i[0] in comps]
        return dict(zip(ids, batched(lambda x: pltpu.roll(x, by % 128, 1), [field[i] for i in ids]))) if ids else {}

    def merge(self, field):
        ids = list(field)
        tiles = [field[i] for i in ids]
        for level, step in enumerate((1, 2, 4)):
            def swap(x):
                return jnp.take_along_axis(x, lax.broadcasted_iota(jnp.int32, x.shape, 1) ^ step, axis=1)
            others = batched(swap, tiles)
            tiles = [t + jnp.where(self.gates[i[1]][level], o, t) for i, t, o in zip(ids, tiles, others)]
        return {i: t * 0.125 for i, t in zip(ids, tiles)}

    def keys(self, field, spread, extra=()):
        found = []
        for source in [i[2] for i in field] + list(extra):
            for s in ([source] if source == "free" else [source, (source[0], source[1] + spread)]):
                if s not in found:
                    found.append(s)
        return found

    def forward(self, e, h, wanted, merged=True):
        ahead = -1 if self.at_north else 1
        fe = self.turn(e, (1, 2), -1)
        new = {}
        for source in self.keys(e, -1, [i[2] for i in h]):
            for c, r in wanted:
                m = self.metric[r]
                up = lambda c: self.shift_layer(e, c, r, source, 1)
                at = lambda c: e.get((c, r, source))
                north = lambda c: e.get((c, r + ahead, source))
                east = lambda c: fe.get((c, r, source))
                if c == 0:
                    curl = [(-NORTH, north(2)), (NORTH, at(2)), (RADIAL, up(1)), (-RADIAL, at(1))]
                elif c == 1:
                    curl = [(-RADIAL, up(0)), (RADIAL, at(0)), (m, east(2)), (-m, at(2))]
                else:
                    curl = [(-m, east(1)), (m, at(1)), (NORTH, north(0)), (-NORTH, at(0))]
                tile = total_of([(1.0, h.get((c, r, source)))] + curl)
                if tile is not None:
                    new[c, r, source] = tile
        return self.merge(new) if merged else new

    def drive(self, e, h, rows):
        behind = 1 if self.at_north else -1
        fw = self.turn(h, (1, 2), 1)
        new = {}
        for source in self.keys(h, 1, [i[2] for i in e]):
            for r in rows:
                m = self.metric[r]
                down = lambda c: self.shift_layer(h, c, r, source, -1)
                at = lambda c: h.get((c, r, source))
                south = lambda c: h.get((c, r + behind, source))
                west = lambda c: fw.get((c, r, source))
                curls = ([(NORTH, at(2)), (-NORTH, south(2)), (-RADIAL, at(1)), (RADIAL, down(1))],
                         [(RADIAL, at(0)), (-RADIAL, down(0)), (-m, at(2)), (m, west(2))],
                         [(m, at(1)), (-m, west(1)), (-NORTH, at(0)), (NORTH, south(0))])
                for c in range(3):
                    tile = total_of([(2.0, e.get((c, r, source)))] + curls[c])
                    if tile is not None:
                        new[c, r, source] = tile
        return new

    def update(self, u, drive, e, wanted, merged=True):
        new = {}
        for source in self.keys(drive, 0, [i[2] for i in e]):
            for a, r in wanted:
                tile = total_of([(u[3 * a + c, r], drive.get((c, r, source))) for c in range(3)]
                                + [(-1.0, e.get((a, r, source)))])
                if tile is not None:
                    new[a, r, source] = tile
        return self.merge(new) if merged else new


def every(rows):
    return [(c, r) for r in rows for c in range(3)]


def only(field, source):
    return {i: t for i, t in field.items() if (i[2] == "free") == source}


def pole_chain(at_north, load, metric, gates):
    p = PoleRows(at_north, metric, gates)
    deep = range(4) if at_north else range(5)
    e = {(c, r, "free"): load("e", c, r) for c in range(3) for r in deep}
    h = {(c, r, "free"): load("h", c, r) for c in range(3) for r in range(4)}
    u = {(i, r): v for r in range(3 if at_north else 4) for i, v in enumerate(inverse([load("c", i, r) for i in range(9)]))}
    out = {}

    def note(n, field, initial=False):
        for (c, r, source), tile in field.items():
            if r == 0 and c != 1:
                out[("free", n) if source == "free" else ("response", n) + source, c] = tile

    unit = jnp.ones((8, 128), jnp.float32)
    ends = [(0, 0), (2, 0)]
    if at_north:
        note(0, e)
        h = p.forward(e, h, every(range(4)))
        h[0, 0, (2, 0)] = -NORTH * unit
        h[2, 0, (0, 0)] = NORTH * unit
        def back(e, h, free_rows, rows, wanted=None, merged=True):
            new = {}
            for free, rr in ((True, free_rows), (False, rows)):
                ee, hh = only(e, free), only(h, free)
                d = p.drive(ee, hh, rr)
                new.update({(i, free): t for i, t in d.items()})
            drive = {i: t for (i, _), t in new.items()}
            want = wanted or every(sorted(set(free_rows) | set(rows)))
            return p.update(u, drive, {i: t for i, t in e.items() if (i[1] in (free_rows if i[2] == "free" else rows))}, want, merged)

        e = back(e, h, range(3), range(1))
        note(1, e)
        h = p.forward(e, h, every(range(3)))
        h = {i: t for i, t in h.items() if i[2] == "free" or i[1] < 2}
        e = back(e, h, range(2), range(2))
        note(2, e)
        h = p.forward(e, h, every(range(2)))
        e = back(e, h, range(1), range(1), ends, False)
        note(3, e)
    else:
        h = p.forward(e, h, every(range(4)))
        note(0, h)
        drive = p.drive(e, h, range(4))
        drive[0, 0, (2, 0)] = -NORTH * unit
        drive[2, 0, (0, 0)] = NORTH * unit
        e = p.update(u, drive, {i: t for i, t in e.items() if i[1] < 4}, every(range(4)))
        h = p.forward(e, {i: t for i, t in h.items() if i[1] < 3}, every(range(3)))
        note(1, h)
        drive = p.drive(e, h, range(3))
        e = p.update(u, drive, {i: t for i, t in e.items() if i[1] < 3}, every(range(3)))
        h = p.forward(e, {i: t for i, t in h.items() if i[1] < 2}, every(range(2)))
        note(2, h)
        drive = p.drive(e, h, range(2))
        e = p.update(u, drive, {i: t for i, t in e.items() if i[1] < 2}, every(range(2)))
        h = p.forward(e, {i: t for i, t in h.items() if i[1] < 1}, ends, False)
        note(3, h)
    return out


def pole_items(at_north):
    return ([("e", c, r) for c in range(3) for r in range(4 if at_north else 5)] + [("h", c, r) for c in range(3) for r in range(4)]
            + [("c", i, r) for i in range(9) for r in range(3 if at_north else 4)])


def columns(tiles):
    lanes = lane_ids()
    count = 128
    tiles = tiles + [None] * (count - len(tiles))
    while count > 1:
        count //= 2
        first, second = tiles[:count], tiles[count:]
        low = (lanes & count) == 0
        zero = jnp.zeros((8, 128), jnp.float32)
        pairs = [(a, b) for a, b in zip(first, second) if a is not None]
        give = [jnp.where(low, zero if b is None else b, a) for a, b in pairs]
        take = [jnp.where(low, a, zero if b is None else b) for a, b in pairs]
        swapped = batched(lambda x: jnp.take_along_axis(x, lax.broadcasted_iota(jnp.int32, x.shape, 1) ^ count, axis=1), give)
        tiles = [t + s for t, s in zip(take, swapped)]
        tiles = tiles + [None] * (count - len(tiles))
    return tiles[0]


def solve_caps(names, total):
    rows = row_ids()
    spread = dict(zip(names, batched(lambda x: x, [jnp.take_along_axis(total, jnp.full((8, 128), q, jnp.int32), axis=1)
                                                   for q in range(len(names))])))
    caps = []

    def moved(tile, d):
        if d == 0:
            return tile
        kept = rows >= d if d > 0 else rows < 8 + d
        return jnp.where(kept, pltpu.roll(tile, d % 8, 0), 0.0)

    for n in range(STEPS):
        value = {c: spread[("free", n), c] for c in (0, 2)}
        for m in range(n):
            shifted = {}
            for name, c in names:
                if name[0] == "response" and name[1] == n - m:
                    if name[2:] not in shifted:
                        shifted[name[2:]] = moved(caps[m][name[2]], name[3])
                    value[c] = value[c] + spread[name, c] * shifted[name[2:]]
        caps.append(value)
    return caps


def kernel(zf_in, zb_in, e_in, h_in, c_in, eo_ref, ho_ref, zf, zb, e_ref, h_ref, c_ref, rows_e, rows_h, rows_c, pack, got, got2, pole_own, pole_pack, pole_got, pole_sum, ee, hh, uu, mine,
           caps, sums, load_sem, send, recv, cap_send, cap_recv, go, *, bands, lons):
    band, lon = lax.axis_index("band"), lax.axis_index("lon")
    at_south, at_north = band == 0, band == bands - 1
    inner_north, inner_south = jnp.logical_not(at_north), jnp.logical_not(at_south)
    north, south = band + 1, band - 1
    east, west = lax.rem(lon + 1, lons), lax.rem(lon + lons - 1, lons)
    pole = jnp.logical_or(at_south, at_north)

    loads = [pltpu.make_async_copy(s, d, load_sem.at[i]) for i, (s, d) in enumerate(((e_in, e_ref), (h_in, h_ref), (c_in, c_ref), (zf_in, zf), (zb_in, zb)))]
    for load in loads:
        load.start()

    barrier = pltpu.get_barrier_semaphore()

    def greet(b, l):
        pl.semaphore_signal(barrier, inc=1, device_id=(b, l), device_id_type=MESH)

    greet(band, east)
    greet(band, west)

    @pl.when(inner_north)
    def _():
        for l in (east, west, lon):
            greet(north, l)

    @pl.when(inner_south)
    def _():
        for l in (east, west, lon):
            greet(south, l)

    @pl.when(pole)
    def _():
        def one(d, _):
            greet(band, lax.rem(lon + d, lons))
            return 0
        lax.fori_loop(2, lons - 1, one, 0)

    lanes, rows = lane_ids(), row_ids()

    def pack_field(ref, first, count):
        def one(i, _):
            tiles = [(c, a) for c in range(3) for a in range(2)]
            rolled = [[roll(ref[i * 3 + c, a * 4 + q], 32 * q, 1) for q in range(4)] for c, a in tiles]
            for n, t in enumerate(rolled):
                lo, hi = t[0], t[1]
                for q in range(1, 4):
                    lo = jnp.where(lanes // 32 == q, t[q], lo)
                    if q > 1:
                        hi = jnp.where(lanes // 32 == q - 1, t[q], hi)
                hi = jnp.where(lanes // 32 == 3, t[0], hi)
                pack[0, first * 2 + i * 6 + n] = lo
                pack[1, first * 2 + i * 6 + n] = hi
            return 0
        if count == 3:
            one(0, 0)
        else:
            lax.fori_loop(0, count // 3, one, 0)

    def remote(src, dst, i, b, l):
        return pltpu.make_async_remote_copy(src_ref=src, dst_ref=dst, send_sem=send.at[i], recv_sem=recv.at[i],
                                            device_id=(b, l), device_id_type=MESH)

    fields, conduct = pl.ds(0, 12), pl.ds(12, 18)
    to_lon = [[remote(pack.at[k, part], got.at[k, part], 2 * n + k, band, (west, east)[k]) for k in range(2)]
              for n, part in enumerate((fields, conduct))]
    to_north = [[remote(pack.at[k, part, pl.ds(8 - d[k], d[k])], got2.at[k, part, pl.ds(8 - d[k], d[k])], 4 + 2 * n + k, north, (west, east)[k])
                 for k in range(2)] for n, (part, d) in enumerate(((fields, (4, 3)), (conduct, (3, 2))))]
    to_south = [[remote(pack.at[k, part, pl.ds(0, d[k])], got2.at[k, part, pl.ds(0, d[k])], 8 + 2 * n + k, south, (west, east)[k])
                 for k in range(2)] for n, (part, d) in enumerate(((fields, (3, 4)), (conduct, (2, 3))))]
    trio = ((e_ref, rows_e), (h_ref, rows_h), (c_ref, rows_c))
    rows_north = [remote(s.at[:, :, pl.ds(8 - d, d)], t.at[:, :, pl.ds(8 - d, d)], 12 + i, north, lon)
                  for i, ((s, t), d) in enumerate(zip(trio, (4, 4, 3)))]
    rows_south = [remote(s.at[:, :, pl.ds(0, d)], t.at[:, :, pl.ds(0, d)], 15 + i, south, lon)
                  for i, ((s, t), d) in enumerate(zip(trio, (4, 3, 3)))]

    def send_part(n):
        for copy in to_lon[n]:
            copy.start()

        @pl.when(inner_north)
        def _():
            for copy in to_north[n] + (rows_north[:2] if n == 0 else rows_north[2:]):
                copy.start()

        @pl.when(inner_south)
        def _():
            for copy in to_south[n] + (rows_south[:2] if n == 0 else rows_south[2:]):
                copy.start()

    loads[0].wait()
    loads[1].wait()
    poles = ((True, at_north), (False, at_south))
    refs = {"e": e_ref, "h": h_ref, "c": c_ref}

    def pole_copy(is_north):
        part = pl.ds(0, (len(pole_items(is_north)) + 1) // 2)
        return remote(pole_pack.at[part], pole_got.at[part], 18, band, east)

    @pl.when(pole)
    def _():
        loads[2].wait()

    for is_north, condition in poles:
        @pl.when(condition)
        def _():
            tiles = [refs[kind][i, pl.ds(0, 8), 7 - r if is_north else r, :] for kind, i, r in pole_items(is_north)]
            for n, tile in enumerate(tiles):
                pole_own[n] = tile
            for n in range(0, len(tiles), 2):
                pole_pack[n // 2] = jnp.where(lanes < 64, pltpu.roll(tiles[n], 64, 1), tiles[min(n + 1, len(tiles) - 1)])

    pack_field(e_ref, 0, 3)
    pack_field(h_ref, 3, 3)

    @pl.when(jnp.logical_not(pole))
    def _():
        pl.semaphore_wait(barrier, 8)

    @pl.when(band == 1)
    def _():
        pl.semaphore_signal(go, inc=1, device_id=(south, lon), device_id_type=MESH)

    @pl.when(band == bands - 2)
    def _():
        pl.semaphore_signal(go, inc=1, device_id=(north, lon), device_id_type=MESH)

    @pl.when(pole)
    def _():
        pl.semaphore_wait(go, 1)

    for is_north, condition in poles:
        @pl.when(condition)
        def _():
            pole_copy(is_north).start()

    send_part(0)

    @pl.when(jnp.logical_not(pole))
    def _():
        loads[2].wait()

    pack_field(c_ref, 6, 9)
    send_part(1)

    loads[3].wait()
    loads[4].wait()
    metric, factors, gates = [], [], []
    for block in range(2):
        shift = 0 if block == 0 else jnp.where(rows < 4, 8, -8)
        m, f = row_tables(zf, zb, band * 8 + rows + shift, 8 * bands)
        metric.append(m)
        factors.append(f)
        gates.append([f > s for s in (1, 2, 4)])
    zero = jnp.zeros((8, 128), jnp.float32)
    for b in range(4):
        for c in range(3):
            ee[b, c, 8] = zero
            hh[b, c, 0] = zero
    for n in range(STEPS):
        for i in range(2):
            sums[n, i] = zero

    def take_in(block, layer, load):
        for c in range(3):
            ee[block, c, layer] = load(c)
            hh[block, c, layer + 1] = load(3 + c)
        for i, value in enumerate(inverse([load(6 + c) for c in range(9)])):
            uu[block, i, layer] = value

    def own(k, _):
        take_in(0, k, lambda f: e_ref[f, k] if f < 3 else (h_ref[f - 3, k] if f < 6 else c_ref[f - 6, k]))
        return 0


    def unpack(block, ref):
        def one(a, _):
            for q in range(4):
                tiles = [roll(jnp.where(lanes // 32 == q, ref[0, 2 * f + a], ref[1, 2 * f + a]), -32 * q, 1) for f in range(FIELDS)]
                take_in(block, a * 4 + q, lambda f: tiles[f])
            return 0
        lax.fori_loop(0, 2, one, 0)

    offsets = sorted(((i // 32, i // 8 % 4, i % 8) for i in range(1, 64)),
                     key=lambda o: 4 * o[0] + min(o[1], 4 - o[1]) + min(o[2], 8 - o[2]))

    def cap_copy(n, offset):
        hi, x, z = lon // 32, lax.rem(lon // 8, 4), lax.rem(lon, 8)
        target = lax.rem(hi + offset[0], 2) * 32 + lax.rem(x + offset[1], 4) * 8 + lax.rem(z + offset[2], 8)
        return pltpu.make_async_remote_copy(src_ref=mine, dst_ref=caps.at[n], send_sem=cap_send.at[0], recv_sem=cap_recv.at[0],
                                            device_id=(band, target), device_id_type=MESH)

    names = {}
    for is_north, condition in poles:
        @pl.when(condition)
        def _():
            items = pole_items(is_north)
            place = {item: n for n, item in enumerate(items)}
            edge = [7 - r if is_north else r for r in range(5)]
            m = [jnp.broadcast_to(metric[0][r : r + 1, :], (8, 128)) for r in edge]
            f = [jnp.broadcast_to(factors[0][r : r + 1, :], (8, 128)) for r in edge]
            g = [[x > k for k in (1, 2, 4)] for x in f]

            def seam(kind, i, r):
                n = place[kind, i, r]
                tile = pole_got[n // 2]
                return jnp.where(lanes < 64, tile if n % 2 == 0 else pltpu.roll(tile, 64, 1), pltpu.roll(pole_own[n], 64, 1))

            inner = pole_chain(is_north, lambda kind, i, r: pole_own[place[kind, i, r]], m, g)
            names[is_north] = list(inner)
            for n, tile in enumerate(inner.values()):
                pole_sum[n] = tile
            pole_copy(is_north).wait_recv()
            outer = pole_chain(is_north, seam, m, g)
            inside = jnp.logical_and(lanes >= 32, lanes < 96)
            mine[...] = columns([jnp.where(inside, pole_sum[n] + outer[name], 0.0) for n, name in enumerate(names[is_north])])

    @pl.when(pole)
    def _():
        pl.semaphore_wait(barrier, lons - 1 + 3)
        for n, offset in enumerate(offsets):
            cap_copy(n, offset).start()

    lax.fori_loop(0, 8, own, 0)

    for n in range(2):
        for copy in to_lon[n]:
            copy.wait_recv()
    unpack(1, got)

    @pl.when(inner_north)
    def _():
        for n in range(2):
            for copy in to_south[n]:
                copy.wait_recv()
        for copy in rows_south:
            copy.wait_recv()

    @pl.when(inner_south)
    def _():
        for n in range(2):
            for copy in to_north[n]:
                copy.wait_recv()
        for copy in rows_north:
            copy.wait_recv()

    def outer(k, _):
        take_in(2, k, lambda f: rows_e[f, k] if f < 3 else (rows_h[f - 3, k] if f < 6 else rows_c[f - 6, k]))
        return 0

    lax.fori_loop(0, 8, outer, 0)
    unpack(3, got2)

    @pl.when(pole)
    def _():
        pltpu.make_async_copy(caps, caps, cap_recv.at[0]).wait()

    for is_north, condition in poles:
        @pl.when(condition)
        def _():
            total = (mine[...] + jnp.sum(caps[...], axis=0)) * (1.0 / (128 * lons))
            for n, value in enumerate(solve_caps(names[is_north], total)):
                sums[n, 0] = value[0]
                sums[n, 1] = value[2]

    lane3 = lax.broadcasted_iota(jnp.int32, (8, 8, 128), 2)
    row3 = lax.broadcasted_iota(jnp.int32, (8, 8, 128), 1)
    metric3 = [jnp.broadcast_to(m, (8, 8, 128)) for m in metric]
    gates3 = [[jnp.broadcast_to(g, (8, 8, 128)).reshape(64, 128) for g in gs] for gs in gates]
    lane2 = lax.broadcasted_iota(jnp.int32, (64, 128), 1)

    def turn(f, by, axis):
        size = 128 if axis == 2 else 8
        seam = (lane3 if axis == 2 else row3) == (0 if by == 1 else size - 1)
        moved = [pltpu.roll(x.reshape(64, 128), by % 128, 1).reshape(8, 8, 128) if axis == 2 else pltpu.roll(x, by % 8, 1) for x in f]
        other = (1, 0, 3, 2) if axis == 2 else (2, 3, 0, 1)
        return [jnp.where(seam, moved[other[b]], moved[b]) for b in range(4)]

    def merge_all(f, store):
        x = {(b, c): f[b][c].reshape(64, 128) for b in range(4) for c in range(3)}
        for level, step in enumerate((1, 2, 4)):
            other = {i: jnp.take_along_axis(v, lane2 ^ step, axis=1) for i, v in x.items()}
            x = {(b, c): v + jnp.where(gates3[b // 2][level], other[b, c], v) for (b, c), v in x.items()}
        for (b, c), v in x.items():
            store(b, c, (v * 0.125).reshape(8, 8, 128))

    def ghost(n, c):
        return jnp.concatenate([jnp.broadcast_to(sums[n, c // 2, k : k + 1, :].reshape(1, 1, 128), (1, 8, 128)) for k in range(8)])

    def forward(n):
        f = [[ee[b, c, 0:8] for b in range(4)] for c in range(3)]
        up = [[ee[b, c, 1:9] for b in range(4)] for c in range(2)]
        fe = {c: turn(f[c], -1, 2) for c in (1, 2)}
        fn = {c: turn(f[c], -1, 1) for c in (0, 2)}
        cap = jnp.logical_and(row3 == 7, at_north)
        for c in (0, 2):
            value = ghost(n, c)
            for b in range(2):
                fn[c][b] = jnp.where(cap, value, fn[c][b])
        new = []
        for b in range(4):
            m = metric3[b // 2]
            curl = (NORTH * (fn[2][b] - f[2][b]) - RADIAL * (up[1][b] - f[1][b]),
                    RADIAL * (up[0][b] - f[0][b]) - m * (fe[2][b] - f[2][b]),
                    m * (fe[1][b] - f[1][b]) - NORTH * (fn[0][b] - f[0][b]))
            new.append([hh[b, c, 1:9] - curl[c] for c in range(3)])

        def store(b, c, v):
            hh[b, c, 1:9] = v

        merge_all(new, store)

    def backward(n):
        f = [[hh[b, c, 1:9] for b in range(4)] for c in range(3)]
        down = [[hh[b, c, 0:8] for b in range(4)] for c in range(2)]
        fw = {c: turn(f[c], 1, 2) for c in (1, 2)}
        fs = {c: turn(f[c], 1, 1) for c in (0, 2)}
        cap = jnp.logical_and(row3 == 0, at_south)
        for c in (0, 2):
            value = ghost(n, c)
            for b in range(2):
                fs[c][b] = jnp.where(cap, value, fs[c][b])
        new = []
        for b in range(4):
            m = metric3[b // 2]
            curl = (NORTH * (f[2][b] - fs[2][b]) - RADIAL * (f[1][b] - down[1][b]),
                    RADIAL * (f[0][b] - down[0][b]) - m * (f[2][b] - fw[2][b]),
                    m * (f[1][b] - fw[1][b]) - NORTH * (f[0][b] - fs[0][b]))
            old = [ee[b, c, 0:8] for c in range(3)]
            drive = [2.0 * old[c] + curl[c] for c in range(3)]
            new.append([uu[b, 3 * a, 0:8] * drive[0] + uu[b, 3 * a + 1, 0:8] * drive[1] + uu[b, 3 * a + 2, 0:8] * drive[2] - old[a]
                        for a in range(3)])

        def store(b, c, v):
            ee[b, c, 0:8] = v

        merge_all(new, store)

    def step(n, _):
        forward(n)
        backward(n)
        return 0

    lax.fori_loop(0, STEPS, step, 0)
    for c in range(3):
        eo_ref[c] = ee[0, c, pl.ds(0, 8)]
        ho_ref[c] = hh[0, c, pl.ds(1, 8)]

    for n in range(2):
        for copy in to_lon[n]:
            copy.wait_send()

    @pl.when(inner_north)
    def _():
        for copy in to_north[0] + to_north[1] + rows_north:
            copy.wait_send()

    @pl.when(inner_south)
    def _():
        for copy in to_south[0] + to_south[1] + rows_south:
            copy.wait_send()

    @pl.when(pole)
    def _():
        pltpu.make_async_copy(caps, caps, cap_send.at[0]).wait()

    for is_north, condition in poles:
        @pl.when(condition)
        def _():
            pole_copy(is_north).wait_send()


def write_out(e_kept, h_kept, e_out, h_out, sem):
    copies = [pltpu.make_async_copy(e_kept, e_out, sem.at[0]), pltpu.make_async_copy(h_kept, h_out, sem.at[1])]
    for copy in copies:
        copy.start()
    for copy in copies:
        copy.wait()


def solution(mesh):
    bands, lons = mesh.shape["band"], mesh.shape["lon"]

    def on_device(e, h, c, zone_factor, zone_bounds):
        vmem, hbm = (pl.BlockSpec(memory_space=m) for m in (pltpu.VMEM, pltpu.HBM))
        f32 = lambda *shape: pltpu.VMEM(shape, jnp.float32)
        kept = pltpu.VMEM(e.shape, e.dtype)
        inputs = [pltpu.with_memory_space_constraint(x, pltpu.HBM) for x in (zone_factor, zone_bounds, e, h, c)]
        fields = pl.pallas_call(
            functools.partial(kernel, bands=bands, lons=lons),
            out_shape=(kept, kept),
            in_specs=[hbm] * 5,
            out_specs=(vmem, vmem),
            scratch_shapes=[
                pltpu.SMEM(zone_factor.shape, jnp.int32), pltpu.SMEM(zone_bounds.shape, jnp.int32),
                f32(3, 8, 8, 128), f32(3, 8, 8, 128), f32(9, 8, 8, 128),
                f32(3, 8, 8, 128), f32(3, 8, 8, 128), f32(9, 8, 8, 128),
                f32(2, 2 * FIELDS, 8, 128), f32(2, 2 * FIELDS, 8, 128), f32(2, 2 * FIELDS, 8, 128),
                f32(64, 8, 128), f32(32, 8, 128), f32(32, 8, 128), f32(64, 8, 128),
                f32(4, 3, 9, 8, 128), f32(4, 3, 9, 8, 128), f32(4, 9, 8, 8, 128),
                f32(8, 128), f32(lons - 1, 8, 128), f32(STEPS, 2, 8, 128),
                pltpu.SemaphoreType.DMA((5,)), pltpu.SemaphoreType.DMA((19,)), pltpu.SemaphoreType.DMA((19,)),
                pltpu.SemaphoreType.DMA((1,)), pltpu.SemaphoreType.DMA((1,)), pltpu.SemaphoreType.REGULAR,
            ],
            compiler_params=pltpu.CompilerParams(collective_id=0, has_side_effects=True, vmem_limit_bytes=60 * 1024 * 1024),
        )(*inputs)
        like = jax.ShapeDtypeStruct(e.shape, e.dtype)
        return pl.pallas_call(
            write_out,
            out_shape=(like, like),
            in_specs=[vmem, vmem],
            out_specs=(hbm, hbm),
            scratch_shapes=[pltpu.SemaphoreType.DMA((2,))],
        )(*(pltpu.with_memory_space_constraint(x, pltpu.VMEM) for x in fields))

    spread = P(None, None, "band", "lon")
    return jax.shard_map(on_device, mesh=mesh, in_specs=(spread, spread, spread, P(), P()), out_specs=(spread, spread),
                         check_vma=False)
```

```python
import functools

import jax
import jax.numpy as jnp
from jax import lax
from jax.experimental import pallas as pl
from jax.experimental.pallas import tpu as pltpu
from jax.sharding import PartitionSpec as P

MESH = pl.DeviceIdType.MESH
STEPS = 4
NORTH, RADIAL, EAST, FLOOR = 0.45, 0.5, 0.12, 0.25
FIELDS = 15


def lane_ids():
    return lax.broadcasted_iota(jnp.int32, (8, 128), 1)


def row_ids():
    return lax.broadcasted_iota(jnp.int32, (8, 128), 0)


def roll(x, by, axis):
    by = by % x.shape[axis]
    return x if by == 0 else pltpu.roll(x, by, axis)


def pair_shift(main, edge, by, axis):
    ids = lane_ids() if axis == 1 else row_ids()
    last = ids == (0 if by == 1 else (127 if axis == 1 else 7))
    rolled_main, rolled_edge = roll(main, by, axis), roll(edge, by, axis)
    return jnp.where(last, rolled_edge, rolled_main), jnp.where(last, rolled_main, rolled_edge)


def merge(x, gates):
    lanes = lane_ids()
    for step, gate in zip((1, 2, 4), gates):
        other = jnp.take_along_axis(x, lanes ^ step, axis=1)
        x = x + jnp.where(gate, other, x)
    return x * 0.125


def inverse(c):
    m = [[c[0] + 1.0, c[1], c[2]], [c[3], c[4] + 1.0, c[5]], [c[6], c[7], c[8] + 1.0]]

    def cof(a, b):
        i, j, p, q = (a + 1) % 3, (a + 2) % 3, (b + 1) % 3, (b + 2) % 3
        return m[i][p] * m[j][q] - m[i][q] * m[j][p]

    cofs = [[cof(a, b) for b in range(3)] for a in range(3)]
    det = m[0][0] * cofs[0][0] + m[0][1] * cofs[0][1] + m[0][2] * cofs[0][2]
    inv = 1.0 / det
    return [cofs[b][a] * inv for a in range(3) for b in range(3)]


def row_tables(zf, zb, rows, total):
    factor = jnp.full((8, 128), zf[0], jnp.int32)
    for z in range(zb.shape[0]):
        factor = jnp.where(rows >= zb[z], zf[z + 1], factor)
    lat = ((rows.astype(jnp.float32) + 0.5) / total - 0.5) * jnp.pi
    metric = EAST / jnp.maximum(factor.astype(jnp.float32) * jnp.cos(lat), FLOOR)
    return metric, factor


def batched(fn, tiles):
    whole = fn(jnp.concatenate(tiles, axis=0))
    return [whole[8 * i : 8 * i + 8] for i in range(len(tiles))]


def total_of(terms):
    out = None
    for factor, tile in terms:
        if tile is None:
            continue
        if out is None:
            out = tile if isinstance(factor, float) and factor == 1.0 else factor * tile
        elif isinstance(factor, float) and factor == 1.0:
            out = out + tile
        elif isinstance(factor, float) and factor == -1.0:
            out = out - tile
        else:
            out = out + factor * tile
    return out


class PoleRows:
    def __init__(self, at_north, metric, gates):
        self.at_north, self.metric, self.gates = at_north, metric, gates

    def shift_layer(self, field, c, r, source, by):
        rows = row_ids()
        key = source if source == "free" else (source[0], source[1] + by)
        tile = field.get((c, r, key))
        if tile is None:
            return None
        return jnp.where(rows == (7 if by == 1 else 0), 0.0, pltpu.roll(tile, 7 if by == 1 else 1, 0))

    def turn(self, field, comps, by):
        ids = [i for i in field if i[0] in comps]
        return dict(zip(ids, batched(lambda x: pltpu.roll(x, by % 128, 1), [field[i] for i in ids]))) if ids else {}

    def merge(self, field):
        ids = list(field)
        tiles = [field[i] for i in ids]
        for level, step in enumerate((1, 2, 4)):
            def swap(x):
                return jnp.take_along_axis(x, lax.broadcasted_iota(jnp.int32, x.shape, 1) ^ step, axis=1)
            others = batched(swap, tiles)
            tiles = [t + jnp.where(self.gates[i[1]][level], o, t) for i, t, o in zip(ids, tiles, others)]
        return {i: t * 0.125 for i, t in zip(ids, tiles)}

    def keys(self, field, spread, extra=()):
        found = []
        for source in [i[2] for i in field] + list(extra):
            for s in ([source] if source == "free" else [source, (source[0], source[1] + spread)]):
                if s not in found:
                    found.append(s)
        return found

    def forward(self, e, h, wanted, merged=True):
        ahead = -1 if self.at_north else 1
        fe = self.turn(e, (1, 2), -1)
        new = {}
        for source in self.keys(e, -1, [i[2] for i in h]):
            for c, r in wanted:
                m = self.metric[r]
                up = lambda c: self.shift_layer(e, c, r, source, 1)
                at = lambda c: e.get((c, r, source))
                north = lambda c: e.get((c, r + ahead, source))
                east = lambda c: fe.get((c, r, source))
                if c == 0:
                    curl = [(-NORTH, north(2)), (NORTH, at(2)), (RADIAL, up(1)), (-RADIAL, at(1))]
                elif c == 1:
                    curl = [(-RADIAL, up(0)), (RADIAL, at(0)), (m, east(2)), (-m, at(2))]
                else:
                    curl = [(-m, east(1)), (m, at(1)), (NORTH, north(0)), (-NORTH, at(0))]
                tile = total_of([(1.0, h.get((c, r, source)))] + curl)
                if tile is not None:
                    new[c, r, source] = tile
        return self.merge(new) if merged else new

    def drive(self, e, h, rows):
        behind = 1 if self.at_north else -1
        fw = self.turn(h, (1, 2), 1)
        new = {}
        for source in self.keys(h, 1, [i[2] for i in e]):
            for r in rows:
                m = self.metric[r]
                down = lambda c: self.shift_layer(h, c, r, source, -1)
                at = lambda c: h.get((c, r, source))
                south = lambda c: h.get((c, r + behind, source))
                west = lambda c: fw.get((c, r, source))
                curls = ([(NORTH, at(2)), (-NORTH, south(2)), (-RADIAL, at(1)), (RADIAL, down(1))],
                         [(RADIAL, at(0)), (-RADIAL, down(0)), (-m, at(2)), (m, west(2))],
                         [(m, at(1)), (-m, west(1)), (-NORTH, at(0)), (NORTH, south(0))])
                for c in range(3):
                    tile = total_of([(2.0, e.get((c, r, source)))] + curls[c])
                    if tile is not None:
                        new[c, r, source] = tile
        return new

    def update(self, u, drive, e, wanted, merged=True):
        new = {}
        for source in self.keys(drive, 0, [i[2] for i in e]):
            for a, r in wanted:
                tile = total_of([(u[3 * a + c, r], drive.get((c, r, source))) for c in range(3)]
                                + [(-1.0, e.get((a, r, source)))])
                if tile is not None:
                    new[a, r, source] = tile
        return self.merge(new) if merged else new


def every(rows):
    return [(c, r) for r in rows for c in range(3)]


def only(field, source):
    return {i: t for i, t in field.items() if (i[2] == "free") == source}


def pole_chain(at_north, load, metric, gates):
    p = PoleRows(at_north, metric, gates)
    deep = range(4) if at_north else range(5)
    e = {(c, r, "free"): load("e", c, r) for c in range(3) for r in deep}
    h = {(c, r, "free"): load("h", c, r) for c in range(3) for r in range(4)}
    u = {(i, r): v for r in range(3 if at_north else 4) for i, v in enumerate(inverse([load("c", i, r) for i in range(9)]))}
    out = {}

    def note(n, field, initial=False):
        for (c, r, source), tile in field.items():
            if r == 0 and c != 1:
                out[("free", n) if source == "free" else ("response", n) + source, c] = tile

    unit = jnp.ones((8, 128), jnp.float32)
    ends = [(0, 0), (2, 0)]
    if at_north:
        note(0, e)
        h = p.forward(e, h, every(range(4)))
        h[0, 0, (2, 0)] = -NORTH * unit
        h[2, 0, (0, 0)] = NORTH * unit
        def back(e, h, free_rows, rows, wanted=None, merged=True):
            new = {}
            for free, rr in ((True, free_rows), (False, rows)):
                ee, hh = only(e, free), only(h, free)
                d = p.drive(ee, hh, rr)
                new.update({(i, free): t for i, t in d.items()})
            drive = {i: t for (i, _), t in new.items()}
            want = wanted or every(sorted(set(free_rows) | set(rows)))
            return p.update(u, drive, {i: t for i, t in e.items() if (i[1] in (free_rows if i[2] == "free" else rows))}, want, merged)

        e = back(e, h, range(3), range(1))
        note(1, e)
        h = p.forward(e, h, every(range(3)))
        h = {i: t for i, t in h.items() if i[2] == "free" or i[1] < 2}
        e = back(e, h, range(2), range(2))
        note(2, e)
        h = p.forward(e, h, every(range(2)))
        e = back(e, h, range(1), range(1), ends, False)
        note(3, e)
    else:
        h = p.forward(e, h, every(range(4)))
        note(0, h)
        drive = p.drive(e, h, range(4))
        drive[0, 0, (2, 0)] = -NORTH * unit
        drive[2, 0, (0, 0)] = NORTH * unit
        e = p.update(u, drive, {i: t for i, t in e.items() if i[1] < 4}, every(range(4)))
        h = p.forward(e, {i: t for i, t in h.items() if i[1] < 3}, every(range(3)))
        note(1, h)
        drive = p.drive(e, h, range(3))
        e = p.update(u, drive, {i: t for i, t in e.items() if i[1] < 3}, every(range(3)))
        h = p.forward(e, {i: t for i, t in h.items() if i[1] < 2}, every(range(2)))
        note(2, h)
        drive = p.drive(e, h, range(2))
        e = p.update(u, drive, {i: t for i, t in e.items() if i[1] < 2}, every(range(2)))
        h = p.forward(e, {i: t for i, t in h.items() if i[1] < 1}, ends, False)
        note(3, h)
    return out


def pole_items(at_north):
    return ([("e", c, r) for c in range(3) for r in range(4 if at_north else 5)] + [("h", c, r) for c in range(3) for r in range(4)]
            + [("c", i, r) for i in range(9) for r in range(3 if at_north else 4)])


def columns(tiles):
    lanes = lane_ids()
    count = 128
    tiles = tiles + [None] * (count - len(tiles))
    while count > 1:
        count //= 2
        first, second = tiles[:count], tiles[count:]
        low = (lanes & count) == 0
        zero = jnp.zeros((8, 128), jnp.float32)
        pairs = [(a, b) for a, b in zip(first, second) if a is not None]
        give = [jnp.where(low, zero if b is None else b, a) for a, b in pairs]
        take = [jnp.where(low, a, zero if b is None else b) for a, b in pairs]
        swapped = batched(lambda x: jnp.take_along_axis(x, lax.broadcasted_iota(jnp.int32, x.shape, 1) ^ count, axis=1), give)
        tiles = [t + s for t, s in zip(take, swapped)]
        tiles = tiles + [None] * (count - len(tiles))
    return tiles[0]


def solve_caps(names, total):
    rows = row_ids()
    spread = dict(zip(names, batched(lambda x: x, [jnp.take_along_axis(total, jnp.full((8, 128), q, jnp.int32), axis=1)
                                                   for q in range(len(names))])))
    caps = []

    def moved(tile, d):
        if d == 0:
            return tile
        kept = rows >= d if d > 0 else rows < 8 + d
        return jnp.where(kept, pltpu.roll(tile, d % 8, 0), 0.0)

    for n in range(STEPS):
        value = {c: spread[("free", n), c] for c in (0, 2)}
        for m in range(n):
            shifted = {}
            for name, c in names:
                if name[0] == "response" and name[1] == n - m:
                    if name[2:] not in shifted:
                        shifted[name[2:]] = moved(caps[m][name[2]], name[3])
                    value[c] = value[c] + spread[name, c] * shifted[name[2:]]
        caps.append(value)
    return caps


def kernel(zf_in, zb_in, e_in, h_in, c_in, eo_ref, ho_ref, zf, zb, e_ref, h_ref, c_ref, rows_e, rows_h, rows_c, pack, got, got2, pole_own, pole_pack, pole_got, pole_sum, ee, hh, uu, mine,
           caps, sums, load_sem, send, recv, cap_send, cap_recv, go, *, bands, lons):
    band, lon = lax.axis_index("band"), lax.axis_index("lon")
    at_south, at_north = band == 0, band == bands - 1
    inner_north, inner_south = jnp.logical_not(at_north), jnp.logical_not(at_south)
    north, south = band + 1, band - 1
    east, west = lax.rem(lon + 1, lons), lax.rem(lon + lons - 1, lons)
    pole = jnp.logical_or(at_south, at_north)

    loads = [pltpu.make_async_copy(s, d, load_sem.at[i]) for i, (s, d) in enumerate(((e_in, e_ref), (h_in, h_ref), (c_in, c_ref), (zf_in, zf), (zb_in, zb)))]
    for load in loads:
        load.start()

    barrier = pltpu.get_barrier_semaphore()

    def greet(b, l):
        pl.semaphore_signal(barrier, inc=1, device_id=(b, l), device_id_type=MESH)

    greet(band, east)
    greet(band, west)

    @pl.when(inner_north)
    def _():
        for l in (east, west, lon):
            greet(north, l)

    @pl.when(inner_south)
    def _():
        for l in (east, west, lon):
            greet(south, l)

    @pl.when(pole)
    def _():
        def one(d, _):
            greet(band, lax.rem(lon + d, lons))
            return 0
        lax.fori_loop(2, lons - 1, one, 0)

    lanes, rows = lane_ids(), row_ids()

    def pack_field(ref, first, count):
        def one(i, _):
            tiles = [(c, a) for c in range(3) for a in range(2)]
            rolled = [[roll(ref[i * 3 + c, a * 4 + q], 32 * q, 1) for q in range(4)] for c, a in tiles]
            for n, t in enumerate(rolled):
                lo, hi = t[0], t[1]
                for q in range(1, 4):
                    lo = jnp.where(lanes // 32 == q, t[q], lo)
                    if q > 1:
                        hi = jnp.where(lanes // 32 == q - 1, t[q], hi)
                hi = jnp.where(lanes // 32 == 3, t[0], hi)
                pack[0, first * 2 + i * 6 + n] = lo
                pack[1, first * 2 + i * 6 + n] = hi
            return 0
        if count == 3:
            one(0, 0)
        else:
            lax.fori_loop(0, count // 3, one, 0)

    def remote(src, dst, i, b, l):
        return pltpu.make_async_remote_copy(src_ref=src, dst_ref=dst, send_sem=send.at[i], recv_sem=recv.at[i],
                                            device_id=(b, l), device_id_type=MESH)

    fields, conduct = pl.ds(0, 12), pl.ds(12, 18)
    to_lon = [[remote(pack.at[k, part], got.at[k, part], 2 * n + k, band, (west, east)[k]) for k in range(2)]
              for n, part in enumerate((fields, conduct))]
    north_parts = [[(k, part, pl.ds(8 - d[k], d[k]), 4 + 2 * n + k) for k in range(2)]
                   for n, (part, d) in enumerate(((fields, (4, 3)), (conduct, (3, 2))))]
    south_parts = [[(k, part, pl.ds(0, d[k]), 8 + 2 * n + k) for k in range(2)]
                   for n, (part, d) in enumerate(((fields, (3, 4)), (conduct, (2, 3))))]
    odd = lax.rem(band, 2) == 1
    to_north = [[remote(pack.at[k, p, r], got2.at[k, p, r], i, north, (west, east)[k]) for k, p, r, i in parts] for parts in north_parts]
    to_south = [[remote(pack.at[k, p, r], got2.at[k, p, r], i, south, (west, east)[k]) for k, p, r, i in parts] for parts in south_parts]
    on_north = [[remote(got.at[k, p, r], got2.at[k, p, r], i, north, lon) for k, p, r, i in parts] for parts in north_parts]
    on_south = [[remote(got.at[k, p, r], got2.at[k, p, r], i, south, lon) for k, p, r, i in parts] for parts in south_parts]
    trio = ((e_ref, rows_e), (h_ref, rows_h), (c_ref, rows_c))
    rows_north = [remote(s.at[:, :, pl.ds(8 - d, d)], t.at[:, :, pl.ds(8 - d, d)], 12 + i, north, lon)
                  for i, ((s, t), d) in enumerate(zip(trio, (4, 4, 3)))]
    rows_south = [remote(s.at[:, :, pl.ds(0, d)], t.at[:, :, pl.ds(0, d)], 15 + i, south, lon)
                  for i, ((s, t), d) in enumerate(zip(trio, (4, 3, 3)))]

    def send_part(n):
        for copy in to_lon[n]:
            copy.start()

        @pl.when(inner_north)
        def _():
            for copy in rows_north[:2] if n == 0 else rows_north[2:]:
                copy.start()

        @pl.when(jnp.logical_and(inner_north, jnp.logical_or(odd, at_south)))
        def _():
            for copy in to_north[n]:
                copy.start()

        @pl.when(inner_south)
        def _():
            for copy in rows_south[:2] if n == 0 else rows_south[2:]:
                copy.start()

        @pl.when(jnp.logical_and(inner_south, jnp.logical_or(jnp.logical_not(odd), at_north)))
        def _():
            for copy in to_south[n]:
                copy.start()

    loads[0].wait()
    loads[1].wait()
    poles = ((True, at_north), (False, at_south))
    refs = {"e": e_ref, "h": h_ref, "c": c_ref}

    def pole_copy(is_north):
        part = pl.ds(0, (len(pole_items(is_north)) + 1) // 2)
        return remote(pole_pack.at[part], pole_got.at[part], 18, band, east)

    @pl.when(pole)
    def _():
        loads[2].wait()

    for is_north, condition in poles:
        @pl.when(condition)
        def _():
            tiles = [refs[kind][i, pl.ds(0, 8), 7 - r if is_north else r, :] for kind, i, r in pole_items(is_north)]
            for n, tile in enumerate(tiles):
                pole_own[n] = tile
            for n in range(0, len(tiles), 2):
                pole_pack[n // 2] = jnp.where(lanes < 64, pltpu.roll(tiles[n], 64, 1), tiles[min(n + 1, len(tiles) - 1)])

    pack_field(e_ref, 0, 3)
    pack_field(h_ref, 3, 3)

    @pl.when(jnp.logical_not(pole))
    def _():
        pl.semaphore_wait(barrier, 8)

    @pl.when(band == 1)
    def _():
        pl.semaphore_signal(go, inc=1, device_id=(south, lon), device_id_type=MESH)

    @pl.when(band == bands - 2)
    def _():
        pl.semaphore_signal(go, inc=1, device_id=(north, lon), device_id_type=MESH)

    @pl.when(pole)
    def _():
        pl.semaphore_wait(go, 1)

    for is_north, condition in poles:
        @pl.when(condition)
        def _():
            pole_copy(is_north).start()

    send_part(0)

    @pl.when(jnp.logical_not(pole))
    def _():
        loads[2].wait()

    pack_field(c_ref, 6, 9)
    send_part(1)

    loads[3].wait()
    loads[4].wait()
    metric, factors, gates = [], [], []
    for block in range(2):
        shift = 0 if block == 0 else jnp.where(rows < 4, 8, -8)
        m, f = row_tables(zf, zb, band * 8 + rows + shift, 8 * bands)
        metric.append(m)
        factors.append(f)
        gates.append([f > s for s in (1, 2, 4)])
    zero = jnp.zeros((8, 128), jnp.float32)
    for b in range(4):
        for c in range(3):
            ee[b, c, 8] = zero
            hh[b, c, 0] = zero
    for n in range(STEPS):
        for i in range(2):
            sums[n, i] = zero

    def take_in(block, layer, load):
        for c in range(3):
            ee[block, c, layer] = load(c)
            hh[block, c, layer + 1] = load(3 + c)
        for i, value in enumerate(inverse([load(6 + c) for c in range(9)])):
            uu[block, i, layer] = value

    def own(k, _):
        take_in(0, k, lambda f: e_ref[f, k] if f < 3 else (h_ref[f - 3, k] if f < 6 else c_ref[f - 6, k]))
        return 0


    def unpack(block, ref):
        def one(a, _):
            for q in range(4):
                tiles = [roll(jnp.where(lanes // 32 == q, ref[0, 2 * f + a], ref[1, 2 * f + a]), -32 * q, 1) for f in range(FIELDS)]
                take_in(block, a * 4 + q, lambda f: tiles[f])
            return 0
        lax.fori_loop(0, 2, one, 0)

    offsets = sorted(((i // 32, i // 8 % 4, i % 8) for i in range(1, 64)),
                     key=lambda o: 4 * o[0] + min(o[1], 4 - o[1]) + min(o[2], 8 - o[2]))

    def cap_copy(n, offset):
        hi, x, z = lon // 32, lax.rem(lon // 8, 4), lax.rem(lon, 8)
        target = lax.rem(hi + offset[0], 2) * 32 + lax.rem(x + offset[1], 4) * 8 + lax.rem(z + offset[2], 8)
        return pltpu.make_async_remote_copy(src_ref=mine, dst_ref=caps.at[n], send_sem=cap_send.at[0], recv_sem=cap_recv.at[0],
                                            device_id=(band, target), device_id_type=MESH)

    names = {}
    for is_north, condition in poles:
        @pl.when(condition)
        def _():
            items = pole_items(is_north)
            place = {item: n for n, item in enumerate(items)}
            edge = [7 - r if is_north else r for r in range(5)]
            m = [jnp.broadcast_to(metric[0][r : r + 1, :], (8, 128)) for r in edge]
            f = [jnp.broadcast_to(factors[0][r : r + 1, :], (8, 128)) for r in edge]
            g = [[x > k for k in (1, 2, 4)] for x in f]

            def seam(kind, i, r):
                n = place[kind, i, r]
                tile = pole_got[n // 2]
                return jnp.where(lanes < 64, tile if n % 2 == 0 else pltpu.roll(tile, 64, 1), pltpu.roll(pole_own[n], 64, 1))

            inner = pole_chain(is_north, lambda kind, i, r: pole_own[place[kind, i, r]], m, g)
            names[is_north] = list(inner)
            for n, tile in enumerate(inner.values()):
                pole_sum[n] = tile
            pole_copy(is_north).wait_recv()
            outer = pole_chain(is_north, seam, m, g)
            inside = jnp.logical_and(lanes >= 32, lanes < 96)
            mine[...] = columns([jnp.where(inside, pole_sum[n] + outer[name], 0.0) for n, name in enumerate(names[is_north])])

    @pl.when(pole)
    def _():
        pl.semaphore_wait(barrier, lons - 1 + 3)
        for n, offset in enumerate(offsets):
            cap_copy(n, offset).start()

    lax.fori_loop(0, 8, own, 0)

    for n in range(2):
        for copy in to_lon[n]:
            copy.wait_recv()

        @pl.when(jnp.logical_and(odd, inner_north))
        def _():
            for copy in on_south[n]:
                copy.start()

        @pl.when(jnp.logical_and(jnp.logical_not(odd), inner_south))
        def _():
            for copy in on_north[n]:
                copy.start()

    unpack(1, got)

    @pl.when(inner_north)
    def _():
        for n in range(2):
            for copy in to_south[n]:
                copy.wait_recv()
        for copy in rows_south:
            copy.wait_recv()

    @pl.when(inner_south)
    def _():
        for n in range(2):
            for copy in to_north[n]:
                copy.wait_recv()
        for copy in rows_north:
            copy.wait_recv()

    def outer(k, _):
        take_in(2, k, lambda f: rows_e[f, k] if f < 3 else (rows_h[f - 3, k] if f < 6 else rows_c[f - 6, k]))
        return 0

    lax.fori_loop(0, 8, outer, 0)
    unpack(3, got2)

    @pl.when(pole)
    def _():
        pltpu.make_async_copy(caps, caps, cap_recv.at[0]).wait()

    for is_north, condition in poles:
        @pl.when(condition)
        def _():
            total = (mine[...] + jnp.sum(caps[...], axis=0)) * (1.0 / (128 * lons))
            for n, value in enumerate(solve_caps(names[is_north], total)):
                sums[n, 0] = value[0]
                sums[n, 1] = value[2]

    lane3 = lax.broadcasted_iota(jnp.int32, (8, 8, 128), 2)
    row3 = lax.broadcasted_iota(jnp.int32, (8, 8, 128), 1)
    metric3 = [jnp.broadcast_to(m, (8, 8, 128)) for m in metric]
    gates3 = [[jnp.broadcast_to(g, (8, 8, 128)).reshape(64, 128) for g in gs] for gs in gates]
    lane2 = lax.broadcasted_iota(jnp.int32, (64, 128), 1)

    def turn(f, by, axis, blocks):
        size = 128 if axis == 2 else 8
        seam = (lane3 if axis == 2 else row3) == (0 if by == 1 else size - 1)
        other = (1, 0, 3, 2) if axis == 2 else (2, 3, 0, 1)
        moved = {b: pltpu.roll(f[b].reshape(64, 128), by % 128, 1).reshape(8, 8, 128) if axis == 2 else pltpu.roll(f[b], by % 8, 1)
                 for b in range(4) if b in blocks or other[b] in blocks}
        return {b: jnp.where(seam, moved[other[b]], moved[b]) for b in blocks}

    def merge_all(f, store):
        x = {(b, c): f[b][c].reshape(64, 128) for b in f for c in range(3)}
        for level, step in enumerate((1, 2, 4)):
            other = {i: jnp.take_along_axis(v, lane2 ^ step, axis=1) for i, v in x.items()}
            x = {(b, c): v + jnp.where(gates3[b // 2][level], other[b, c], v) for (b, c), v in x.items()}
        for (b, c), v in x.items():
            store(b, c, (v * 0.125).reshape(8, 8, 128))

    def ghost(n, c):
        return jnp.concatenate([jnp.broadcast_to(sums[n, c // 2, k : k + 1, :].reshape(1, 1, 128), (1, 8, 128)) for k in range(8)])

    def forward(n, blocks):
        f = [[ee[b, c, 0:8] for b in range(4)] for c in range(3)]
        up = [[ee[b, c, 1:9] for b in range(4)] for c in range(2)]
        fe = {c: turn(f[c], -1, 2, blocks) for c in (1, 2)}
        fn = {c: turn(f[c], -1, 1, blocks) for c in (0, 2)}
        cap = jnp.logical_and(row3 == 7, at_north)
        for c in (0, 2):
            value = ghost(n, c)
            for b in (0, 1):
                if b in blocks:
                    fn[c][b] = jnp.where(cap, value, fn[c][b])
        new = {}
        for b in blocks:
            m = metric3[b // 2]
            curl = (NORTH * (fn[2][b] - f[2][b]) - RADIAL * (up[1][b] - f[1][b]),
                    RADIAL * (up[0][b] - f[0][b]) - m * (fe[2][b] - f[2][b]),
                    m * (fe[1][b] - f[1][b]) - NORTH * (fn[0][b] - f[0][b]))
            new[b] = [hh[b, c, 1:9] - curl[c] for c in range(3)]

        def store(b, c, v):
            hh[b, c, 1:9] = v

        merge_all(new, store)

    def backward(n, blocks):
        f = [[hh[b, c, 1:9] for b in range(4)] for c in range(3)]
        down = [[hh[b, c, 0:8] for b in range(4)] for c in range(2)]
        fw = {c: turn(f[c], 1, 2, blocks) for c in (1, 2)}
        fs = {c: turn(f[c], 1, 1, blocks) for c in (0, 2)}
        cap = jnp.logical_and(row3 == 0, at_south)
        for c in (0, 2):
            value = ghost(n, c)
            for b in (0, 1):
                if b in blocks:
                    fs[c][b] = jnp.where(cap, value, fs[c][b])
        new = {}
        for b in blocks:
            m = metric3[b // 2]
            curl = (NORTH * (f[2][b] - fs[2][b]) - RADIAL * (f[1][b] - down[1][b]),
                    RADIAL * (f[0][b] - down[0][b]) - m * (f[2][b] - fw[2][b]),
                    m * (f[1][b] - fw[1][b]) - NORTH * (f[0][b] - fs[0][b]))
            old = [ee[b, c, 0:8] for c in range(3)]
            drive = [2.0 * old[c] + curl[c] for c in range(3)]
            new[b] = [uu[b, 3 * a, 0:8] * drive[0] + uu[b, 3 * a + 1, 0:8] * drive[1] + uu[b, 3 * a + 2, 0:8] * drive[2] - old[a]
                      for a in range(3)]

        def store(b, c, v):
            ee[b, c, 0:8] = v

        merge_all(new, store)

    def step(n, _):
        forward(n, range(4))
        backward(n, range(4))
        return 0

    lax.fori_loop(0, STEPS - 1, step, 0)
    forward(STEPS - 1, range(3))
    backward(STEPS - 1, range(1))
    for c in range(3):
        eo_ref[c] = ee[0, c, pl.ds(0, 8)]
        ho_ref[c] = hh[0, c, pl.ds(1, 8)]

    for n in range(2):
        for copy in to_lon[n]:
            copy.wait_send()

    @pl.when(inner_north)
    def _():
        for copy in to_north[0] + to_north[1] + rows_north:
            copy.wait_send()

    @pl.when(inner_south)
    def _():
        for copy in to_south[0] + to_south[1] + rows_south:
            copy.wait_send()

    @pl.when(pole)
    def _():
        pltpu.make_async_copy(caps, caps, cap_send.at[0]).wait()

    for is_north, condition in poles:
        @pl.when(condition)
        def _():
            pole_copy(is_north).wait_send()


def write_out(e_kept, h_kept, e_out, h_out, sem):
    copies = [pltpu.make_async_copy(e_kept, e_out, sem.at[0]), pltpu.make_async_copy(h_kept, h_out, sem.at[1])]
    for copy in copies:
        copy.start()
    for copy in copies:
        copy.wait()


def solution(mesh):
    bands, lons = mesh.shape["band"], mesh.shape["lon"]

    def on_device(e, h, c, zone_factor, zone_bounds):
        vmem, hbm = (pl.BlockSpec(memory_space=m) for m in (pltpu.VMEM, pltpu.HBM))
        f32 = lambda *shape: pltpu.VMEM(shape, jnp.float32)
        kept = pltpu.VMEM(e.shape, e.dtype)
        inputs = [pltpu.with_memory_space_constraint(x, pltpu.HBM) for x in (zone_factor, zone_bounds, e, h, c)]
        fields = pl.pallas_call(
            functools.partial(kernel, bands=bands, lons=lons),
            out_shape=(kept, kept),
            in_specs=[hbm] * 5,
            out_specs=(vmem, vmem),
            scratch_shapes=[
                pltpu.SMEM(zone_factor.shape, jnp.int32), pltpu.SMEM(zone_bounds.shape, jnp.int32),
                f32(3, 8, 8, 128), f32(3, 8, 8, 128), f32(9, 8, 8, 128),
                f32(3, 8, 8, 128), f32(3, 8, 8, 128), f32(9, 8, 8, 128),
                f32(2, 2 * FIELDS, 8, 128), f32(2, 2 * FIELDS, 8, 128), f32(2, 2 * FIELDS, 8, 128),
                f32(64, 8, 128), f32(32, 8, 128), f32(32, 8, 128), f32(64, 8, 128),
                f32(4, 3, 9, 8, 128), f32(4, 3, 9, 8, 128), f32(4, 9, 8, 8, 128),
                f32(8, 128), f32(lons - 1, 8, 128), f32(STEPS, 2, 8, 128),
                pltpu.SemaphoreType.DMA((5,)), pltpu.SemaphoreType.DMA((19,)), pltpu.SemaphoreType.DMA((19,)),
                pltpu.SemaphoreType.DMA((1,)), pltpu.SemaphoreType.DMA((1,)), pltpu.SemaphoreType.REGULAR,
            ],
            compiler_params=pltpu.CompilerParams(collective_id=0, has_side_effects=True, vmem_limit_bytes=60 * 1024 * 1024),
        )(*inputs)
        like = jax.ShapeDtypeStruct(e.shape, e.dtype)
        return pl.pallas_call(
            write_out,
            out_shape=(like, like),
            in_specs=[vmem, vmem],
            out_specs=(hbm, hbm),
            scratch_shapes=[pltpu.SemaphoreType.DMA((2,))],
        )(*(pltpu.with_memory_space_constraint(x, pltpu.VMEM) for x in fields))

    spread = P(None, None, "band", "lon")
    return jax.shard_map(on_device, mesh=mesh, in_specs=(spread, spread, spread, P(), P()), out_specs=(spread, spread),
                         check_vma=False)
```

```python
import functools

import jax
import jax.numpy as jnp
from jax import lax
from jax.experimental import pallas as pl
from jax.experimental.pallas import tpu as pltpu
from jax.sharding import PartitionSpec as P

MESH = pl.DeviceIdType.MESH
STEPS = 4
NORTH, RADIAL, EAST, FLOOR = 0.45, 0.5, 0.12, 0.25


def lane_ids():
    return lax.broadcasted_iota(jnp.int32, (8, 128), 1)


def row_ids():
    return lax.broadcasted_iota(jnp.int32, (8, 128), 0)


def roll(x, by, axis):
    by = by % x.shape[axis]
    return x if by == 0 else pltpu.roll(x, by, axis)


def pair_shift(main, edge, by, axis):
    ids = lane_ids() if axis == 1 else row_ids()
    last = ids == (0 if by == 1 else (127 if axis == 1 else 7))
    rolled_main, rolled_edge = roll(main, by, axis), roll(edge, by, axis)
    return jnp.where(last, rolled_edge, rolled_main), jnp.where(last, rolled_main, rolled_edge)


def merge(x, gates):
    lanes = lane_ids()
    for step, gate in zip((1, 2, 4), gates):
        other = jnp.take_along_axis(x, lanes ^ step, axis=1)
        x = x + jnp.where(gate, other, x)
    return x * 0.125


def inverse(c):
    m = [[c[0] + 1.0, c[1], c[2]], [c[3], c[4] + 1.0, c[5]], [c[6], c[7], c[8] + 1.0]]

    def cof(a, b):
        i, j, p, q = (a + 1) % 3, (a + 2) % 3, (b + 1) % 3, (b + 2) % 3
        return m[i][p] * m[j][q] - m[i][q] * m[j][p]

    cofs = [[cof(a, b) for b in range(3)] for a in range(3)]
    det = m[0][0] * cofs[0][0] + m[0][1] * cofs[0][1] + m[0][2] * cofs[0][2]
    inv = 1.0 / det
    return [cofs[b][a] * inv for a in range(3) for b in range(3)]


def row_tables(zf, zb, rows, total):
    factor = jnp.full((8, 128), zf[0], jnp.int32)
    for z in range(zb.shape[0]):
        factor = jnp.where(rows >= zb[z], zf[z + 1], factor)
    lat = ((rows.astype(jnp.float32) + 0.5) / total - 0.5) * jnp.pi
    metric = EAST / jnp.maximum(factor.astype(jnp.float32) * jnp.cos(lat), FLOOR)
    return metric, factor


def batched(fn, tiles):
    whole = fn(jnp.concatenate(tiles, axis=0))
    return [whole[8 * i : 8 * i + 8] for i in range(len(tiles))]


def total_of(terms):
    out = None
    for factor, tile in terms:
        if tile is None:
            continue
        if out is None:
            out = tile if isinstance(factor, float) and factor == 1.0 else factor * tile
        elif isinstance(factor, float) and factor == 1.0:
            out = out + tile
        elif isinstance(factor, float) and factor == -1.0:
            out = out - tile
        else:
            out = out + factor * tile
    return out


class PoleRows:
    def __init__(self, at_north, metric, gates):
        self.at_north, self.metric, self.gates = at_north, metric, gates

    def shift_layer(self, field, c, r, source, by):
        rows = row_ids()
        key = source if source == "free" else (source[0], source[1] + by)
        tile = field.get((c, r, key))
        if tile is None:
            return None
        return jnp.where(rows == (7 if by == 1 else 0), 0.0, pltpu.roll(tile, 7 if by == 1 else 1, 0))

    def turn(self, field, comps, by):
        ids = [i for i in field if i[0] in comps]
        return dict(zip(ids, batched(lambda x: pltpu.roll(x, by % 128, 1), [field[i] for i in ids]))) if ids else {}

    def merge(self, field):
        ids = list(field)
        tiles = [field[i] for i in ids]
        for level, step in enumerate((1, 2, 4)):
            def swap(x):
                return jnp.take_along_axis(x, lax.broadcasted_iota(jnp.int32, x.shape, 1) ^ step, axis=1)
            others = batched(swap, tiles)
            tiles = [t + jnp.where(self.gates[i[1]][level], o, t) for i, t, o in zip(ids, tiles, others)]
        return {i: t * 0.125 for i, t in zip(ids, tiles)}

    def keys(self, field, spread, extra=()):
        found = []
        for source in [i[2] for i in field] + list(extra):
            for s in ([source] if source == "free" else [source, (source[0], source[1] + spread)]):
                if s not in found:
                    found.append(s)
        return found

    def forward(self, e, h, wanted, merged=True):
        ahead = -1 if self.at_north else 1
        fe = self.turn(e, (1, 2), -1)
        new = {}
        for source in self.keys(e, -1, [i[2] for i in h]):
            for c, r in wanted:
                m = self.metric[r]
                up = lambda c: self.shift_layer(e, c, r, source, 1)
                at = lambda c: e.get((c, r, source))
                north = lambda c: e.get((c, r + ahead, source))
                east = lambda c: fe.get((c, r, source))
                if c == 0:
                    curl = [(-NORTH, north(2)), (NORTH, at(2)), (RADIAL, up(1)), (-RADIAL, at(1))]
                elif c == 1:
                    curl = [(-RADIAL, up(0)), (RADIAL, at(0)), (m, east(2)), (-m, at(2))]
                else:
                    curl = [(-m, east(1)), (m, at(1)), (NORTH, north(0)), (-NORTH, at(0))]
                tile = total_of([(1.0, h.get((c, r, source)))] + curl)
                if tile is not None:
                    new[c, r, source] = tile
        return self.merge(new) if merged else new

    def drive(self, e, h, rows):
        behind = 1 if self.at_north else -1
        fw = self.turn(h, (1, 2), 1)
        new = {}
        for source in self.keys(h, 1, [i[2] for i in e]):
            for r in rows:
                m = self.metric[r]
                down = lambda c: self.shift_layer(h, c, r, source, -1)
                at = lambda c: h.get((c, r, source))
                south = lambda c: h.get((c, r + behind, source))
                west = lambda c: fw.get((c, r, source))
                curls = ([(NORTH, at(2)), (-NORTH, south(2)), (-RADIAL, at(1)), (RADIAL, down(1))],
                         [(RADIAL, at(0)), (-RADIAL, down(0)), (-m, at(2)), (m, west(2))],
                         [(m, at(1)), (-m, west(1)), (-NORTH, at(0)), (NORTH, south(0))])
                for c in range(3):
                    tile = total_of([(2.0, e.get((c, r, source)))] + curls[c])
                    if tile is not None:
                        new[c, r, source] = tile
        return new

    def update(self, u, drive, e, wanted, merged=True):
        new = {}
        for source in self.keys(drive, 0, [i[2] for i in e]):
            for a, r in wanted:
                tile = total_of([(u[3 * a + c, r], drive.get((c, r, source))) for c in range(3)]
                                + [(-1.0, e.get((a, r, source)))])
                if tile is not None:
                    new[a, r, source] = tile
        return self.merge(new) if merged else new


def every(rows):
    return [(c, r) for r in rows for c in range(3)]


def only(field, source):
    return {i: t for i, t in field.items() if (i[2] == "free") == source}


def pole_chain(at_north, load, metric, gates):
    p = PoleRows(at_north, metric, gates)
    deep = range(4) if at_north else range(5)
    e = {(c, r, "free"): load("e", c, r) for c in range(3) for r in deep}
    h = {(c, r, "free"): load("h", c, r) for c in range(3) for r in range(4)}
    u = {(i, r): v for r in range(3 if at_north else 4) for i, v in enumerate(inverse([load("c", i, r) for i in range(9)]))}
    out = {}

    def note(n, field, initial=False):
        for (c, r, source), tile in field.items():
            if r == 0 and c != 1:
                out[("free", n) if source == "free" else ("response", n) + source, c] = tile

    unit = jnp.ones((8, 128), jnp.float32)
    ends = [(0, 0), (2, 0)]
    if at_north:
        note(0, e)
        h = p.forward(e, h, every(range(4)))
        h[0, 0, (2, 0)] = -NORTH * unit
        h[2, 0, (0, 0)] = NORTH * unit
        def back(e, h, free_rows, rows, wanted=None, merged=True):
            new = {}
            for free, rr in ((True, free_rows), (False, rows)):
                ee, hh = only(e, free), only(h, free)
                d = p.drive(ee, hh, rr)
                new.update({(i, free): t for i, t in d.items()})
            drive = {i: t for (i, _), t in new.items()}
            want = wanted or every(sorted(set(free_rows) | set(rows)))
            return p.update(u, drive, {i: t for i, t in e.items() if (i[1] in (free_rows if i[2] == "free" else rows))}, want, merged)

        e = back(e, h, range(3), range(1))
        note(1, e)
        h = p.forward(e, h, every(range(3)))
        h = {i: t for i, t in h.items() if i[2] == "free" or i[1] < 2}
        e = back(e, h, range(2), range(2))
        note(2, e)
        h = p.forward(e, h, every(range(2)))
        e = back(e, h, range(1), range(1), ends, False)
        note(3, e)
    else:
        h = p.forward(e, h, every(range(4)))
        note(0, h)
        drive = p.drive(e, h, range(4))
        drive[0, 0, (2, 0)] = -NORTH * unit
        drive[2, 0, (0, 0)] = NORTH * unit
        e = p.update(u, drive, {i: t for i, t in e.items() if i[1] < 4}, every(range(4)))
        h = p.forward(e, {i: t for i, t in h.items() if i[1] < 3}, every(range(3)))
        note(1, h)
        drive = p.drive(e, h, range(3))
        e = p.update(u, drive, {i: t for i, t in e.items() if i[1] < 3}, every(range(3)))
        h = p.forward(e, {i: t for i, t in h.items() if i[1] < 2}, every(range(2)))
        note(2, h)
        drive = p.drive(e, h, range(2))
        e = p.update(u, drive, {i: t for i, t in e.items() if i[1] < 2}, every(range(2)))
        h = p.forward(e, {i: t for i, t in h.items() if i[1] < 1}, ends, False)
        note(3, h)
    return out


def pole_items(at_north):
    return ([("e", c, r) for c in range(3) for r in range(4 if at_north else 5)] + [("h", c, r) for c in range(3) for r in range(4)]
            + [("c", i, r) for i in range(9) for r in range(3 if at_north else 4)])


def columns(tiles):
    lanes = lane_ids()
    count = 128
    tiles = tiles + [None] * (count - len(tiles))
    while count > 1:
        count //= 2
        first, second = tiles[:count], tiles[count:]
        low = (lanes & count) == 0
        zero = jnp.zeros((8, 128), jnp.float32)
        pairs = [(a, b) for a, b in zip(first, second) if a is not None]
        give = [jnp.where(low, zero if b is None else b, a) for a, b in pairs]
        take = [jnp.where(low, a, zero if b is None else b) for a, b in pairs]
        swapped = batched(lambda x: jnp.take_along_axis(x, lax.broadcasted_iota(jnp.int32, x.shape, 1) ^ count, axis=1), give)
        tiles = [t + s for t, s in zip(take, swapped)]
        tiles = tiles + [None] * (count - len(tiles))
    return tiles[0]


def solve_caps(names, total):
    rows = row_ids()
    spread = dict(zip(names, batched(lambda x: x, [jnp.take_along_axis(total, jnp.full((8, 128), q, jnp.int32), axis=1)
                                                   for q in range(len(names))])))
    caps = []

    def moved(tile, d):
        if d == 0:
            return tile
        kept = rows >= d if d > 0 else rows < 8 + d
        return jnp.where(kept, pltpu.roll(tile, d % 8, 0), 0.0)

    for n in range(STEPS):
        value = {c: spread[("free", n), c] for c in (0, 2)}
        for m in range(n):
            shifted = {}
            for name, c in names:
                if name[0] == "response" and name[1] == n - m:
                    if name[2:] not in shifted:
                        shifted[name[2:]] = moved(caps[m][name[2]], name[3])
                    value[c] = value[c] + spread[name, c] * shifted[name[2:]]
        caps.append(value)
    return caps


def kernel(zf_in, zb_in, e_in, h_in, c_in, eo_ref, ho_ref, zf, zb, e_ref, h_ref, c_ref, rows_e, rows_h, rows_c, pack, got, got2, pole_own, pole_pack, pole_got, pole_sum, ee, hh, uu, mine,
           caps, sums, load_sem, send, recv, cap_send, cap_recv, go, *, bands, lons):
    band, lon = lax.axis_index("band"), lax.axis_index("lon")
    at_south, at_north = band == 0, band == bands - 1
    inner_north, inner_south = jnp.logical_not(at_north), jnp.logical_not(at_south)
    north, south = band + 1, band - 1
    east, west = lax.rem(lon + 1, lons), lax.rem(lon + lons - 1, lons)
    pole = jnp.logical_or(at_south, at_north)

    loads = [pltpu.make_async_copy(s, d, load_sem.at[i]) for i, (s, d) in enumerate(((e_in, e_ref), (h_in, h_ref), (c_in, c_ref), (zf_in, zf), (zb_in, zb)))]
    for load in loads:
        load.start()

    barrier = pltpu.get_barrier_semaphore()

    def greet(b, l):
        pl.semaphore_signal(barrier, inc=1, device_id=(b, l), device_id_type=MESH)

    greet(band, east)
    greet(band, west)

    @pl.when(inner_north)
    def _():
        for l in (east, west, lon):
            greet(north, l)

    @pl.when(inner_south)
    def _():
        for l in (east, west, lon):
            greet(south, l)

    @pl.when(pole)
    def _():
        def one(d, _):
            greet(band, lax.rem(lon + d, lons))
            return 0
        lax.fori_loop(2, lons - 1, one, 0)

    lanes, rows = lane_ids(), row_ids()

    def pack_field(ref, first):
        rolled = [[roll(ref[c, a * 4 + q], 32 * q, 1) for q in range(4)] for c in range(3) for a in range(2)]
        for n, t in enumerate(rolled):
            lo, hi = t[0], t[1]
            for q in range(1, 4):
                lo = jnp.where(lanes // 32 == q, t[q], lo)
                if q > 1:
                    hi = jnp.where(lanes // 32 == q - 1, t[q], hi)
            pack[0, first + n] = lo
            pack[1, first + n] = jnp.where(lanes // 32 == 3, t[0], hi)

    def at_slot(s):
        return jnp.logical_and(lanes >= 24 * s, lanes < 24 * s + 24)

    def pack_conduct():
        for tile in range(15):
            blocks = [divmod(n, 8) for n in range(5 * tile, min(5 * tile + 5, 72))]
            rolled = [roll(c_ref[i, k], 24 * s, 1) for s, (i, k) in enumerate(blocks)]
            lo = hi = rolled[0]
            for s in range(1, len(rolled)):
                lo = jnp.where(at_slot(s), rolled[s], lo)
                hi = jnp.where(at_slot(s - 1), rolled[s], hi)
            pack[0, 12 + tile] = lo
            pack[1, 12 + tile] = hi

    def remote(src, dst, i, b, l):
        return pltpu.make_async_remote_copy(src_ref=src, dst_ref=dst, send_sem=send.at[i], recv_sem=recv.at[i],
                                            device_id=(b, l), device_id_type=MESH)

    fields, conduct = pl.ds(0, 12), pl.ds(12, 15)
    to_lon = [[remote(pack.at[k, part], got.at[k, part], 2 * n + k, band, (west, east)[k]) for k in range(2)]
              for n, part in enumerate((fields, conduct))]
    north_parts = [[(k, part, pl.ds(8 - d[k], d[k]), 4 + 2 * n + k) for k in range(2)]
                   for n, (part, d) in enumerate(((fields, (4, 3)), (conduct, (3, 2))))]
    south_parts = [[(k, part, pl.ds(0, d[k]), 8 + 2 * n + k) for k in range(2)]
                   for n, (part, d) in enumerate(((fields, (3, 4)), (conduct, (2, 3))))]
    odd = lax.rem(band, 2) == 1
    to_north = [[remote(pack.at[k, p, r], got2.at[k, p, r], i, north, (west, east)[k]) for k, p, r, i in parts] for parts in north_parts]
    to_south = [[remote(pack.at[k, p, r], got2.at[k, p, r], i, south, (west, east)[k]) for k, p, r, i in parts] for parts in south_parts]
    on_north = [[remote(got.at[k, p, r], got2.at[k, p, r], i, north, lon) for k, p, r, i in parts] for parts in north_parts]
    on_south = [[remote(got.at[k, p, r], got2.at[k, p, r], i, south, lon) for k, p, r, i in parts] for parts in south_parts]
    trio = ((e_ref, rows_e), (h_ref, rows_h), (c_ref, rows_c))
    rows_north = [remote(s.at[:, :, pl.ds(8 - d, d)], t.at[:, :, pl.ds(8 - d, d)], 12 + i, north, lon)
                  for i, ((s, t), d) in enumerate(zip(trio, (4, 4, 3)))]
    rows_south = [remote(s.at[:, :, pl.ds(0, d)], t.at[:, :, pl.ds(0, d)], 15 + i, south, lon)
                  for i, ((s, t), d) in enumerate(zip(trio, (4, 3, 3)))]

    def send_part(n):
        for copy in to_lon[n]:
            copy.start()

        @pl.when(inner_north)
        def _():
            for copy in rows_north[:2] if n == 0 else rows_north[2:]:
                copy.start()

        @pl.when(jnp.logical_and(inner_north, jnp.logical_or(odd, at_south)))
        def _():
            for copy in to_north[n]:
                copy.start()

        @pl.when(inner_south)
        def _():
            for copy in rows_south[:2] if n == 0 else rows_south[2:]:
                copy.start()

        @pl.when(jnp.logical_and(inner_south, jnp.logical_or(jnp.logical_not(odd), at_north)))
        def _():
            for copy in to_south[n]:
                copy.start()

    loads[0].wait()
    loads[1].wait()
    poles = ((True, at_north), (False, at_south))
    refs = {"e": e_ref, "h": h_ref, "c": c_ref}

    def pole_copy(is_north):
        part = pl.ds(0, (len(pole_items(is_north)) + 1) // 2)
        return remote(pole_pack.at[part], pole_got.at[part], 18, band, east)

    @pl.when(pole)
    def _():
        loads[2].wait()

    for is_north, condition in poles:
        @pl.when(condition)
        def _():
            tiles = [refs[kind][i, pl.ds(0, 8), 7 - r if is_north else r, :] for kind, i, r in pole_items(is_north)]
            for n, tile in enumerate(tiles):
                pole_own[n] = tile
            for n in range(0, len(tiles), 2):
                pole_pack[n // 2] = jnp.where(lanes < 64, pltpu.roll(tiles[n], 64, 1), tiles[min(n + 1, len(tiles) - 1)])

    pack_field(e_ref, 0)
    pack_field(h_ref, 6)

    @pl.when(jnp.logical_not(pole))
    def _():
        pl.semaphore_wait(barrier, 8)

    @pl.when(band == 1)
    def _():
        pl.semaphore_signal(go, inc=1, device_id=(south, lon), device_id_type=MESH)

    @pl.when(band == bands - 2)
    def _():
        pl.semaphore_signal(go, inc=1, device_id=(north, lon), device_id_type=MESH)

    @pl.when(pole)
    def _():
        pl.semaphore_wait(go, 1)

    for is_north, condition in poles:
        @pl.when(condition)
        def _():
            pole_copy(is_north).start()

    send_part(0)

    @pl.when(jnp.logical_not(pole))
    def _():
        loads[2].wait()

    pack_conduct()
    send_part(1)

    loads[3].wait()
    loads[4].wait()
    metric, factors, gates = [], [], []
    for block in range(2):
        shift = 0 if block == 0 else jnp.where(rows < 4, 8, -8)
        m, f = row_tables(zf, zb, band * 8 + rows + shift, 8 * bands)
        metric.append(m)
        factors.append(f)
        gates.append([f > s for s in (1, 2, 4)])
    zero = jnp.zeros((8, 128), jnp.float32)
    for b in range(4):
        for c in range(3):
            ee[b, c, 8] = zero
            hh[b, c, 0] = zero
    for n in range(STEPS):
        for i in range(2):
            sums[n, i] = zero

    def take_in(block, layer, load):
        for c in range(3):
            ee[block, c, layer] = load(c)
            hh[block, c, layer + 1] = load(3 + c)
        for i, value in enumerate(inverse([load(6 + c) for c in range(9)])):
            uu[block, i, layer] = value

    def own(k, _):
        take_in(0, k, lambda f: e_ref[f, k] if f < 3 else (h_ref[f - 3, k] if f < 6 else c_ref[f - 6, k]))
        return 0


    def unpack(block, ref):
        for k in range(8):
            a, q = divmod(k, 4)
            tiles = [roll(jnp.where(lanes // 32 == q, ref[0, 2 * f + a], ref[1, 2 * f + a]), -32 * q, 1) for f in range(6)]
            for i in range(9):
                tile, slot = divmod(8 * i + k, 5)
                tiles.append(roll(jnp.where(at_slot(slot), ref[0, 12 + tile], ref[1, 12 + tile]), -24 * slot, 1))
            take_in(block, k, lambda f: tiles[f])

    near = sorted(((i // 4, i % 4) for i in range(8)), key=lambda o: 4 * o[0] + min(o[1], 4 - o[1]))
    z_here = lax.rem(lon, 8)

    def cap_copy(z, n):
        hi, x = lax.rem(lon // 32 + near[n][0], 2), lax.rem(lax.rem(lon // 8, 4) + near[n][1], 4)
        slot = lax.rem(z - z_here + 8, 8) * 8 + n - 1
        return pltpu.make_async_remote_copy(src_ref=mine, dst_ref=caps.at[slot], send_sem=cap_send.at[0], recv_sem=cap_recv.at[0],
                                            device_id=(band, hi * 32 + x * 8 + z), device_id_type=MESH)

    names = {}
    for is_north, condition in poles:
        @pl.when(condition)
        def _():
            items = pole_items(is_north)
            place = {item: n for n, item in enumerate(items)}
            edge = [7 - r if is_north else r for r in range(5)]
            m = [jnp.broadcast_to(metric[0][r : r + 1, :], (8, 128)) for r in edge]
            f = [jnp.broadcast_to(factors[0][r : r + 1, :], (8, 128)) for r in edge]
            g = [[x > k for k in (1, 2, 4)] for x in f]

            def seam(kind, i, r):
                n = place[kind, i, r]
                tile = pole_got[n // 2]
                return jnp.where(lanes < 64, tile if n % 2 == 0 else pltpu.roll(tile, 64, 1), pltpu.roll(pole_own[n], 64, 1))

            inner = pole_chain(is_north, lambda kind, i, r: pole_own[place[kind, i, r]], m, g)
            names[is_north] = list(inner)
            for n, tile in enumerate(inner.values()):
                pole_sum[n] = tile
            pole_copy(is_north).wait_recv()
            outer = pole_chain(is_north, seam, m, g)
            inside = jnp.logical_and(lanes >= 32, lanes < 96)
            mine[...] = columns([jnp.where(inside, pole_sum[n] + outer[name], 0.0) for n, name in enumerate(names[is_north])])

    @pl.when(pole)
    def _():
        pl.semaphore_wait(barrier, lons - 1 + 3)
        for z in range(8):
            @pl.when(z_here != z)
            def _():
                cap_copy(z, 0).start()

            for n in range(1, 8):
                cap_copy(z, n).start()

    lax.fori_loop(0, 8, own, 0)

    for n in range(2):
        for copy in to_lon[n]:
            copy.wait_recv()

        @pl.when(jnp.logical_and(odd, inner_north))
        def _():
            for copy in on_south[n]:
                copy.start()

        @pl.when(jnp.logical_and(jnp.logical_not(odd), inner_south))
        def _():
            for copy in on_north[n]:
                copy.start()

    unpack(1, got)

    @pl.when(inner_north)
    def _():
        for n in range(2):
            for copy in to_south[n]:
                copy.wait_recv()
        for copy in rows_south:
            copy.wait_recv()

    @pl.when(inner_south)
    def _():
        for n in range(2):
            for copy in to_north[n]:
                copy.wait_recv()
        for copy in rows_north:
            copy.wait_recv()

    def outer(k, _):
        take_in(2, k, lambda f: rows_e[f, k] if f < 3 else (rows_h[f - 3, k] if f < 6 else rows_c[f - 6, k]))
        return 0

    lax.fori_loop(0, 8, outer, 0)
    unpack(3, got2)

    @pl.when(pole)
    def _():
        pltpu.make_async_copy(caps, caps, cap_recv.at[0]).wait()

    for is_north, condition in poles:
        @pl.when(condition)
        def _():
            total = (mine[...] + jnp.sum(caps[...], axis=0)) * (1.0 / (128 * lons))
            for n, value in enumerate(solve_caps(names[is_north], total)):
                sums[n, 0] = value[0]
                sums[n, 1] = value[2]

    lane3 = lax.broadcasted_iota(jnp.int32, (8, 8, 128), 2)
    row3 = lax.broadcasted_iota(jnp.int32, (8, 8, 128), 1)
    metric3 = [jnp.broadcast_to(m, (8, 8, 128)) for m in metric]
    gates3 = [[jnp.broadcast_to(g, (8, 8, 128)).reshape(64, 128) for g in gs] for gs in gates]
    lane2 = lax.broadcasted_iota(jnp.int32, (64, 128), 1)

    def turn(f, by, axis, blocks):
        size = 128 if axis == 2 else 8
        seam = (lane3 if axis == 2 else row3) == (0 if by == 1 else size - 1)
        other = (1, 0, 3, 2) if axis == 2 else (2, 3, 0, 1)
        moved = {b: pltpu.roll(f[b].reshape(64, 128), by % 128, 1).reshape(8, 8, 128) if axis == 2 else pltpu.roll(f[b], by % 8, 1)
                 for b in range(4) if b in blocks or other[b] in blocks}
        return {b: jnp.where(seam, moved[other[b]], moved[b]) for b in blocks}

    def merge_all(f, store):
        x = {(b, c): f[b][c].reshape(64, 128) for b in f for c in range(3)}
        for level, step in enumerate((1, 2, 4)):
            other = {i: jnp.take_along_axis(v, lane2 ^ step, axis=1) for i, v in x.items()}
            x = {(b, c): v + jnp.where(gates3[b // 2][level], other[b, c], v) for (b, c), v in x.items()}
        for (b, c), v in x.items():
            store(b, c, (v * 0.125).reshape(8, 8, 128))

    def ghost(n, c):
        return jnp.concatenate([jnp.broadcast_to(sums[n, c // 2, k : k + 1, :].reshape(1, 1, 128), (1, 8, 128)) for k in range(8)])

    def forward(n, blocks):
        f = [[ee[b, c, 0:8] for b in range(4)] for c in range(3)]
        up = [[ee[b, c, 1:9] for b in range(4)] for c in range(2)]
        fe = {c: turn(f[c], -1, 2, blocks) for c in (1, 2)}
        fn = {c: turn(f[c], -1, 1, blocks) for c in (0, 2)}
        cap = jnp.logical_and(row3 == 7, at_north)
        for c in (0, 2):
            value = ghost(n, c)
            for b in (0, 1):
                if b in blocks:
                    fn[c][b] = jnp.where(cap, value, fn[c][b])
        new = {}
        for b in blocks:
            m = metric3[b // 2]
            curl = (NORTH * (fn[2][b] - f[2][b]) - RADIAL * (up[1][b] - f[1][b]),
                    RADIAL * (up[0][b] - f[0][b]) - m * (fe[2][b] - f[2][b]),
                    m * (fe[1][b] - f[1][b]) - NORTH * (fn[0][b] - f[0][b]))
            new[b] = [hh[b, c, 1:9] - curl[c] for c in range(3)]

        def store(b, c, v):
            hh[b, c, 1:9] = v

        merge_all(new, store)

    def backward(n, blocks):
        f = [[hh[b, c, 1:9] for b in range(4)] for c in range(3)]
        down = [[hh[b, c, 0:8] for b in range(4)] for c in range(2)]
        fw = {c: turn(f[c], 1, 2, blocks) for c in (1, 2)}
        fs = {c: turn(f[c], 1, 1, blocks) for c in (0, 2)}
        cap = jnp.logical_and(row3 == 0, at_south)
        for c in (0, 2):
            value = ghost(n, c)
            for b in (0, 1):
                if b in blocks:
                    fs[c][b] = jnp.where(cap, value, fs[c][b])
        new = {}
        for b in blocks:
            m = metric3[b // 2]
            curl = (NORTH * (f[2][b] - fs[2][b]) - RADIAL * (f[1][b] - down[1][b]),
                    RADIAL * (f[0][b] - down[0][b]) - m * (f[2][b] - fw[2][b]),
                    m * (f[1][b] - fw[1][b]) - NORTH * (f[0][b] - fs[0][b]))
            old = [ee[b, c, 0:8] for c in range(3)]
            drive = [2.0 * old[c] + curl[c] for c in range(3)]
            new[b] = [uu[b, 3 * a, 0:8] * drive[0] + uu[b, 3 * a + 1, 0:8] * drive[1] + uu[b, 3 * a + 2, 0:8] * drive[2] - old[a]
                      for a in range(3)]

        def store(b, c, v):
            ee[b, c, 0:8] = v

        merge_all(new, store)

    def step(n, _):
        forward(n, range(4))
        backward(n, range(4))
        return 0

    lax.fori_loop(0, STEPS - 1, step, 0)
    forward(STEPS - 1, range(3))
    backward(STEPS - 1, range(1))
    for c in range(3):
        eo_ref[c] = ee[0, c, pl.ds(0, 8)]
        ho_ref[c] = hh[0, c, pl.ds(1, 8)]

    for n in range(2):
        for copy in to_lon[n]:
            copy.wait_send()

    @pl.when(inner_north)
    def _():
        for copy in to_north[0] + to_north[1] + rows_north:
            copy.wait_send()

    @pl.when(inner_south)
    def _():
        for copy in to_south[0] + to_south[1] + rows_south:
            copy.wait_send()

    @pl.when(pole)
    def _():
        pltpu.make_async_copy(caps, caps, cap_send.at[0]).wait()

    for is_north, condition in poles:
        @pl.when(condition)
        def _():
            pole_copy(is_north).wait_send()


def write_out(e_kept, h_kept, e_out, h_out, sem):
    copies = [pltpu.make_async_copy(e_kept, e_out, sem.at[0]), pltpu.make_async_copy(h_kept, h_out, sem.at[1])]
    for copy in copies:
        copy.start()
    for copy in copies:
        copy.wait()


def solution(mesh):
    bands, lons = mesh.shape["band"], mesh.shape["lon"]

    def on_device(e, h, c, zone_factor, zone_bounds):
        vmem, hbm = (pl.BlockSpec(memory_space=m) for m in (pltpu.VMEM, pltpu.HBM))
        f32 = lambda *shape: pltpu.VMEM(shape, jnp.float32)
        kept = pltpu.VMEM(e.shape, e.dtype)
        inputs = [pltpu.with_memory_space_constraint(x, pltpu.HBM) for x in (zone_factor, zone_bounds, e, h, c)]
        fields = pl.pallas_call(
            functools.partial(kernel, bands=bands, lons=lons),
            out_shape=(kept, kept),
            in_specs=[hbm] * 5,
            out_specs=(vmem, vmem),
            scratch_shapes=[
                pltpu.SMEM(zone_factor.shape, jnp.int32), pltpu.SMEM(zone_bounds.shape, jnp.int32),
                f32(3, 8, 8, 128), f32(3, 8, 8, 128), f32(9, 8, 8, 128),
                f32(3, 8, 8, 128), f32(3, 8, 8, 128), f32(9, 8, 8, 128),
                f32(2, 27, 8, 128), f32(2, 27, 8, 128), f32(2, 27, 8, 128),
                f32(64, 8, 128), f32(32, 8, 128), f32(32, 8, 128), f32(64, 8, 128),
                f32(4, 3, 9, 8, 128), f32(4, 3, 9, 8, 128), f32(4, 9, 8, 8, 128),
                f32(8, 128), f32(lons - 1, 8, 128), f32(STEPS, 2, 8, 128),
                pltpu.SemaphoreType.DMA((5,)), pltpu.SemaphoreType.DMA((19,)), pltpu.SemaphoreType.DMA((19,)),
                pltpu.SemaphoreType.DMA((1,)), pltpu.SemaphoreType.DMA((1,)), pltpu.SemaphoreType.REGULAR,
            ],
            compiler_params=pltpu.CompilerParams(collective_id=0, has_side_effects=True, vmem_limit_bytes=60 * 1024 * 1024),
        )(*inputs)
        like = jax.ShapeDtypeStruct(e.shape, e.dtype)
        return pl.pallas_call(
            write_out,
            out_shape=(like, like),
            in_specs=[vmem, vmem],
            out_specs=(hbm, hbm),
            scratch_shapes=[pltpu.SemaphoreType.DMA((2,))],
        )(*(pltpu.with_memory_space_constraint(x, pltpu.VMEM) for x in fields))

    spread = P(None, None, "band", "lon")
    return jax.shard_map(on_device, mesh=mesh, in_specs=(spread, spread, spread, P(), P()), out_specs=(spread, spread),
                         check_vma=False)
```

```python
import functools

import jax
import jax.numpy as jnp
from jax import lax
from jax.experimental import pallas as pl
from jax.experimental.pallas import tpu as pltpu
from jax.sharding import PartitionSpec as P

MESH = pl.DeviceIdType.MESH
STEPS = 4
NORTH, RADIAL, EAST, FLOOR = 0.45, 0.5, 0.12, 0.25


def lane_ids():
    return lax.broadcasted_iota(jnp.int32, (8, 128), 1)


def row_ids():
    return lax.broadcasted_iota(jnp.int32, (8, 128), 0)


def roll(x, by, axis):
    by = by % x.shape[axis]
    return x if by == 0 else pltpu.roll(x, by, axis)


def pair_shift(main, edge, by, axis):
    ids = lane_ids() if axis == 1 else row_ids()
    last = ids == (0 if by == 1 else (127 if axis == 1 else 7))
    rolled_main, rolled_edge = roll(main, by, axis), roll(edge, by, axis)
    return jnp.where(last, rolled_edge, rolled_main), jnp.where(last, rolled_main, rolled_edge)


def merge(x, gates):
    lanes = lane_ids()
    for step, gate in zip((1, 2, 4), gates):
        other = jnp.take_along_axis(x, lanes ^ step, axis=1)
        x = x + jnp.where(gate, other, x)
    return x * 0.125


def inverse(c):
    m = [[c[0] + 1.0, c[1], c[2]], [c[3], c[4] + 1.0, c[5]], [c[6], c[7], c[8] + 1.0]]

    def cof(a, b):
        i, j, p, q = (a + 1) % 3, (a + 2) % 3, (b + 1) % 3, (b + 2) % 3
        return m[i][p] * m[j][q] - m[i][q] * m[j][p]

    cofs = [[cof(a, b) for b in range(3)] for a in range(3)]
    det = m[0][0] * cofs[0][0] + m[0][1] * cofs[0][1] + m[0][2] * cofs[0][2]
    inv = 1.0 / det
    return [cofs[b][a] * inv for a in range(3) for b in range(3)]


def row_tables(zf, zb, rows, total):
    factor = jnp.full((8, 128), zf[0], jnp.int32)
    for z in range(zb.shape[0]):
        factor = jnp.where(rows >= zb[z], zf[z + 1], factor)
    lat = ((rows.astype(jnp.float32) + 0.5) / total - 0.5) * jnp.pi
    metric = EAST / jnp.maximum(factor.astype(jnp.float32) * jnp.cos(lat), FLOOR)
    return metric, factor


def batched(fn, tiles):
    whole = fn(jnp.concatenate(tiles, axis=0))
    return [whole[8 * i : 8 * i + 8] for i in range(len(tiles))]


def total_of(terms):
    out = None
    for factor, tile in terms:
        if tile is None:
            continue
        if out is None:
            out = tile if isinstance(factor, float) and factor == 1.0 else factor * tile
        elif isinstance(factor, float) and factor == 1.0:
            out = out + tile
        elif isinstance(factor, float) and factor == -1.0:
            out = out - tile
        else:
            out = out + factor * tile
    return out


class PoleRows:
    def __init__(self, at_north, metric, gates):
        self.at_north, self.metric, self.gates = at_north, metric, gates

    def shift_layer(self, field, c, r, source, by):
        rows = row_ids()
        key = source if source == "free" else (source[0], source[1] + by)
        tile = field.get((c, r, key))
        if tile is None:
            return None
        return jnp.where(rows == (7 if by == 1 else 0), 0.0, pltpu.roll(tile, 7 if by == 1 else 1, 0))

    def turn(self, field, comps, by):
        ids = [i for i in field if i[0] in comps]
        return dict(zip(ids, batched(lambda x: pltpu.roll(x, by % 128, 1), [field[i] for i in ids]))) if ids else {}

    def merge(self, field):
        ids = list(field)
        tiles = [field[i] for i in ids]
        for level, step in enumerate((1, 2, 4)):
            def swap(x):
                return jnp.take_along_axis(x, lax.broadcasted_iota(jnp.int32, x.shape, 1) ^ step, axis=1)
            others = batched(swap, tiles)
            tiles = [t + jnp.where(self.gates[i[1]][level], o, t) for i, t, o in zip(ids, tiles, others)]
        return {i: t * 0.125 for i, t in zip(ids, tiles)}

    def keys(self, field, spread, extra=()):
        found = []
        for source in [i[2] for i in field] + list(extra):
            for s in ([source] if source == "free" else [source, (source[0], source[1] + spread)]):
                if s not in found:
                    found.append(s)
        return found

    def forward(self, e, h, wanted, merged=True):
        ahead = -1 if self.at_north else 1
        fe = self.turn(e, (1, 2), -1)
        new = {}
        for source in self.keys(e, -1, [i[2] for i in h]):
            for c, r in wanted:
                m = self.metric[r]
                up = lambda c: self.shift_layer(e, c, r, source, 1)
                at = lambda c: e.get((c, r, source))
                north = lambda c: e.get((c, r + ahead, source))
                east = lambda c: fe.get((c, r, source))
                if c == 0:
                    curl = [(-NORTH, north(2)), (NORTH, at(2)), (RADIAL, up(1)), (-RADIAL, at(1))]
                elif c == 1:
                    curl = [(-RADIAL, up(0)), (RADIAL, at(0)), (m, east(2)), (-m, at(2))]
                else:
                    curl = [(-m, east(1)), (m, at(1)), (NORTH, north(0)), (-NORTH, at(0))]
                tile = total_of([(1.0, h.get((c, r, source)))] + curl)
                if tile is not None:
                    new[c, r, source] = tile
        return self.merge(new) if merged else new

    def drive(self, e, h, rows):
        behind = 1 if self.at_north else -1
        fw = self.turn(h, (1, 2), 1)
        new = {}
        for source in self.keys(h, 1, [i[2] for i in e]):
            for r in rows:
                m = self.metric[r]
                down = lambda c: self.shift_layer(h, c, r, source, -1)
                at = lambda c: h.get((c, r, source))
                south = lambda c: h.get((c, r + behind, source))
                west = lambda c: fw.get((c, r, source))
                curls = ([(NORTH, at(2)), (-NORTH, south(2)), (-RADIAL, at(1)), (RADIAL, down(1))],
                         [(RADIAL, at(0)), (-RADIAL, down(0)), (-m, at(2)), (m, west(2))],
                         [(m, at(1)), (-m, west(1)), (-NORTH, at(0)), (NORTH, south(0))])
                for c in range(3):
                    tile = total_of([(2.0, e.get((c, r, source)))] + curls[c])
                    if tile is not None:
                        new[c, r, source] = tile
        return new

    def update(self, u, drive, e, wanted, merged=True):
        new = {}
        for source in self.keys(drive, 0, [i[2] for i in e]):
            for a, r in wanted:
                tile = total_of([(u[3 * a + c, r], drive.get((c, r, source))) for c in range(3)]
                                + [(-1.0, e.get((a, r, source)))])
                if tile is not None:
                    new[a, r, source] = tile
        return self.merge(new) if merged else new


def every(rows):
    return [(c, r) for r in rows for c in range(3)]


def only(field, source):
    return {i: t for i, t in field.items() if (i[2] == "free") == source}


def pole_chain(at_north, load, metric, gates):
    p = PoleRows(at_north, metric, gates)
    deep = range(4) if at_north else range(5)
    e = {(c, r, "free"): load("e", c, r) for c in range(3) for r in deep}
    h = {(c, r, "free"): load("h", c, r) for c in range(3) for r in range(4)}
    u = {(i, r): v for r in range(3 if at_north else 4) for i, v in enumerate(inverse([load("c", i, r) for i in range(9)]))}
    out = {}

    def note(n, field, initial=False):
        for (c, r, source), tile in field.items():
            if r == 0 and c != 1:
                out[("free", n) if source == "free" else ("response", n) + source, c] = tile

    unit = jnp.ones((8, 128), jnp.float32)
    ends = [(0, 0), (2, 0)]
    if at_north:
        note(0, e)
        h = p.forward(e, h, every(range(4)))
        h[0, 0, (2, 0)] = -NORTH * unit
        h[2, 0, (0, 0)] = NORTH * unit
        def back(e, h, free_rows, rows, wanted=None, merged=True):
            new = {}
            for free, rr in ((True, free_rows), (False, rows)):
                ee, hh = only(e, free), only(h, free)
                d = p.drive(ee, hh, rr)
                new.update({(i, free): t for i, t in d.items()})
            drive = {i: t for (i, _), t in new.items()}
            want = wanted or every(sorted(set(free_rows) | set(rows)))
            return p.update(u, drive, {i: t for i, t in e.items() if (i[1] in (free_rows if i[2] == "free" else rows))}, want, merged)

        e = back(e, h, range(3), range(1))
        note(1, e)
        h = p.forward(e, h, every(range(3)))
        h = {i: t for i, t in h.items() if i[2] == "free" or i[1] < 2}
        e = back(e, h, range(2), range(2))
        note(2, e)
        h = p.forward(e, h, every(range(2)))
        e = back(e, h, range(1), range(1), ends, False)
        note(3, e)
    else:
        h = p.forward(e, h, every(range(4)))
        note(0, h)
        drive = p.drive(e, h, range(4))
        drive[0, 0, (2, 0)] = -NORTH * unit
        drive[2, 0, (0, 0)] = NORTH * unit
        e = p.update(u, drive, {i: t for i, t in e.items() if i[1] < 4}, every(range(4)))
        h = p.forward(e, {i: t for i, t in h.items() if i[1] < 3}, every(range(3)))
        note(1, h)
        drive = p.drive(e, h, range(3))
        e = p.update(u, drive, {i: t for i, t in e.items() if i[1] < 3}, every(range(3)))
        h = p.forward(e, {i: t for i, t in h.items() if i[1] < 2}, every(range(2)))
        note(2, h)
        drive = p.drive(e, h, range(2))
        e = p.update(u, drive, {i: t for i, t in e.items() if i[1] < 2}, every(range(2)))
        h = p.forward(e, {i: t for i, t in h.items() if i[1] < 1}, ends, False)
        note(3, h)
    return out


def pole_items(at_north):
    return ([("e", c, r) for c in range(3) for r in range(4 if at_north else 5)] + [("h", c, r) for c in range(3) for r in range(4)]
            + [("c", i, r) for i in range(9) for r in range(3 if at_north else 4)])


def columns(tiles):
    lanes = lane_ids()
    count = 128
    tiles = tiles + [None] * (count - len(tiles))
    while count > 1:
        count //= 2
        first, second = tiles[:count], tiles[count:]
        low = (lanes & count) == 0
        zero = jnp.zeros((8, 128), jnp.float32)
        pairs = [(a, b) for a, b in zip(first, second) if a is not None]
        give = [jnp.where(low, zero if b is None else b, a) for a, b in pairs]
        take = [jnp.where(low, a, zero if b is None else b) for a, b in pairs]
        swapped = batched(lambda x: jnp.take_along_axis(x, lax.broadcasted_iota(jnp.int32, x.shape, 1) ^ count, axis=1), give)
        tiles = [t + s for t, s in zip(take, swapped)]
        tiles = tiles + [None] * (count - len(tiles))
    return tiles[0]


def solve_caps(names, total):
    rows = row_ids()
    spread = dict(zip(names, batched(lambda x: x, [jnp.take_along_axis(total, jnp.full((8, 128), q, jnp.int32), axis=1)
                                                   for q in range(len(names))])))
    caps = []

    def moved(tile, d):
        if d == 0:
            return tile
        kept = rows >= d if d > 0 else rows < 8 + d
        return jnp.where(kept, pltpu.roll(tile, d % 8, 0), 0.0)

    for n in range(STEPS):
        value = {c: spread[("free", n), c] for c in (0, 2)}
        for m in range(n):
            shifted = {}
            for name, c in names:
                if name[0] == "response" and name[1] == n - m:
                    if name[2:] not in shifted:
                        shifted[name[2:]] = moved(caps[m][name[2]], name[3])
                    value[c] = value[c] + spread[name, c] * shifted[name[2:]]
        caps.append(value)
    return caps


def kernel(zf_in, zb_in, e_in, h_in, c_in, eo_ref, ho_ref, zf, zb, e_ref, h_ref, c_ref, rows_e, rows_h, rows_c, pack, got, got2, pole_own, pole_pack, pole_got, pole_sum, ee, hh, uu, mine,
           caps, sums, load_sem, send, recv, cap_send, cap_recv, go, *, bands, lons):
    band, lon = lax.axis_index("band"), lax.axis_index("lon")
    at_south, at_north = band == 0, band == bands - 1
    inner_north, inner_south = jnp.logical_not(at_north), jnp.logical_not(at_south)
    north, south = band + 1, band - 1
    east, west = lax.rem(lon + 1, lons), lax.rem(lon + lons - 1, lons)
    pole = jnp.logical_or(at_south, at_north)

    loads = [pltpu.make_async_copy(s, d, load_sem.at[i]) for i, (s, d) in enumerate(((e_in, e_ref), (h_in, h_ref), (c_in, c_ref), (zf_in, zf), (zb_in, zb)))]
    for load in loads:
        load.start()

    barrier = pltpu.get_barrier_semaphore()

    def greet(b, l):
        pl.semaphore_signal(barrier, inc=1, device_id=(b, l), device_id_type=MESH)

    greet(band, east)
    greet(band, west)

    @pl.when(inner_north)
    def _():
        for l in (east, west, lon):
            greet(north, l)

    @pl.when(inner_south)
    def _():
        for l in (east, west, lon):
            greet(south, l)

    @pl.when(pole)
    def _():
        def one(d, _):
            greet(band, lax.rem(lon + d, lons))
            return 0
        lax.fori_loop(2, lons - 1, one, 0)

    lanes, rows = lane_ids(), row_ids()

    def pack_field(ref, first):
        rolled = [[roll(ref[c, a * 4 + q], 32 * q, 1) for q in range(4)] for c in range(3) for a in range(2)]
        for n, t in enumerate(rolled):
            lo, hi = t[0], t[1]
            for q in range(1, 4):
                lo = jnp.where(lanes // 32 == q, t[q], lo)
                if q > 1:
                    hi = jnp.where(lanes // 32 == q - 1, t[q], hi)
            pack[0, first + n] = lo
            pack[1, first + n] = jnp.where(lanes // 32 == 3, t[0], hi)

    def at_slot(s):
        return jnp.logical_and(lanes >= 24 * s, lanes < 24 * s + 24)

    def pack_conduct():
        for tile in range(15):
            blocks = [divmod(n, 8) for n in range(5 * tile, min(5 * tile + 5, 72))]
            rolled = [roll(c_ref[i, k], 24 * s, 1) for s, (i, k) in enumerate(blocks)]
            lo = hi = rolled[0]
            for s in range(1, len(rolled)):
                lo = jnp.where(at_slot(s), rolled[s], lo)
                hi = jnp.where(at_slot(s - 1), rolled[s], hi)
            pack[0, 12 + tile] = lo
            pack[1, 12 + tile] = hi

    def remote(src, dst, i, b, l):
        return pltpu.make_async_remote_copy(src_ref=src, dst_ref=dst, send_sem=send.at[i], recv_sem=recv.at[i],
                                            device_id=(b, l), device_id_type=MESH)

    fields, conduct = pl.ds(0, 12), pl.ds(12, 15)
    to_lon = [[remote(pack.at[k, part], got.at[k, part], 2 * n + k, band, (west, east)[k]) for k in range(2)]
              for n, part in enumerate((fields, conduct))]
    north_parts = [[(k, part, pl.ds(8 - d[k], d[k]), 4 + 2 * n + k) for k in range(2)]
                   for n, (part, d) in enumerate(((fields, (4, 3)), (conduct, (3, 2))))]
    south_parts = [[(k, part, pl.ds(0, d[k]), 8 + 2 * n + k) for k in range(2)]
                   for n, (part, d) in enumerate(((fields, (3, 4)), (conduct, (2, 3))))]
    odd = lax.rem(band, 2) == 1
    to_north = [[remote(pack.at[k, p, r], got2.at[k, p, r], i, north, (west, east)[k]) for k, p, r, i in parts] for parts in north_parts]
    to_south = [[remote(pack.at[k, p, r], got2.at[k, p, r], i, south, (west, east)[k]) for k, p, r, i in parts] for parts in south_parts]
    on_north = [[remote(got.at[k, p, r], got2.at[k, p, r], i, north, lon) for k, p, r, i in parts] for parts in north_parts]
    on_south = [[remote(got.at[k, p, r], got2.at[k, p, r], i, south, lon) for k, p, r, i in parts] for parts in south_parts]
    trio = ((e_ref, rows_e), (h_ref, rows_h), (c_ref, rows_c))
    rows_north = [remote(s.at[:, :, pl.ds(8 - d, d)], t.at[:, :, pl.ds(8 - d, d)], 12 + i, north, lon)
                  for i, ((s, t), d) in enumerate(zip(trio, (4, 4, 3)))]
    rows_south = [remote(s.at[:, :, pl.ds(0, d)], t.at[:, :, pl.ds(0, d)], 15 + i, south, lon)
                  for i, ((s, t), d) in enumerate(zip(trio, (4, 3, 3)))]

    def send_part(n):
        for copy in reversed(to_lon[n]):
            copy.start()

        @pl.when(inner_north)
        def _():
            for copy in rows_north[:2] if n == 0 else rows_north[2:]:
                copy.start()

        @pl.when(jnp.logical_and(inner_north, jnp.logical_or(odd, at_south)))
        def _():
            for copy in to_north[n]:
                copy.start()

        @pl.when(inner_south)
        def _():
            for copy in rows_south[:2] if n == 0 else rows_south[2:]:
                copy.start()

        @pl.when(jnp.logical_and(inner_south, jnp.logical_or(jnp.logical_not(odd), at_north)))
        def _():
            for copy in to_south[n]:
                copy.start()

    loads[0].wait()
    loads[1].wait()
    poles = ((True, at_north), (False, at_south))
    refs = {"e": e_ref, "h": h_ref, "c": c_ref}

    def pole_copy(is_north):
        part = pl.ds(0, (len(pole_items(is_north)) + 1) // 2)
        return remote(pole_pack.at[part], pole_got.at[part], 18, band, east)

    @pl.when(pole)
    def _():
        loads[2].wait()

    for is_north, condition in poles:
        @pl.when(condition)
        def _():
            tiles = [refs[kind][i, pl.ds(0, 8), 7 - r if is_north else r, :] for kind, i, r in pole_items(is_north)]
            for n, tile in enumerate(tiles):
                pole_own[n] = tile
            for n in range(0, len(tiles), 2):
                pole_pack[n // 2] = jnp.where(lanes < 64, pltpu.roll(tiles[n], 64, 1), tiles[min(n + 1, len(tiles) - 1)])

    pack_field(e_ref, 0)
    pack_field(h_ref, 6)

    @pl.when(jnp.logical_not(pole))
    def _():
        pl.semaphore_wait(barrier, 8)

    @pl.when(band == 1)
    def _():
        pl.semaphore_signal(go, inc=1, device_id=(south, lon), device_id_type=MESH)

    @pl.when(band == bands - 2)
    def _():
        pl.semaphore_signal(go, inc=1, device_id=(north, lon), device_id_type=MESH)

    @pl.when(pole)
    def _():
        pl.semaphore_wait(go, 1)

    for is_north, condition in poles:
        @pl.when(condition)
        def _():
            pole_copy(is_north).start()

    send_part(0)

    @pl.when(jnp.logical_not(pole))
    def _():
        loads[2].wait()

    pack_conduct()
    send_part(1)

    loads[3].wait()
    loads[4].wait()
    metric, factors, gates = [], [], []
    for block in range(2):
        shift = 0 if block == 0 else jnp.where(rows < 4, 8, -8)
        m, f = row_tables(zf, zb, band * 8 + rows + shift, 8 * bands)
        metric.append(m)
        factors.append(f)
        gates.append([f > s for s in (1, 2, 4)])
    zero = jnp.zeros((8, 128), jnp.float32)
    for b in range(4):
        for c in range(3):
            for field in (ee, hh):
                field[b, c, 0:8] = zero
                field[b, c, 72:80] = zero
    for n in range(STEPS):
        for i in range(2):
            sums[n, i] = zero

    def take_in(block, layer, load):
        for c in range(3):
            place = pl.ds(8 * layer + 8 if isinstance(layer, int) else pl.multiple_of(8 * layer + 8, 8), 8)
            ee[block, c, place] = load(c)
            hh[block, c, place] = load(3 + c)
        for i, value in enumerate(inverse([load(6 + c) for c in range(9)])):
            uu[block, i, layer] = value

    def own(k, _):
        take_in(0, k, lambda f: e_ref[f, k] if f < 3 else (h_ref[f - 3, k] if f < 6 else c_ref[f - 6, k]))
        return 0


    def unpack(block, ref):
        for k in range(8):
            a, q = divmod(k, 4)
            tiles = [roll(jnp.where(lanes // 32 == q, ref[0, 2 * f + a], ref[1, 2 * f + a]), -32 * q, 1) for f in range(6)]
            for i in range(9):
                tile, slot = divmod(8 * i + k, 5)
                tiles.append(roll(jnp.where(at_slot(slot), ref[0, 12 + tile], ref[1, 12 + tile]), -24 * slot, 1))
            take_in(block, k, lambda f: tiles[f])

    near = sorted(((i // 4, i % 4) for i in range(8)), key=lambda o: 4 * o[0] + min(o[1], 4 - o[1]))
    z_here = lax.rem(lon, 8)

    def cap_copy(z, n):
        hi, x = lax.rem(lon // 32 + near[n][0], 2), lax.rem(lax.rem(lon // 8, 4) + near[n][1], 4)
        slot = lax.rem(z - z_here + 8, 8) * 8 + n - 1
        return pltpu.make_async_remote_copy(src_ref=mine, dst_ref=caps.at[slot], send_sem=cap_send.at[0], recv_sem=cap_recv.at[0],
                                            device_id=(band, hi * 32 + x * 8 + z), device_id_type=MESH)

    names = {}
    for is_north, condition in poles:
        @pl.when(condition)
        def _():
            items = pole_items(is_north)
            place = {item: n for n, item in enumerate(items)}
            edge = [7 - r if is_north else r for r in range(5)]
            m = [jnp.broadcast_to(metric[0][r : r + 1, :], (8, 128)) for r in edge]
            f = [jnp.broadcast_to(factors[0][r : r + 1, :], (8, 128)) for r in edge]
            g = [[x > k for k in (1, 2, 4)] for x in f]

            def seam(kind, i, r):
                n = place[kind, i, r]
                tile = pole_got[n // 2]
                return jnp.where(lanes < 64, tile if n % 2 == 0 else pltpu.roll(tile, 64, 1), pltpu.roll(pole_own[n], 64, 1))

            inner = pole_chain(is_north, lambda kind, i, r: pole_own[place[kind, i, r]], m, g)
            names[is_north] = list(inner)
            for n, tile in enumerate(inner.values()):
                pole_sum[n] = tile
            pole_copy(is_north).wait_recv()
            outer = pole_chain(is_north, seam, m, g)
            inside = jnp.logical_and(lanes >= 32, lanes < 96)
            mine[...] = columns([jnp.where(inside, pole_sum[n] + outer[name], 0.0) for n, name in enumerate(names[is_north])])

    @pl.when(pole)
    def _():
        pl.semaphore_wait(barrier, lons - 1 + 3)
        for z in range(8):
            @pl.when(z_here != z)
            def _():
                cap_copy(z, 0).start()

            for n in range(1, 8):
                cap_copy(z, n).start()

    lax.fori_loop(0, 8, own, 0)

    for n in range(2):
        for copy in to_lon[n]:
            copy.wait_recv()

        @pl.when(jnp.logical_and(odd, inner_north))
        def _():
            for copy in on_south[n]:
                copy.start()

        @pl.when(jnp.logical_and(jnp.logical_not(odd), inner_south))
        def _():
            for copy in on_north[n]:
                copy.start()

    unpack(1, got)

    @pl.when(inner_north)
    def _():
        for n in range(2):
            for copy in to_south[n]:
                copy.wait_recv()
        for copy in rows_south:
            copy.wait_recv()

    @pl.when(inner_south)
    def _():
        for n in range(2):
            for copy in to_north[n]:
                copy.wait_recv()
        for copy in rows_north:
            copy.wait_recv()

    def outer(k, _):
        take_in(2, k, lambda f: rows_e[f, k] if f < 3 else (rows_h[f - 3, k] if f < 6 else rows_c[f - 6, k]))
        return 0

    lax.fori_loop(0, 8, outer, 0)
    unpack(3, got2)

    @pl.when(pole)
    def _():
        pltpu.make_async_copy(caps, caps, cap_recv.at[0]).wait()

    for is_north, condition in poles:
        @pl.when(condition)
        def _():
            total = (mine[...] + jnp.sum(caps[...], axis=0)) * (1.0 / (128 * lons))
            for n, value in enumerate(solve_caps(names[is_north], total)):
                sums[n, 0] = value[0]
                sums[n, 1] = value[2]

    lane3 = lax.broadcasted_iota(jnp.int32, (8, 8, 128), 2)
    row3 = lax.broadcasted_iota(jnp.int32, (8, 8, 128), 1)
    metric3 = [jnp.broadcast_to(m, (8, 8, 128)) for m in metric]
    gates3 = [[jnp.broadcast_to(g, (8, 8, 128)).reshape(64, 128) for g in gs] for gs in gates]
    lane2 = lax.broadcasted_iota(jnp.int32, (64, 128), 1)

    def layers(ref, b, c, start=8):
        return ref[b, c, start : start + 64].reshape(8, 8, 128)

    def turn(f, by, blocks):
        seam = lane3 == (0 if by == 1 else 127)
        other = (1, 0, 3, 2)
        moved = {b: pltpu.roll(f[b].reshape(64, 128), by % 128, 1).reshape(8, 8, 128)
                 for b in range(4) if b in blocks or other[b] in blocks}
        return {b: jnp.where(seam, moved[other[b]], moved[b]) for b in blocks}

    def turn_rows(ref, c, by, blocks):
        seam = row3 == (0 if by == 1 else 7)
        return {b: jnp.where(seam, layers(ref, (2, 3, 0, 1)[b], c, 8 + 7 * by), layers(ref, b, c, 8 - by)) for b in blocks}

    def merge_all(f, store):
        x = {(b, c): f[b][c].reshape(64, 128) for b in f for c in range(3)}
        for level, step in enumerate((1, 2, 4)):
            other = {i: jnp.take_along_axis(v, lane2 ^ step, axis=1) for i, v in x.items()}
            x = {(b, c): v + jnp.where(gates3[b // 2][level], other[b, c], v) for (b, c), v in x.items()}
        for (b, c), v in x.items():
            store(b, c, v * 0.125)

    def ghost(n, c):
        return jnp.concatenate([jnp.broadcast_to(sums[n, c // 2, k : k + 1, :].reshape(1, 1, 128), (1, 8, 128)) for k in range(8)])

    def forward(n, blocks):
        f = [[layers(ee, b, c) for b in range(4)] for c in range(3)]
        up = [[layers(ee, b, c, 16) for b in range(4)] for c in range(2)]
        fe = {c: turn(f[c], -1, blocks) for c in (1, 2)}
        fn = {c: turn_rows(ee, c, -1, blocks) for c in (0, 2)}
        cap = jnp.logical_and(row3 == 7, at_north)
        for c in (0, 2):
            value = ghost(n, c)
            for b in (0, 1):
                if b in blocks:
                    fn[c][b] = jnp.where(cap, value, fn[c][b])
        new = {}
        for b in blocks:
            m = metric3[b // 2]
            curl = (NORTH * (fn[2][b] - f[2][b]) - RADIAL * (up[1][b] - f[1][b]),
                    RADIAL * (up[0][b] - f[0][b]) - m * (fe[2][b] - f[2][b]),
                    m * (fe[1][b] - f[1][b]) - NORTH * (fn[0][b] - f[0][b]))
            new[b] = [layers(hh, b, c) - curl[c] for c in range(3)]

        def store(b, c, v):
            hh[b, c, 8:72] = v

        merge_all(new, store)

    def backward(n, blocks):
        f = [[layers(hh, b, c) for b in range(4)] for c in range(3)]
        down = [[layers(hh, b, c, 0) for b in range(4)] for c in range(2)]
        fw = {c: turn(f[c], 1, blocks) for c in (1, 2)}
        fs = {c: turn_rows(hh, c, 1, blocks) for c in (0, 2)}
        cap = jnp.logical_and(row3 == 0, at_south)
        for c in (0, 2):
            value = ghost(n, c)
            for b in (0, 1):
                if b in blocks:
                    fs[c][b] = jnp.where(cap, value, fs[c][b])
        new = {}
        for b in blocks:
            m = metric3[b // 2]
            curl = (NORTH * (f[2][b] - fs[2][b]) - RADIAL * (f[1][b] - down[1][b]),
                    RADIAL * (f[0][b] - down[0][b]) - m * (f[2][b] - fw[2][b]),
                    m * (f[1][b] - fw[1][b]) - NORTH * (f[0][b] - fs[0][b]))
            old = [layers(ee, b, c) for c in range(3)]
            drive = [2.0 * old[c] + curl[c] for c in range(3)]
            new[b] = [uu[b, 3 * a, 0:8] * drive[0] + uu[b, 3 * a + 1, 0:8] * drive[1] + uu[b, 3 * a + 2, 0:8] * drive[2] - old[a]
                      for a in range(3)]

        def store(b, c, v):
            ee[b, c, 8:72] = v

        merge_all(new, store)

    def step(n, _):
        forward(n, range(4))
        backward(n, range(4))
        return 0

    lax.fori_loop(0, STEPS - 1, step, 0)
    forward(STEPS - 1, range(3))
    backward(STEPS - 1, range(1))
    for c in range(3):
        eo_ref[c] = layers(ee, 0, c)
        ho_ref[c] = layers(hh, 0, c)

    for n in range(2):
        for copy in to_lon[n]:
            copy.wait_send()

    @pl.when(inner_north)
    def _():
        for copy in to_north[0] + to_north[1] + rows_north:
            copy.wait_send()

    @pl.when(inner_south)
    def _():
        for copy in to_south[0] + to_south[1] + rows_south:
            copy.wait_send()

    @pl.when(pole)
    def _():
        pltpu.make_async_copy(caps, caps, cap_send.at[0]).wait()

    for is_north, condition in poles:
        @pl.when(condition)
        def _():
            pole_copy(is_north).wait_send()


def write_out(e_kept, h_kept, e_out, h_out, sem):
    copies = [pltpu.make_async_copy(e_kept, e_out, sem.at[0]), pltpu.make_async_copy(h_kept, h_out, sem.at[1])]
    for copy in copies:
        copy.start()
    for copy in copies:
        copy.wait()


def solution(mesh):
    bands, lons = mesh.shape["band"], mesh.shape["lon"]

    def on_device(e, h, c, zone_factor, zone_bounds):
        vmem, hbm = (pl.BlockSpec(memory_space=m) for m in (pltpu.VMEM, pltpu.HBM))
        f32 = lambda *shape: pltpu.VMEM(shape, jnp.float32)
        kept = pltpu.VMEM(e.shape, e.dtype)
        inputs = [pltpu.with_memory_space_constraint(x, pltpu.HBM) for x in (zone_factor, zone_bounds, e, h, c)]
        fields = pl.pallas_call(
            functools.partial(kernel, bands=bands, lons=lons),
            out_shape=(kept, kept),
            in_specs=[hbm] * 5,
            out_specs=(vmem, vmem),
            scratch_shapes=[
                pltpu.SMEM(zone_factor.shape, jnp.int32), pltpu.SMEM(zone_bounds.shape, jnp.int32),
                f32(3, 8, 8, 128), f32(3, 8, 8, 128), f32(9, 8, 8, 128),
                f32(3, 8, 8, 128), f32(3, 8, 8, 128), f32(9, 8, 8, 128),
                f32(2, 27, 8, 128), f32(2, 27, 8, 128), f32(2, 27, 8, 128),
                f32(64, 8, 128), f32(32, 8, 128), f32(32, 8, 128), f32(64, 8, 128),
                f32(4, 3, 80, 128), f32(4, 3, 80, 128), f32(4, 9, 8, 8, 128),
                f32(8, 128), f32(lons - 1, 8, 128), f32(STEPS, 2, 8, 128),
                pltpu.SemaphoreType.DMA((5,)), pltpu.SemaphoreType.DMA((19,)), pltpu.SemaphoreType.DMA((19,)),
                pltpu.SemaphoreType.DMA((1,)), pltpu.SemaphoreType.DMA((1,)), pltpu.SemaphoreType.REGULAR,
            ],
            compiler_params=pltpu.CompilerParams(collective_id=0, has_side_effects=True, vmem_limit_bytes=60 * 1024 * 1024),
        )(*inputs)
        like = jax.ShapeDtypeStruct(e.shape, e.dtype)
        return pl.pallas_call(
            write_out,
            out_shape=(like, like),
            in_specs=[vmem, vmem],
            out_specs=(hbm, hbm),
            scratch_shapes=[pltpu.SemaphoreType.DMA((2,))],
        )(*(pltpu.with_memory_space_constraint(x, pltpu.VMEM) for x in fields))

    spread = P(None, None, "band", "lon")
    return jax.shard_map(on_device, mesh=mesh, in_specs=(spread, spread, spread, P(), P()), out_specs=(spread, spread),
                         check_vma=False)
```
